32 devices in a mesh: dom: 8 (over z, x), sub: 4 (over y, core).
Axes of the slice: x: 2, y: 2, z: 4, core: 2. Of those that a mesh axis runs over, the one named last changes fastest.
Arguments:
- feats: bfloat16 [12032, 1024], P(('dom', 'sub')), may hold values from -8 to 8
- w_proj: bfloat16 [1024, 1024], replicated, may hold values from -0.375 to 0.375
- w_skip: bfloat16 [1024, 1024], replicated, may hold values from -0.1875 to 0.1875
- attn_src: float32 [4, 256], replicated, may hold values from -0.25 to 0.25
- attn_dst: float32 [4, 256], replicated, may hold values from -0.25 to 0.25
- bias: float32 [1024], replicated, may hold values from -3 to 3
- gain: float32 [1024], replicated, may hold values from 0.5 to 1.5
- shift: float32 [1024], replicated, may hold values from -3 to 3
- cotangent: bfloat16 [12032, 1024], P(('dom', 'sub')), may hold values from -6 to 6
- neighbours: int32 [12032, 16], P(('dom', 'sub')), may hold values from 0 to 469, as said below
- edge_mask: int32 [12032, 16], P(('dom', 'sub')), may hold values from 0 to 1, as said below
- node_mask: int32 [12032], P(('dom', 'sub')), may hold values from 0 to 1, as said below
- send_index: int32 [32, 2, 47], P(('dom', 'sub')), may hold values from 0 to 375, as said below
Outputs:
- output: bfloat16 [12032, 1024], P(('dom', 'sub'))
- grad_feats: bfloat16 [12032, 1024], P(('dom', 'sub'))
- grad_proj: float32 [1024, 1024], replicated
- grad_skip: float32 [1024, 1024], replicated
- grad_attn_src: float32 [4, 256], replicated
- grad_attn_dst: float32 [4, 256], replicated
- grad_bias: float32 [1024], replicated
- grad_gain: float32 [1024], replicated
- grad_shift: float32 [1024], replicated
The draws below stay inside these ranges and needn't reach their ends.
Inputs may be any that keep to these rules, and one draw needn't show every extreme that they name: `neighbours`: values below 376 are rows of the node's own partition; 376 + j names row send_index[p - 1, 1, j] of the partition below and 423 + j row send_index[p + 1, 0, j] of the partition above. A live slot never names a padded row and never names a partition outside 0 to 31. `edge_mask`: 0 on every slot of a padded node. `node_mask`: on each partition the real nodes come first and fill at least three quarters of its rows. `send_index`: each entry is a real node of the sending partition.
All inputs are finite; a program needn't handle non-finite values.
Results may differ from the reference program's by a relative error of at most 0.015.
Values may be sent and summed in bfloat16 or wider, within the bound.
No kernel may reach another device: no remote copies, remote signals or barrier semaphores. Data moves between devices by JAX's collectives and lax.ppermute only.
A program may use at most 128 MiB of HBM per device.

```python
import jax
import jax.numpy as jnp
from jax import lax

D_IN = 1024
HEADS = 4
HEAD_SIZE = 256
DEG = 16
NODE_DEV = 376
CONCAT = 1024
HALO = 47
PARTITIONS = 32
NODES = 12032


def graph_tables(key):
    keys = jax.random.split(key, 8)
    padding = jax.random.randint(keys[0], (PARTITIONS,), 0, NODE_DEV // 4 + 1)
    padding = padding.at[0].set(0)
    real_count = NODE_DEV - padding
    row_ids = jnp.arange(NODE_DEV, dtype=jnp.int32)
    node_flags = (row_ids[None, :] < real_count[:, None]).astype(jnp.int32)
    sent_count = jax.random.randint(keys[1], (PARTITIONS, 2), HALO // 2, HALO + 1)
    sent_count = sent_count.at[0, 1].set(HALO)
    send_rows = jax.random.randint(keys[2], (PARTITIONS, 2, HALO), 0, real_count[:, None, None])
    nothing = jnp.zeros((1,), jnp.int32)
    low_count = jnp.concatenate([nothing, sent_count[:-1, 1]])
    high_count = jnp.concatenate([sent_count[1:, 0], nothing])
    table_shape = (PARTITIONS, NODE_DEV, DEG)
    kinds = jax.random.randint(keys[3], table_shape, 0, 10)
    local_pick = jax.random.randint(keys[4], table_shape, 0, real_count[:, None, None])
    low_pick = NODE_DEV + jax.random.randint(keys[5], table_shape, 0, jnp.maximum(low_count, 1)[:, None, None])
    high_pick = NODE_DEV + HALO + jax.random.randint(keys[6], table_shape, 0, jnp.maximum(high_count, 1)[:, None, None])
    use_low = (kinds == 0) & (low_count[:, None, None] > 0)
    use_high = (kinds == 1) & (high_count[:, None, None] > 0)
    chosen = jnp.where(use_low, low_pick, jnp.where(use_high, high_pick, local_pick))
    keep_edge = jax.random.randint(keys[7], table_shape, 0, 4) > 0
    edge_flags = (keep_edge & (node_flags[:, :, None] > 0)).astype(jnp.int32)
    return (chosen.reshape(NODES, DEG).astype(jnp.int32), edge_flags.reshape(NODES, DEG), node_flags.reshape(NODES), send_rows.astype(jnp.int32))


def draw_neighbours(key, part):
    return graph_tables(key)[0]


def draw_edge_mask(key, part):
    return graph_tables(key)[1]


def draw_node_mask(key, part):
    return graph_tables(key)[2]


def draw_send_index(key, part):
    return graph_tables(key)[3]


def draw_feats(key, part):
    key = jax.random.fold_in(key, 11)
    placed = jnp.arange(NODES, dtype=jnp.float32) / NODES
    row_scale = (0.6 * 3.0 ** placed)[:, None]
    spread = jnp.clip(jax.random.normal(key, (NODES, D_IN), jnp.float32), -4.0, 4.0)
    return (row_scale * spread).astype(jnp.bfloat16)


def shard_levels(rng, extent, cuts, least, top_value):
    level, own = 1.0, jax.random.fold_in(rng, 6)
    for dim, blocks in cuts:
        draws = jnp.exp(jax.random.uniform(jax.random.fold_in(own, dim), (blocks,), jnp.float32, least / len(cuts), top_value / len(cuts)))
        level = level * jnp.repeat(draws, extent[dim] // blocks).reshape([-1 if axis == dim else 1 for axis in range(len(extent))])
    return level


def noise(rng, shape, width, limit, cuts=(), kind=jnp.bfloat16):
    level = shard_levels(rng, shape, cuts, -0.22, 0.18) if cuts else 1.0
    entries = jax.random.normal(rng, shape, jnp.float32) * width * level
    return jnp.minimum(jnp.maximum(entries, -limit), limit).astype(kind)


def setup_inputs(seed: int = 0) -> dict:
    key_of = jax.random.split(jax.random.key(seed), 14)
    return {
        "feats": draw_feats(jax.random.fold_in(key_of[13], 71), 0),
        "w_proj": noise(key_of[1], (D_IN, CONCAT), (D_IN // 4) ** -0.5, 0.375),
        "w_skip": noise(key_of[2], (D_IN, CONCAT), D_IN ** -0.5, 0.1875),
        "attn_src": noise(key_of[3], (HEADS, HEAD_SIZE), (2 * HEAD_SIZE) ** -0.5, 0.25, (), jnp.float32),
        "attn_dst": noise(key_of[4], (HEADS, HEAD_SIZE), (2 * HEAD_SIZE) ** -0.5, 0.25, (), jnp.float32),
        "bias": noise(key_of[5], (CONCAT,), 0.5, 3.0, (), jnp.float32),
        "gain": jnp.clip(1.0 + 0.1 * jax.random.normal(key_of[6], (CONCAT,), jnp.float32), 0.5, 1.5),
        "shift": noise(key_of[7], (CONCAT,), 0.5, 3.0, (), jnp.float32),
        "cotangent": noise(key_of[8], (NODES, CONCAT), 1.0, 6.0, ((0, 32),)),
        "neighbours": draw_neighbours(jax.random.fold_in(key_of[13], 71), 0),
        "edge_mask": draw_edge_mask(jax.random.fold_in(key_of[13], 71), 0),
        "node_mask": draw_node_mask(jax.random.fold_in(key_of[13], 71), 0),
        "send_index": draw_send_index(jax.random.fold_in(key_of[13], 71), 0),
    }


@jax.custom_vjp
def low(v):
    return lax.optimization_barrier(v.astype(jnp.bfloat16)).astype(jnp.float32)

@jax.custom_vjp
def low_back(v):
    return v

def low_keep(v):
    return (low(v), None)

def low_pass(kept, grad):
    return (grad,)

def back_keep(v):
    return (v, None)

def back_low(kept, grad):
    return (low(grad),)
low.defvjp(low_keep, low_pass)
low_back.defvjp(back_keep, back_low)

def leaky_soft(values):
    return 0.2 * values + 0.8 * jax.nn.softplus(values)

def global_rows(neighbours, send_index):
    local_slot = neighbours.reshape(PARTITIONS, NODE_DEV, DEG).astype(jnp.int32)
    owner = jnp.arange(PARTITIONS, dtype=jnp.int32)[:, None, None]
    below = jnp.clip(owner - 1, 0, PARTITIONS - 1).astype(jnp.int32)
    above = jnp.clip(owner + 1, 0, PARTITIONS - 1).astype(jnp.int32)
    slot_low = jnp.clip(local_slot - NODE_DEV, 0, HALO - 1).astype(jnp.int32)
    slot_high = jnp.clip(local_slot - NODE_DEV - HALO, 0, HALO - 1).astype(jnp.int32)
    row_low = send_index[below, 1, slot_low].astype(jnp.int32)
    row_high = send_index[above, 0, slot_high].astype(jnp.int32)
    inside = owner * NODE_DEV + local_slot
    from_low = below * NODE_DEV + row_low
    from_high = above * NODE_DEV + row_high
    joined = jnp.where(local_slot < NODE_DEV, inside, jnp.where(local_slot < NODE_DEV + HALO, from_low, from_high))
    return joined.reshape(NODES, DEG).astype(jnp.int32)

def reference(feats, w_proj, w_skip, attn_src, attn_dst, bias, gain, shift, cotangent, neighbours, edge_mask, node_mask, send_index):
    highest = lax.Precision.HIGHEST
    source_rows = global_rows(neighbours, send_index)
    live_mask = edge_mask.astype(jnp.int32)
    real = node_mask.astype(jnp.float32)[:, None]

    def forward(feat_f, proj_f, skip_f, src_vec, dst_vec, bias_vec, gain_vec, shift_vec):
        projected = jnp.dot(feat_f, proj_f, precision=highest)
        rounded = low(low_back(projected))
        head_rows = rounded.reshape(NODES, HEADS, HEAD_SIZE)
        el_source = lax.optimization_barrier(jnp.sum(head_rows * src_vec, axis=-1))
        el_target = lax.optimization_barrier(jnp.sum(head_rows * dst_vec, axis=-1))

        def block(pieces):
            self_rows, self_source, target_b, rows_b, mask_b = pieces
            scores = leaky_soft(el_source[rows_b] + target_b[:, None, :])
            self_score = leaky_soft(self_source + target_b)
            live = mask_b[:, :, None] > 0
            masked = jnp.where(live, scores, -1e+30)
            highest_score = jnp.maximum(self_score, lax.optimization_barrier(jnp.max(masked, axis=1)))
            weights = jnp.where(live, jnp.exp(masked - highest_score[:, None, :]), 0.0)
            self_weight = jnp.exp(self_score - highest_score)
            denominator = self_weight + lax.optimization_barrier(jnp.sum(weights, axis=1))
            gathered = head_rows[rows_b]
            summed = jnp.einsum('bkh,bkhc->bhc', weights / denominator[:, None, :], gathered, precision=highest)
            return (self_weight / denominator)[:, :, None] * self_rows + summed
        aggregated = lax.map(jax.checkpoint(block), (head_rows.reshape(PARTITIONS, NODE_DEV, HEADS, HEAD_SIZE), el_source.reshape(PARTITIONS, NODE_DEV, HEADS), el_target.reshape(PARTITIONS, NODE_DEV, HEADS), source_rows.reshape(PARTITIONS, NODE_DEV, DEG), live_mask.reshape(PARTITIONS, NODE_DEV, DEG)))
        aggregated = aggregated.reshape(NODES, CONCAT)
        skip_part = low_back(jnp.dot(feat_f, skip_f, precision=highest))
        pre_act = aggregated + skip_part + bias_vec
        activated = jax.nn.elu(pre_act)
        node_total = jnp.sum(real)
        mean_value = lax.optimization_barrier(jnp.sum(real * activated, axis=0)) / node_total
        variance = lax.optimization_barrier(jnp.sum(real * (activated - mean_value) ** 2, axis=0)) / node_total
        normed = (activated - mean_value) * lax.rsqrt(variance + 1e-05)
        return real * (gain_vec * normed + shift_vec)
    inputs = (feats.astype(jnp.float32), w_proj.astype(jnp.float32), w_skip.astype(jnp.float32), attn_src, attn_dst, bias, gain, shift)
    result, pullback = jax.vjp(forward, *inputs)
    grads = pullback(cotangent.astype(jnp.float32))
    return (result.astype(jnp.bfloat16), grads[0].astype(jnp.bfloat16), grads[1], grads[2], grads[3], grads[4], grads[5], grads[6], grads[7])
```

```python
import functools

import jax
import jax.numpy as jnp
from jax import lax
from jax.experimental import pallas as pl
from jax.experimental.pallas import tpu as pltpu
from jax.sharding import PartitionSpec as P

AXES = ("dom", "sub")
F32 = jnp.float32
BF16 = jnp.bfloat16
NEG = -1e30
STEP = 64
SHARDS = 16
CHUNK = 32
LANES = 128
VMEM = 56 * 1024 * 1024


def params(**more):
    return pltpu.CompilerParams(vmem_limit_bytes=VMEM, **more)


def mm(a, b, contract):
    return lax.dot_general(a, b, ((contract[:1], contract[1:]), ((), ())), preferred_element_type=F32)


def pad_rows(value, rows):
    extra = rows - value.shape[0]
    if extra == 0:
        return value
    return jnp.concatenate([value, jnp.zeros((extra,) + value.shape[1:], value.dtype)], axis=0)


def three_parts(value):
    high = value.astype(BF16)
    rest = value - high.astype(F32)
    middle = rest.astype(BF16)
    low = (rest - middle.astype(F32)).astype(BF16)
    return high, middle, low


def one_hot(rows, index_ref, side, scratch, width):
    halo = index_ref.shape[2]
    scratch[...] = jnp.full(scratch.shape, -1, jnp.int32)
    scratch[0:1, 0:halo] = index_ref[0, side : side + 1, :]
    wanted = scratch[0:1, 0:width]
    return (lax.broadcasted_iota(jnp.int32, (rows, width), 0) == wanted).astype(BF16)


def halo_rows_kernel(feats_ref, index_ref, down_ref, up_ref, scratch):
    rows = feats_ref.shape[0]
    for side, out in ((0, down_ref), (1, up_ref)):
        picked = one_hot(rows, index_ref, side, scratch, out.shape[0])
        out[...] = mm(picked, feats_ref[...], (0, 0)).astype(BF16)


def project_kernel(feats_ref, proj_ref, skip_w_ref, neighbours_ref, mask_ref, zq_ref, skip_ref, count_ref, padded_ref):
    node_rows = feats_ref.shape[0]
    rows, columns = count_ref.shape
    halo = (columns - rows) // 2

    @pl.when(pl.program_id(0) == 0)
    def _():
        padded_ref[...] = pad_rows(feats_ref[...].astype(F32), rows).astype(BF16)
        base = lax.broadcasted_iota(jnp.int32, (8, columns), 1)
        for start in range(0, rows, 8):
            own = lax.broadcasted_iota(jnp.int32, (8, columns), 0) + start
            total = (base == own).astype(F32)
            if start < node_rows:
                names = neighbours_ref[start : start + 8, :]
                live = mask_ref[start : start + 8, :] > 0
                names = jnp.where(live, names, -1)
                for slot in range(names.shape[1]):
                    total += (base == names[:, slot : slot + 1]).astype(F32)
            count_ref[start : start + 8, :] = total

    feats = padded_ref[...]
    zq_ref[...] = mm(feats, proj_ref[...], (1, 0)).astype(BF16)
    skip_ref[...] = mm(feats, skip_w_ref[...], (1, 0))


def attend_kernel(
    zq_ref, below_ref, above_ref, proj_ref, skip_ref, count_ref, src_ref, dst_ref, bias_ref, cot_ref, real_ref,
    ext_ref, weight_ref, slope_ref, pre_ref, stats_ref, halo_ref, target_scr,
):
    rows, columns = count_ref.shape
    half = (columns - rows) // 2

    @pl.when(pl.program_id(0) == 0)
    def _():
        halo_ref[...] = jnp.zeros_like(halo_ref)
        halo_ref[0 : below_ref.shape[0], :] = below_ref[...]
        halo_ref[half : half + above_ref.shape[0], :] = above_ref[...]

    ext_ref[0:rows, :] = zq_ref[...]
    ext_ref[rows:columns, :] = mm(halo_ref[...], proj_ref[...], (1, 0)).astype(BF16)
    ext = ext_ref[...]
    own = zq_ref[...]
    width = ext.shape[1]
    source = jnp.zeros((8, columns), F32)
    target = jnp.zeros((rows, LANES), F32)
    for part in three_parts(src_ref[0]):
        source += mm(jnp.broadcast_to(part, (8, width)), ext, (1, 1))
    for part in three_parts(dst_ref[0]):
        target += mm(own, jnp.broadcast_to(part, (LANES, width)), (1, 1))
    target_scr[...] = target
    source = source[0:1, :]

    def chunk(index, carry):
        where = pl.ds(pl.multiple_of(index * CHUNK, CHUNK), CHUNK)
        column = target_scr[where, :]
        value = jnp.concatenate([column] * (columns // LANES), axis=1) + source
        count = count_ref[where, :]
        small = jnp.exp(-jnp.abs(value))
        score = 0.2 * value + 0.8 * (jnp.maximum(value, 0.0) + jnp.log(1.0 + small))
        masked = jnp.where(count > 0, score, NEG)
        highest = jnp.max(masked, axis=1, keepdims=True)
        weight = jnp.exp(masked - highest) * count
        sigmoid = jnp.where(value >= 0, 1.0, small) / (1.0 + small)
        weight_ref[0, where, :] = weight.astype(BF16)
        slope_ref[0, where, :] = (weight * (0.2 + 0.8 * sigmoid)).astype(BF16)
        return carry

    lax.fori_loop(0, rows // CHUNK, chunk, 0)
    weights = weight_ref[0]
    total = mm(weights, jnp.ones((columns, LANES), BF16), (1, 0))
    scale = 1.0 / total
    scale = jnp.concatenate([scale] * (width // LANES), axis=1)
    pre = mm(weights, ext, (1, 0)) * scale + skip_ref[...] + bias_ref[...]
    pre_ref[...] = pre
    act = jnp.where(pre > 0, pre, jnp.exp(jnp.minimum(pre, 0.0)) - 1.0)
    real = real_ref[...]
    cot = pad_rows(cot_ref[...].astype(F32), rows) * real
    nodes = jnp.sum(jnp.broadcast_to(real, act.shape), axis=0, keepdims=True)
    mean = jnp.sum(act * real, axis=0, keepdims=True) / nodes
    centred = act - mean
    stats_ref[...] = jnp.zeros_like(stats_ref)
    stats_ref[0:1, :] = nodes
    stats_ref[1:2, :] = mean
    stats_ref[2:3, :] = jnp.sum(real * centred * centred, axis=0, keepdims=True)
    stats_ref[3:4, :] = jnp.sum(cot, axis=0, keepdims=True)
    stats_ref[4:5, :] = jnp.sum(cot * centred, axis=0, keepdims=True)


def merge(first, second):
    nodes = first[0:1] + second[0:1]
    gap = second[1:2] - first[1:2]
    part = second[0:1] / nodes
    mean = first[1:2] + gap * part
    spread = first[2:3] + second[2:3] + gap * gap * first[0:1] * part
    shift = first[3:4] + second[3:4]
    gain = first[4:5] + second[4:5] - (mean - first[1:2]) * first[3:4] - (mean - second[1:2]) * second[3:4]
    return jnp.concatenate([nodes, mean, spread, shift, gain, first[5:]], axis=0)


def place_blocks(out_ref, slot, value, me):
    size = value.shape[0] // SHARDS
    for block in range(SHARDS):
        at = pl.multiple_of((block ^ me) * size, size)
        out_ref[slot, pl.ds(at, size), :] = value[block * size : (block + 1) * size, :]


def norm_kernel(
    where_ref, pre_ref, stats_ref, cot_ref, real_ref, gain_ref, shift_ref, feats_ref,
    out_ref, dskip_ref, send_ref, keep_ref, bias_ref,
):
    rows = pre_ref.shape[0]
    node_rows = out_ref.shape[0]
    step = pl.program_id(0)
    pre = pre_ref[...]
    act = jnp.where(pre > 0, pre, jnp.exp(jnp.minimum(pre, 0.0)) - 1.0)
    steep = jnp.where(pre > 0, 1.0, jnp.exp(jnp.minimum(pre, 0.0)))
    real = real_ref[...]
    grad = pad_rows(cot_ref[...].astype(F32), rows) * real
    nodes = stats_ref[0:1, :]
    inverse = lax.rsqrt(stats_ref[2:3, :] / nodes + 1e-05)
    normed = (act - stats_ref[1:2, :]) * inverse
    gain = gain_ref[...]
    out_ref[...] = (real * (gain * normed + shift_ref[...]))[:node_rows].astype(BF16)
    grad_shift = stats_ref[3:4, :] / nodes
    grad_gain = stats_ref[4:5, :] * inverse / nodes
    grad_pre = real * (inverse * gain) * (grad - grad_shift - normed * grad_gain) * steep
    bias_ref[0] = jnp.broadcast_to(jnp.sum(grad_pre, axis=0, keepdims=True), bias_ref.shape[1:])
    dskip = grad_pre.astype(BF16)
    dskip_ref[...] = dskip
    grads = mm(feats_ref[...], dskip, (0, 0)).astype(BF16)

    @pl.when(step < 2)
    def _():
        place_blocks(send_ref, 0, grads, where_ref[4 + step % 2])

    @pl.when(step >= 2)
    def _():
        place_blocks(keep_ref, 0, grads, where_ref[4 + step % 2])


def back_kernel(
    where_ref, weight_ref, slope_ref, ext_ref, dskip_ref, src_ref, dst_ref, feats_ref, halo_ref,
    grad_ref, own_ref, below_ref, above_ref, small_ref, dal_scr, tgt_scr, inv_scr,
):
    rows, columns = weight_ref.shape[1:]
    half = (columns - rows) // 2
    width = ext_ref.shape[1]
    weights = weight_ref[0]
    ext = ext_ref[...]
    dskip = dskip_ref[...]
    dal_scr[...] = mm(dskip, ext, (1, 1))
    inverse = 1.0 / mm(weights, jnp.ones((columns, LANES), BF16), (1, 0))
    inv_scr[...] = inverse
    dst = dst_ref[0]

    def chunk(index, carry):
        by_source, by_target = carry
        where = pl.ds(pl.multiple_of(index * CHUNK, CHUNK), CHUNK)
        scale = jnp.concatenate([inv_scr[where, :]] * (columns // LANES), axis=1)
        dalpha = dal_scr[where, :]
        mean = jnp.sum(weight_ref[0, where, :].astype(F32) * scale * dalpha, axis=1, keepdims=True)
        du = slope_ref[0, where, :].astype(F32) * scale * (dalpha - mean)
        target = jnp.sum(du, axis=1, keepdims=True)
        tgt_scr[where, :] = target * dst
        by_target += (target * ext_ref[where, :].astype(F32)).reshape(CHUNK // 8, 8, width).sum(axis=0)
        by_source += du.reshape(CHUNK // 8, 8, columns).sum(axis=0)
        return by_source, by_target

    start = (jnp.zeros((8, columns), F32), jnp.zeros((8, width), F32))
    by_source, by_target = lax.fori_loop(0, rows // CHUNK, chunk, start)
    spread = jnp.concatenate([inverse] * (width // LANES), axis=1)
    scaled = (dskip.astype(F32) * spread).astype(BF16)
    dz = mm(weights, scaled, (0, 0))
    source = jnp.broadcast_to(jnp.sum(by_source, axis=0, keepdims=True), by_source.shape)
    dz += mm(source.astype(BF16), jnp.broadcast_to(src_ref[0] * 0.125, (8, width)).astype(BF16), (0, 0))
    dz_own = dz[:rows] + tgt_scr[...]
    own_ref[...] = dz_own
    dz_halo = dz[rows:].astype(BF16)
    below_ref[...] = dz_halo[: below_ref.shape[0]]
    above_ref[...] = dz_halo[half : half + above_ref.shape[0]]
    small_ref[0] = jnp.zeros(small_ref.shape[1:], F32)
    high, middle, low = three_parts(source)
    small_ref[0, 0:1, :] = (mm(high, ext, (1, 0)) + mm(middle, ext, (1, 0)) + mm(low, ext, (1, 0)))[0:1]
    small_ref[0, 1:2, :] = jnp.sum(by_target, axis=0, keepdims=True)
    grads = mm(feats_ref[...], dz_own.astype(BF16), (0, 0)) + mm(halo_ref[...], dz_halo, (0, 0))
    place_blocks(grad_ref, 0, grads.astype(BF16), where_ref[4 + pl.program_id(0)])


def feats_kernel(where_ref, send_ref, keep_ref, low_ref, high_ref, index_ref, dskip_ref, proj_ref, skip_ref, out_ref, total, picks, scratch):
    step = pl.program_id(0)
    rows = send_ref.shape[0]
    count = low_ref.shape[0]

    @pl.when(step == 0)
    def _():
        total[...] = jnp.zeros_like(total)
        picks[0] = one_hot(rows, index_ref, 1, scratch, count)
        picks[1] = one_hot(rows, index_ref, 0, scratch, count)

    own = jnp.where(step < 2, send_ref[...], keep_ref[...])
    own += mm(picks[0], high_ref[...], (1, 0)) + mm(picks[1], low_ref[...], (1, 0))
    total[...] += mm(own.astype(BF16), proj_ref[...], (1, 1)) + mm(dskip_ref[...], skip_ref[...], (1, 1))

    @pl.when(step == pl.num_programs(0) - 1)
    def _():
        out_ref[...] = total[: out_ref.shape[0]].astype(BF16)


def assemble_kernel(where_ref, send_ref, keep_ref, out_ref):
    step = pl.program_id(0)
    me = where_ref[4 + step % 2]
    size = out_ref.shape[0] // SHARDS
    for block in range(SHARDS):
        at = pl.multiple_of((block ^ me) * size, size)
        rows = slice(block * size, (block + 1) * size)
        out_ref[pl.ds(at, size), :] = jnp.where(step < 2, send_ref[0, rows, :], keep_ref[0, rows, :]).astype(F32)


def per_device(
    feats, w_proj, w_skip, attn_src, attn_dst, bias, gain, shift, cotangent, neighbours, edge_mask, node_mask, send_index,
):
    node_rows, depth = feats.shape
    heads, width = attn_src.shape
    concat = heads * width
    halo = send_index.shape[2]
    devices = lax.axis_size(AXES)
    bits = devices.bit_length() - 1
    rows = -(-node_rows // LANES) * LANES
    columns = rows + 2 * STEP
    halo_pad = -(-halo // 16) * 16
    me = lax.axis_index(AXES)
    pair_count = heads // 2

    def passed(value, steps):
        initial, last = (max(0, -steps), min(devices, devices - steps))
        return lax.ppermute(value, AXES, [(source, source + steps) for source in range(initial, last)])

    def swapped(value, bit):
        return lax.ppermute(value, AXES, [(source, source ^ (1 << bit)) for source in range(devices)])

    def bit(which):
        return (me >> which) & 1

    order_a, order_b = (2, 1, 3, 4), (1, 2, 3, 4)
    place_a = sum(bit(b) << (3 - i) for i, b in enumerate(order_a))
    place_b = sum(bit(b) << (3 - i) for i, b in enumerate(order_b))
    core = bit(0)
    where = jnp.stack([2 * (1 - core), 2 * (1 - core) + 1, 2 * core, 2 * core + 1, place_a, place_b]).astype(jnp.int32)
    where_send = where
    where_keep = jnp.concatenate([where[2:4], where[:2], where[4:]])

    real = jnp.pad(node_mask.astype(F32), (0, rows - node_rows))[:, None]
    names = neighbours + jnp.where(neighbours >= node_rows, rows - node_rows, 0)
    names = names + jnp.where(neighbours >= node_rows + halo, STEP - halo, 0)
    src3, dst3 = attn_src[:, None, :], attn_dst[:, None, :]
    bias2, gain2, shift2 = bias[None], gain[None], shift[None]

    down, up = pl.pallas_call(
        halo_rows_kernel,
        out_shape=[jax.ShapeDtypeStruct((halo_pad, depth), BF16)] * 2,
        scratch_shapes=[pltpu.VMEM((8, LANES), jnp.int32)],
        compiler_params=params(),
        name="halo_rows",
    )(feats, send_index)
    from_below = passed(up, 1)
    from_above = passed(down, -1)

    by_head = lambda n: pl.BlockSpec((n, width), lambda h: (0, h))
    whole = lambda *shape: pl.BlockSpec(shape, lambda *_: (0,) * len(shape))
    vector = pl.BlockSpec((1, 1, width), lambda h: (h, 0, 0))
    zq, skip, count, padded = pl.pallas_call(
        project_kernel,
        grid=(heads,),
        in_specs=[
            whole(node_rows, depth), by_head(depth), by_head(depth), whole(*neighbours.shape), whole(*edge_mask.shape),
        ],
        out_specs=[by_head(rows), by_head(rows), whole(rows, columns), whole(rows, depth)],
        out_shape=[
            jax.ShapeDtypeStruct((rows, concat), BF16),
            jax.ShapeDtypeStruct((rows, concat), F32),
            jax.ShapeDtypeStruct((rows, columns), F32),
            jax.ShapeDtypeStruct((rows, depth), BF16),
        ],
        compiler_params=params(),
        cost_estimate=pl.CostEstimate(flops=4 * rows * depth * concat, bytes_accessed=8_000_000, transcendentals=0),
        name="project",
    )(feats, w_proj, w_skip, names, edge_mask)

    by_edges = pl.BlockSpec((1, rows, columns), lambda h: (h, 0, 0))
    ext, weight, slope, pre, stats, halo_feats = pl.pallas_call(
        attend_kernel,
        grid=(heads,),
        in_specs=[
            by_head(rows), whole(halo_pad, depth), whole(halo_pad, depth), by_head(depth), by_head(rows),
            whole(rows, columns), vector, vector, by_head(1), by_head(node_rows), whole(rows, 1),
        ],
        out_specs=[
            by_head(columns), by_edges, by_edges, by_head(rows), by_head(8), whole(columns - rows, depth),
        ],
        out_shape=[
            jax.ShapeDtypeStruct((columns, concat), BF16),
            jax.ShapeDtypeStruct((heads, rows, columns), BF16),
            jax.ShapeDtypeStruct((heads, rows, columns), BF16),
            jax.ShapeDtypeStruct((rows, concat), F32),
            jax.ShapeDtypeStruct((8, concat), F32),
            jax.ShapeDtypeStruct((columns - rows, depth), BF16),
        ],
        scratch_shapes=[pltpu.VMEM((rows, LANES), F32)],
        compiler_params=params(),
        cost_estimate=pl.CostEstimate(flops=10**9, bytes_accessed=8_000_000, transcendentals=10**6),
        name="attend",
    )(zq, from_below, from_above, w_proj, skip, count, src3, dst3, bias2, cotangent, real)

    for which in range(bits):
        other = swapped(stats, which)
        mine_first = bit(which) == 0
        stats = merge(jnp.where(mine_first, stats, other), jnp.where(mine_first, other, stats))

    head_of = lambda n: pl.BlockSpec((n, width), lambda t, w: (0, w[t]))
    vector_of = pl.BlockSpec((1, 1, width), lambda t, w: (w[t], 0, 0))
    early = pl.BlockSpec((1, depth, width), lambda t, w: (jnp.minimum(t, 1), 0, 0))
    late = pl.BlockSpec((1, depth, width), lambda t, w: (jnp.maximum(t - 2, 0), 0, 0))
    half_grad = jax.ShapeDtypeStruct((2, depth, width), BF16)
    output, dskip, skip_send, skip_keep, bias_part = pl.pallas_call(
        norm_kernel,
        grid_spec=pltpu.PrefetchScalarGridSpec(
            num_scalar_prefetch=1,
            grid=(heads,),
            in_specs=[
                head_of(rows), head_of(8), head_of(node_rows), whole(rows, 1), head_of(1), head_of(1), whole(rows, depth),
            ],
            out_specs=[
                head_of(node_rows), head_of(rows), early, late, pl.BlockSpec((1, 8, width), lambda t, w: (w[t], 0, 0)),
            ],
        ),
        out_shape=[
            jax.ShapeDtypeStruct((node_rows, concat), BF16),
            jax.ShapeDtypeStruct((rows, concat), BF16),
            half_grad,
            half_grad,
            jax.ShapeDtypeStruct((heads, 8, width), F32),
        ],
        compiler_params=params(),
        cost_estimate=pl.CostEstimate(flops=2 * rows * depth * concat, bytes_accessed=8_000_000, transcendentals=0),
        name="norm",
    )(where, pre, stats, cotangent, real, gain2, shift2, padded)

    def backward(order):
        spec = lambda n: pl.BlockSpec((n, width), lambda t, w: (0, t))
        edges = pl.BlockSpec((1, rows, columns), lambda t, w: (w[t], 0, 0))
        return pl.pallas_call(
            back_kernel,
            grid_spec=pltpu.PrefetchScalarGridSpec(
                num_scalar_prefetch=1,
                grid=(2,),
                in_specs=[
                    edges, edges, head_of(columns), head_of(rows), vector_of, vector_of,
                    whole(rows, depth), whole(columns - rows, depth),
                ],
                out_specs=[
                    pl.BlockSpec((1, depth, width), lambda t, w: (t, 0, 0)), spec(rows), spec(halo_pad), spec(halo_pad),
                    pl.BlockSpec((1, 8, width), lambda t, w: (t, 0, 0)),
                ],
                scratch_shapes=[
                    pltpu.VMEM((rows, columns), F32), pltpu.VMEM((rows, width), F32), pltpu.VMEM((rows, LANES), F32),
                ],
            ),
            out_shape=[
                half_grad,
                jax.ShapeDtypeStruct((rows, 2 * width), F32),
                jax.ShapeDtypeStruct((halo_pad, 2 * width), BF16),
                jax.ShapeDtypeStruct((halo_pad, 2 * width), BF16),
                jax.ShapeDtypeStruct((2, 8, width), F32),
            ],
            compiler_params=params(),
            cost_estimate=pl.CostEstimate(flops=10**9, bytes_accessed=8_000_000, transcendentals=0),
            name="back",
        )(order, weight, slope, ext, dskip, src3, dst3, padded, halo_feats)

    proj_send, own_send, below_send, above_send, small_send = backward(where_send)
    proj_keep, own_keep, below_keep, above_keep, small_keep = backward(where_keep)

    def scatter(send, keep):
        both = keep + swapped(send, 0)
        one, two = both[0], both[1]
        for which in range(2):
            cut = one.shape[0] // 2
            one, two = (
                one[:cut] + swapped(one[cut:], order_a[which]),
                two[:cut] + swapped(two[cut:], order_b[which]),
            )
        both = jnp.stack([one, two])
        for which in order_a[2:]:
            cut = both.shape[1] // 2
            both = both[:, :cut] + swapped(both[:, cut:], which)
        for which in range(5, bits):
            both = both + swapped(both, which)
        return both

    def gather(both):
        for which in order_a[:1:-1]:
            both = jnp.concatenate([both, swapped(both, which)], axis=1)
        one, two = both[0], both[1]
        for which in (1, 0):
            one, two = (
                jnp.concatenate([one, swapped(one, order_a[which])], axis=0),
                jnp.concatenate([two, swapped(two, order_b[which])], axis=0),
            )
        both = jnp.stack([one, two])
        return pl.pallas_call(
            assemble_kernel,
            grid_spec=pltpu.PrefetchScalarGridSpec(
                num_scalar_prefetch=1, grid=(heads,), in_specs=[early, late], out_specs=head_of(depth)
            ),
            out_shape=jax.ShapeDtypeStruct((depth, concat), F32),
            compiler_params=params(),
            name="assemble",
        )(where, swapped(both, 0), both)

    grad_skip = gather(scatter(skip_send, skip_keep))
    back_below = passed(jnp.concatenate([below_send, below_keep], axis=1), -1)
    back_above = passed(jnp.concatenate([above_send, above_keep], axis=1), 1)
    grad_proj = gather(scatter(proj_send, proj_keep))

    pair = lambda first: pl.BlockSpec((rows, width), lambda t, w: (0, jnp.clip(t - first, 0, 1)))
    returned = pl.BlockSpec((halo_pad, width), lambda t, w: (0, (t + 2) % 4))
    grad_feats = pl.pallas_call(
        feats_kernel,
        grid_spec=pltpu.PrefetchScalarGridSpec(
            num_scalar_prefetch=1,
            grid=(heads,),
            in_specs=[
                pair(0), pair(2), returned, returned, whole(*send_index.shape), head_of(rows), head_of(depth), head_of(depth),
            ],
            out_specs=whole(node_rows, depth),
            scratch_shapes=[
                pltpu.VMEM((rows, depth), F32), pltpu.VMEM((2, rows, halo_pad), BF16), pltpu.VMEM((8, LANES), jnp.int32),
            ],
        ),
        out_shape=jax.ShapeDtypeStruct((node_rows, depth), BF16),
        compiler_params=params(),
        cost_estimate=pl.CostEstimate(flops=4 * rows * depth * concat, bytes_accessed=8_000_000, transcendentals=0),
        name="features",
    )(where, own_send, own_keep, back_above, back_below, send_index, dskip, w_proj, w_skip)

    small = jnp.where(
        core == 0,
        jnp.concatenate([small_keep, small_send], axis=0),
        jnp.concatenate([small_send, small_keep], axis=0),
    )[:, :2]
    small = jnp.concatenate([small, bias_part[:, :1]], axis=1)
    for which in range(bits):
        small = small + swapped(small, which)
    inverse = lax.rsqrt(stats[2] / stats[0] + 1e-05)
    return (
        output,
        grad_feats,
        grad_proj,
        grad_skip,
        small[:, 0],
        small[:, 1],
        small[:, 2].reshape(concat),
        stats[4] * inverse,
        stats[3],
    )


def solution(mesh):
    rows = P(AXES, None)
    in_specs = (rows,) + (P(),) * 7 + (rows, rows, rows, P(AXES), P(AXES, None, None))
    out_specs = (rows, rows) + (P(),) * 7
    return jax.shard_map(per_device, mesh=mesh, in_specs=in_specs, out_specs=out_specs, check_vma=False)
```

```python
import functools

import jax
import jax.numpy as jnp
from jax import lax
from jax.experimental import pallas as pl
from jax.experimental.pallas import tpu as pltpu
from jax.sharding import PartitionSpec as P

AXES = ("dom", "sub")
F32 = jnp.float32
BF16 = jnp.bfloat16
NEG = -1e30
LN2 = 0.6931471805599453
STEP = 64
SHARDS = 16
CHUNK = 32
LANES = 128
MIB = 1024 * 1024


def params(mib=24):
    return pltpu.CompilerParams(vmem_limit_bytes=mib * MIB)


def cost(us):
    return pl.CostEstimate(flops=int(us * 1.1e9), bytes_accessed=1_000_000, transcendentals=0)


def mm(a, b, contract):
    return lax.dot_general(a, b, ((contract[:1], contract[1:]), ((), ())), preferred_element_type=F32)


def pad_rows(value, rows):
    extra = rows - value.shape[0]
    if extra == 0:
        return value
    return jnp.concatenate([value, jnp.zeros((extra,) + value.shape[1:], value.dtype)], axis=0)


def three_parts(value):
    high = value.astype(BF16)
    rest = value - high.astype(F32)
    middle = rest.astype(BF16)
    low = (rest - middle.astype(F32)).astype(BF16)
    return high, middle, low


def repeat_lanes(value, columns):
    return jnp.concatenate([value] * (columns // value.shape[1]), axis=1)


def fold_rows(value):
    return value.reshape(value.shape[0] // 8, 8, value.shape[1])


def real_rows(mask_ref, rows, columns):
    count = jnp.sum(mask_ref[...].astype(F32), axis=1, keepdims=True)
    real = lax.broadcasted_iota(jnp.int32, (rows, columns), 0).astype(F32) < count
    return count, real


def one_hot(rows, index_ref, scratch):
    halo = index_ref.shape[2]
    scratch[...] = jnp.full(scratch.shape, -1, jnp.int32)
    scratch[0:1, 0:halo] = index_ref[0, 0:1, :]
    scratch[0:1, LANES : LANES + halo] = index_ref[0, 1:2, :]
    wanted = scratch[0:1, :]
    return (lax.broadcasted_iota(jnp.int32, (rows, 2 * LANES), 0) == wanted).astype(BF16)


def halo_rows_kernel(feats_ref, index_ref, down_ref, up_ref, scratch):
    picked = one_hot(feats_ref.shape[0], index_ref, scratch)
    rows = mm(picked, feats_ref[...], (0, 0)).astype(BF16)
    down_ref[...] = rows[: down_ref.shape[0]]
    up_ref[...] = rows[LANES : LANES + up_ref.shape[0]]


def project_kernel(
    where_ref, feats_ref, proj_ref, skip_w_ref, neighbours_ref, mask_ref, zq_ref, skip_ref, count_ref, flipped_ref, padded,
    *, halo,
):
    node_rows = feats_ref.shape[0]
    columns, rows = count_ref.shape

    @pl.when(pl.program_id(0) == 0)
    def _():
        feats = pad_rows(feats_ref[...].astype(F32), rows).astype(BF16)
        padded[...] = feats
        flipped_ref[...] = feats.T

    zq_ref[...] = mm(padded[...], proj_ref[...], (1, 0)).astype(BF16)
    skip_ref[...] = mm(padded[...], skip_w_ref[...], (1, 0))

    names = neighbours_ref[...]
    names = names + jnp.where(names >= node_rows, rows - node_rows, 0)
    names = names + jnp.where(names >= rows + halo, STEP - halo, 0)
    names = jnp.where(mask_ref[...] > 0, names, -1)
    names = jnp.concatenate([names, jnp.full((names.shape[0], rows - node_rows), -1, jnp.int32)], axis=1)
    own = lax.broadcasted_iota(jnp.int32, (8, rows), 1)
    share = columns // 4

    def chunk(index, carry):
        start = pl.multiple_of(pl.program_id(0) * share + index * 8, 8)
        source = lax.broadcasted_iota(jnp.int32, (8, rows), 0) + start
        total = (source == own).astype(F32)
        for slot in range(names.shape[0]):
            total += jnp.where(source == names[slot : slot + 1, :], 1.0, 0.0)
        count_ref[pl.ds(start, 8), :] = jnp.where(total > 0, jnp.log(jnp.maximum(total, 1.0)) * (1.0 / LN2), NEG)
        return carry

    lax.fori_loop(0, share // 8, chunk, 0)


def attend_kernel(
    zq_ref, below_ref, above_ref, proj_ref, skip_ref, count_ref, src_ref, dst_ref, bias_ref, cot_ref, mask_ref,
    ext_ref, weight_ref, source_ref, target_ref, scale_ref, pre_ref, stats_ref, flipped_ref, halo_scr, score_scr,
):
    columns, rows = count_ref.shape
    half = (columns - rows) // 2
    head = pl.program_id(0)

    @pl.when(head == 0)
    def _():
        halo_scr[...] = jnp.zeros_like(halo_scr)
        halo_scr[0 : below_ref.shape[0], :] = below_ref[...]
        halo_scr[half : half + above_ref.shape[0], :] = above_ref[...]
        flipped_ref[...] = halo_scr[...].T

    ext_ref[0:rows, :] = zq_ref[...]
    ext_ref[rows:columns, :] = mm(halo_scr[...], proj_ref[...], (1, 0)).astype(BF16)
    ext = ext_ref[...]
    width = ext.shape[1]
    parts = three_parts(src_ref[pl.ds(head, 1), :] * (1.0 / LN2))
    vectors = jnp.concatenate([jnp.broadcast_to(part, (LANES, width)) for part in parts], axis=0)
    source = mm(ext, vectors, (1, 1))
    source_ref[0] = source[:, :LANES] + source[:, LANES : 2 * LANES] + source[:, 2 * LANES :]
    parts = three_parts(dst_ref[pl.ds(head, 1), :] * (1.0 / LN2))
    vectors = jnp.concatenate([jnp.broadcast_to(part, (16, width)) for part in parts], axis=0)
    target = mm(vectors, zq_ref[...], (1, 1))
    target = target[0:8] + target[16:24] + target[32:40]
    target_ref[0] = target
    target = target[0:1]

    def score(index, highest):
        where = pl.ds(pl.multiple_of(index * CHUNK, CHUNK), CHUNK)
        value = repeat_lanes(source_ref[0, where, :], rows) + target
        small = jnp.exp2(-jnp.abs(value))
        result = jnp.maximum(value, 0.2 * value) + (0.8 / LN2) * jnp.log(1.0 + small) + count_ref[where, :]
        score_scr[where, :] = result
        return jnp.maximum(highest, jnp.max(fold_rows(result), axis=0))

    highest = lax.fori_loop(0, columns // CHUNK, score, jnp.full((8, rows), NEG, F32))
    highest = jnp.max(highest, axis=0, keepdims=True)

    def weigh(index, carry):
        where = pl.ds(pl.multiple_of(index * CHUNK, CHUNK), CHUNK)
        weight_ref[0, where, :] = jnp.exp2(score_scr[where, :] - highest).astype(BF16)
        return carry

    lax.fori_loop(0, columns // CHUNK, weigh, 0)
    weights = weight_ref[0]
    wide = jnp.concatenate([ext, jnp.ones((columns, LANES), BF16)], axis=1)
    summed = mm(weights, wide, (0, 0))
    scale = 1.0 / summed[:, width:]
    scale_ref[0] = scale
    pre = summed[:, :width] * repeat_lanes(scale, width) + skip_ref[...] + bias_ref[...]
    pre_ref[...] = pre
    act = jnp.where(pre > 0, pre, jnp.exp(jnp.minimum(pre, 0.0)) - 1.0)
    nodes, real = real_rows(mask_ref, rows, width)
    cot = jnp.where(real, pad_rows(cot_ref[...].astype(F32), rows), 0.0)
    mean = jnp.sum(jnp.where(real, act, 0.0), axis=0, keepdims=True) / nodes
    centred = jnp.where(real, act - mean, 0.0)
    stats_ref[...] = jnp.zeros_like(stats_ref)
    stats_ref[0:1, :] = jnp.broadcast_to(nodes, mean.shape)
    stats_ref[1:2, :] = mean
    stats_ref[2:3, :] = jnp.sum(centred * centred, axis=0, keepdims=True)
    stats_ref[3:4, :] = jnp.sum(cot, axis=0, keepdims=True)
    stats_ref[4:5, :] = jnp.sum(cot * centred, axis=0, keepdims=True)


def merged(first, second):
    nodes = first[0:1] + second[0:1]
    gap = second[1:2] - first[1:2]
    part = second[0:1] / nodes
    mean = first[1:2] + gap * part
    spread = first[2:3] + second[2:3] + gap * gap * first[0:1] * part
    shift = first[3:4] + second[3:4]
    gain = first[4:5] + second[4:5] - (mean - first[1:2]) * first[3:4] - (mean - second[1:2]) * second[3:4]
    return nodes, mean, spread, shift, gain


def in_order(mine, other, bit):
    mine_first = bit == 0
    return jnp.where(mine_first, mine, other), jnp.where(mine_first, other, mine)


def merge_kernel(where_ref, mine_ref, other_ref, out_ref, *, which):
    bit = (where_ref[6] >> which) & 1
    lines = merged(*in_order(mine_ref[...], other_ref[...], bit))
    out_ref[...] = jnp.zeros_like(out_ref)
    for line, value in enumerate(lines):
        out_ref[line : line + 1, :] = value


def place_blocks(out_ref, value, me):
    size = value.shape[0] // SHARDS
    for block in range(SHARDS):
        at = pl.multiple_of((block ^ me) * size, size)
        out_ref[pl.ds(at, size), :] = value[block * size : (block + 1) * size, :]


def core_sum_kernel(mine, other, out_refs):
    for out_index, out_ref in enumerate(out_refs):
        size = out_ref.shape[1]
        rows = slice(out_index * size, (out_index + 1) * size)
        for head in range(2):
            out_ref[head] = (mine(head, rows).astype(F32) + other(head, rows).astype(F32)).astype(BF16)


def share_sum_kernel(*refs, deps):
    ins, outs = refs[:4], refs[4 + deps :]
    size = outs[0].shape[1]
    for piece, out_ref in enumerate(outs):
        rows = slice(piece * size, (piece + 1) * size)
        total = ins[0][:, rows, :].astype(F32) + ins[1][:, rows, :].astype(F32)
        out_ref[...] = (total + ins[2][:, rows, :].astype(F32) + ins[3][:, rows, :].astype(F32)).astype(BF16)


def join_kernel(*refs):
    out_ref = refs[-1]
    size = refs[0].shape[1]
    for piece in range(4):
        out_ref[:, piece * size : (piece + 1) * size, :] = refs[piece][...]


def norm_kernel(
    where_ref, pre_ref, stats_ref, other_ref, cot_ref, mask_ref, gain_ref, shift_ref, flipped_ref,
    out_ref, dskip_ref, send_ref, keep_ref, small_ref, norm_grad_ref, *, last_bit,
):
    rows = pre_ref.shape[0]
    node_rows = out_ref.shape[0]
    step = pl.program_id(0)
    pre = pre_ref[...]
    steep = jnp.exp(jnp.minimum(pre, 0.0))
    act = jnp.where(pre > 0, pre, steep - 1.0)
    real = real_rows(mask_ref, rows, pre.shape[1])[1]
    first, second = in_order(stats_ref[...], other_ref[...], (where_ref[6] >> last_bit) & 1)
    nodes, mean, spread, total, cross = merged(first, second)
    inverse = lax.rsqrt(spread / nodes + 1e-05)
    normed = (act - mean) * inverse
    gain = gain_ref[...]
    out_ref[...] = jnp.where(real, gain * normed + shift_ref[...], 0.0)[:node_rows].astype(BF16)
    norm_grad_ref[...] = jnp.zeros_like(norm_grad_ref)
    norm_grad_ref[0:1, :] = cross * inverse
    norm_grad_ref[1:2, :] = total
    grad = pad_rows(cot_ref[...].astype(F32), rows) - total / nodes - normed * (cross * inverse / nodes)
    grad_pre = jnp.where(real, grad * (inverse * gain) * steep, 0.0)
    small_ref[0] = jnp.zeros(small_ref.shape[1:], F32)
    small_ref[0, 2:3, :] = jnp.sum(grad_pre, axis=0, keepdims=True)
    dskip = grad_pre.astype(BF16)
    dskip_ref[...] = dskip
    grads = mm(flipped_ref[...], dskip, (1, 0)).astype(BF16)

    @pl.when(step < 2)
    def _():
        place_blocks(send_ref.at[0], grads, where_ref[4])

    @pl.when(step >= 2)
    def _():
        place_blocks(keep_ref.at[0], grads, where_ref[4])


def back_kernel(
    where_ref, weight_ref, source_ref, target_ref, scale_ref, ext_ref, dskip_ref, src_ref, dst_ref, flipped_ref, halo_ref,
    small_in, *rest, part,
):
    send_ref, keep_ref, small_ref, own_ref, below_ref, above_ref, dal_scr, sum_scr = rest[-8:]
    columns, rows = weight_ref.shape[1:]
    half = (columns - rows) // 2
    width = ext_ref.shape[1]
    step = pl.program_id(0)
    head = where_ref[2 * step + part]
    ext = ext_ref[...]
    dskip = dskip_ref[...]
    dal_scr[...] = mm(ext, dskip, (1, 1))
    target = target_ref[0, 0:1, :]

    def average(index, carry):
        total, mean = carry
        where = pl.ds(pl.multiple_of(index * CHUNK, CHUNK), CHUNK)
        weight = weight_ref[0, where, :].astype(F32)
        return total + jnp.sum(fold_rows(weight), axis=0), mean + jnp.sum(fold_rows(weight * dal_scr[where, :]), axis=0)

    nothing = jnp.zeros((8, rows), F32)
    total, mean = lax.fori_loop(0, columns // CHUNK, average, (nothing, nothing))
    scale = 1.0 / jnp.sum(total, axis=0, keepdims=True)
    mean = jnp.sum(mean, axis=0, keepdims=True) * scale

    def slopes(index, by_target):
        where = pl.ds(pl.multiple_of(index * CHUNK, CHUNK), CHUNK)
        value = repeat_lanes(source_ref[0, where, :], rows) + target
        slope = (0.6 + 0.4 * jnp.tanh(value * (0.5 * LN2))) * scale
        du = weight_ref[0, where, :].astype(F32) * slope * (dal_scr[where, :] - mean)
        sum_scr[where, :] = sum(du[:, at : at + LANES] for at in range(0, rows, LANES))
        return by_target + jnp.sum(fold_rows(du), axis=0)

    by_target = lax.fori_loop(0, columns // CHUNK, slopes, nothing)
    by_target = jnp.sum(by_target, axis=0, keepdims=True)
    by_source = jnp.sum(sum_scr[...], axis=1, keepdims=True)
    scaled = (dskip.astype(F32) * repeat_lanes(scale_ref[0], width)).astype(BF16)
    dz = mm(weight_ref[0], scaled, (1, 0)) + by_source * src_ref[pl.ds(head, 1), :]
    high, middle, low = three_parts(by_target)
    row = lax.broadcasted_iota(jnp.int32, (16, rows), 0)
    lines = jnp.where(row == 1, middle.astype(F32), jnp.where(row == 3, low.astype(F32), high.astype(F32)))
    lines = jnp.where(row < 4, lines, 0.0).astype(BF16)
    dst_high, dst_middle, _ = three_parts(dst_ref[pl.ds(head, 1), :])
    row = lax.broadcasted_iota(jnp.int32, (16, width), 0)
    vectors = jnp.where(row == 2, dst_middle.astype(F32), dst_high.astype(F32)).astype(BF16)
    dz_own = dz[:rows] + mm(lines, vectors, (0, 0))
    own_ref[...] = dz_own
    dz_halo = dz[rows:].astype(BF16)
    below_ref[...] = dz_halo[: below_ref.shape[0]]
    above_ref[...] = dz_halo[half : half + above_ref.shape[0]]
    sums = mm(lines, ext[:rows], (1, 0))
    small_ref[0] = small_in[0]
    small_ref[0, 0:1, :] = jnp.sum(by_source * ext.astype(F32), axis=0, keepdims=True)
    small_ref[0, 1:2, :] = sums[0:1] + sums[1:2] + sums[3:4]
    grads = mm(flipped_ref[...], dz_own.astype(BF16), (1, 0)) + mm(halo_ref[...], dz_halo, (1, 0))
    grads = grads.astype(BF16)

    @pl.when(step == 0)
    def _():
        place_blocks(send_ref, grads, where_ref[4])

    @pl.when(step == 1)
    def _():
        place_blocks(keep_ref, grads, where_ref[4])


def feats_kernel(own_ref, low_ref, high_ref, index_ref, dskip_ref, proj_ref, skip_ref, out_ref, total, picks, scratch):
    step = pl.program_id(0)
    rows = own_ref.shape[0]
    count = low_ref.shape[0]

    @pl.when(step == 0)
    def _():
        total[...] = jnp.zeros_like(total)
        picks[...] = one_hot(rows, index_ref, scratch)

    own = own_ref[...] + mm(picks[:, :count], low_ref[...], (1, 0))
    own += mm(picks[:, LANES : LANES + count], high_ref[...], (1, 0))
    total[...] += mm(own.astype(BF16), proj_ref[...], (1, 1)) + mm(dskip_ref[...], skip_ref[...], (1, 1))

    @pl.when(step == pl.num_programs(0) - 1)
    def _():
        out_ref[...] = total[: out_ref.shape[0]].astype(BF16)


def assemble_kernel(where_ref, *refs):
    out_ref = refs[-1]
    me = where_ref[4]
    size = out_ref.shape[0] // SHARDS
    for block in range(SHARDS):
        at = pl.multiple_of((block ^ me) * size, size)
        rows = slice(block % 4 * size, (block % 4 + 1) * size)
        out_ref[pl.ds(at, size), :] = refs[block // 4][0, rows, :].astype(F32)


def per_device(
    feats, w_proj, w_skip, attn_src, attn_dst, bias, gain, shift, cotangent, neighbours, edge_mask, node_mask, send_index,
):
    node_rows, depth = feats.shape
    heads, width = attn_src.shape
    concat = heads * width
    slots = neighbours.shape[1]
    halo = send_index.shape[2]
    devices = lax.axis_size(AXES)
    bits = devices.bit_length() - 1
    rows = -(-node_rows // LANES) * LANES
    columns = rows + 2 * STEP
    halo_pad = -(-halo // 16) * 16
    me = lax.axis_index(AXES)

    def passed(value, steps):
        initial, last = (max(0, -steps), min(devices, devices - steps))
        return lax.ppermute(value, AXES, [(source, source + steps) for source in range(initial, last)])

    def swapped(value, distance):
        return lax.ppermute(value, AXES, [(source, source ^ distance) for source in range(devices)])

    def bit(which):
        return (me >> which) & 1

    place = ((me >> 1) & 3) * 4 + ((me >> 3) & 3)
    core = bit(0)
    send, keep = 2 * (1 - core), 2 * core
    where = jnp.stack([send, send + 1, keep, keep + 1, place, place, me]).astype(jnp.int32)

    mask = node_mask.reshape(1, node_rows)
    bias2, gain2, shift2 = bias[None], gain[None], shift[None]

    down, up = pl.pallas_call(
        halo_rows_kernel,
        out_shape=[jax.ShapeDtypeStruct((halo_pad, depth), BF16)] * 2,
        scratch_shapes=[pltpu.VMEM((8, 2 * LANES), jnp.int32)],
        compiler_params=params(8),
        name="halo_rows",
    )(feats, send_index)
    from_below = passed(up, 1)
    from_above = passed(down, -1)

    def spec(shape, index):
        return pl.BlockSpec(shape, index)

    def whole(*shape):
        return pl.BlockSpec(shape, lambda *_: (0,) * len(shape))

    by_head = lambda n: pl.BlockSpec((n, width), lambda h, *_: (0, h))
    stacked = lambda *shape: pl.BlockSpec((1, *shape), lambda h, *_: (h, 0, 0))
    shape_of = jax.ShapeDtypeStruct
    in_hbm = lambda value: pltpu.with_memory_space_constraint(value, pltpu.HBM)
    zq, skip, count, flipped = pl.pallas_call(
        lambda *refs: project_kernel(*refs, halo=halo),
        grid_spec=pltpu.PrefetchScalarGridSpec(
            num_scalar_prefetch=1,
            grid=(heads,),
            in_specs=[
                whole(node_rows, depth), by_head(depth), by_head(depth), whole(slots, node_rows), whole(slots, node_rows),
            ],
            out_specs=[by_head(rows), by_head(rows), whole(columns, rows), whole(depth, rows)],
            scratch_shapes=[pltpu.VMEM((rows, depth), BF16)],
        ),
        out_shape=[
            shape_of((rows, concat), BF16),
            shape_of((rows, concat), F32),
            shape_of((columns, rows), F32),
            shape_of((depth, rows), BF16),
        ],
        compiler_params=params(),
        cost_estimate=cost(5),
        name="project",
    )(where, in_hbm(feats), in_hbm(w_proj), in_hbm(w_skip), neighbours.T, edge_mask.T)

    ext, weight, source, target, scale, pre, stats, halo_flipped = pl.pallas_call(
        attend_kernel,
        grid=(heads,),
        in_specs=[
            by_head(rows), whole(halo_pad, depth), whole(halo_pad, depth), by_head(depth), by_head(rows),
            whole(columns, rows), whole(heads, width), whole(heads, width), by_head(1), by_head(node_rows),
            whole(1, node_rows),
        ],
        out_specs=[
            by_head(columns), stacked(columns, rows), stacked(columns, LANES), stacked(8, rows), stacked(rows, LANES),
            by_head(rows), by_head(8), whole(depth, columns - rows),
        ],
        out_shape=[
            shape_of((columns, concat), BF16),
            shape_of((heads, columns, rows), BF16),
            shape_of((heads, columns, LANES), F32),
            shape_of((heads, 8, rows), F32),
            shape_of((heads, rows, LANES), F32),
            shape_of((rows, concat), F32),
            shape_of((8, concat), F32),
            shape_of((depth, columns - rows), BF16),
        ],
        scratch_shapes=[pltpu.VMEM((columns - rows, depth), BF16), pltpu.VMEM((columns, rows), F32)],
        compiler_params=params(),
        cost_estimate=cost(8),
        name="attend",
    )(zq, from_below, from_above, in_hbm(w_proj), skip, count, attn_src, attn_dst, bias2, in_hbm(cotangent), mask)

    for which in range(bits - 1):
        stats = pl.pallas_call(
            functools.partial(merge_kernel, which=which),
            in_specs=[pl.BlockSpec(memory_space=pltpu.SMEM)] + [pl.BlockSpec(memory_space=pltpu.VMEM)] * 2,
            out_shape=shape_of(stats.shape, F32),
            compiler_params=params(1),
            name="merge",
        )(where, stats, swapped(stats, 1 << which))
    other = swapped(stats, 1 << (bits - 1))

    head_of = lambda n: pl.BlockSpec((n, width), lambda t, w: (0, w[t]))
    early = pl.BlockSpec((1, depth, width), lambda t, w: (jnp.minimum(t, 1), 0, 0))
    late = pl.BlockSpec((1, depth, width), lambda t, w: (jnp.maximum(t - 2, 0), 0, 0))
    half_grad = shape_of((2, depth, width), BF16)
    output, dskip, skip_send, skip_keep, small, norm_grad = pl.pallas_call(
        functools.partial(norm_kernel, last_bit=bits - 1),
        grid_spec=pltpu.PrefetchScalarGridSpec(
            num_scalar_prefetch=1,
            grid=(heads,),
            in_specs=[
                head_of(rows), head_of(8), head_of(8), head_of(node_rows), whole(1, node_rows), head_of(1), head_of(1),
                whole(depth, rows),
            ],
            out_specs=[
                head_of(node_rows), head_of(rows), early, late, pl.BlockSpec((1, 8, width), lambda t, w: (w[t], 0, 0)),
                head_of(8),
            ],
        ),
        out_shape=[
            shape_of((node_rows, concat), BF16),
            shape_of((rows, concat), BF16),
            half_grad,
            half_grad,
            shape_of((heads, 8, width), F32),
            shape_of((8, concat), F32),
        ],
        compiler_params=params(),
        cost_estimate=cost(4),
        name="norm",
    )(where, pre, stats, other, cotangent, mask, gain2, shift2, flipped)

    def backward(part, small, *rest):
        shared, deps = rest[:3], rest[3:]
        head_at = lambda n: pl.BlockSpec((n, width), lambda t, w: (0, w[2 * t + part]))
        stack_at = lambda *shape: pl.BlockSpec((1, *shape), lambda t, w: (w[2 * t + part], 0, 0))
        return pl.pallas_call(
            lambda *refs: back_kernel(*refs, part=part),
            grid_spec=pltpu.PrefetchScalarGridSpec(
                num_scalar_prefetch=1,
                grid=(2,),
                in_specs=[
                    stack_at(columns, rows), stack_at(columns, LANES), stack_at(8, rows), stack_at(rows, LANES),
                    head_at(columns), head_at(rows), whole(heads, width), whole(heads, width),
                    whole(depth, rows), whole(depth, columns - rows), stack_at(8, width),
                ] + [pl.BlockSpec(memory_space=pl.ANY)] * len(rest),
                out_specs=[
                    whole(depth, width), whole(depth, width), stack_at(8, width),
                    head_at(rows), head_at(halo_pad), head_at(halo_pad),
                ],
                scratch_shapes=[pltpu.VMEM((columns, rows), F32), pltpu.VMEM((columns, LANES), F32)],
            ),
            out_shape=[
                shape_of((depth, width), BF16),
                shape_of((depth, width), BF16),
                shape_of((heads, 8, width), F32),
                shape_of((rows, concat), F32),
                shape_of((halo_pad, concat), BF16),
                shape_of((halo_pad, concat), BF16),
            ],
            input_output_aliases={11 + i: 2 + i for i in range(1 + len(shared))},
            compiler_params=params(),
            cost_estimate=cost(6),
            name="back",
        )(where, weight, source, target, scale, ext, dskip, attn_src, attn_dst, flipped, halo_flipped, small, *rest)

    half = (2, depth, width)
    quarter = (2, depth // 4, width)
    piece = (2, depth // SHARDS, width)
    anywhere = pl.BlockSpec(memory_space=pl.ANY)
    vmem = pl.BlockSpec(memory_space=pltpu.VMEM)

    def step_call(kernel, name, shapes, arrays, deps=()):
        return pl.pallas_call(
            kernel,
            in_specs=[vmem] * len(arrays) + [anywhere] * len(deps),
            out_shape=[shape_of(shape, BF16) for shape in shapes],
            compiler_params=params(1),
            cost_estimate=cost(0.7),
            name=name,
        )(*arrays, *deps)

    def over_plane(shares):
        return [swapped(share, distance << 1) for distance, share in zip((1, 2, 3), shares)]

    def over_line(shares):
        return [swapped(share, distance << 3) for distance, share in zip((1, 2, 3), shares)]

    def skip_core_sum(keep_ref, other_ref, *refs):
        core_sum_kernel(lambda h, rows: keep_ref[h, rows, :], lambda h, rows: other_ref[h, rows, :], refs[-4:])

    def proj_core_sum(one_ref, two_ref, other_one, other_two, *refs):
        mine, other = (one_ref, two_ref), (other_one, other_two)
        core_sum_kernel(lambda h, rows: mine[h][rows, :], lambda h, rows: other[h][rows, :], refs[-4:])

    def share_sum(name, arrays, count, deps):
        shapes = [(2, arrays[0].shape[1] // count, width)] * count
        return step_call(functools.partial(share_sum_kernel, deps=len(deps)), name, shapes, arrays, deps)

    def join(name, arrays, deps):
        return step_call(join_kernel, name, [(2, 4 * arrays[0].shape[1], width)], arrays, deps)[0]

    def assemble(pieces, first, *out):
        def block(share):
            at = share if pieces[share].shape[1] == depth else 0
            return pl.BlockSpec((1, depth // 4, width), lambda t, w: (t, at, 0))

        return pl.pallas_call(
            assemble_kernel,
            grid_spec=pltpu.PrefetchScalarGridSpec(
                num_scalar_prefetch=1,
                grid=(2,),
                in_specs=[block(share) for share in range(4)] + [anywhere] * len(out),
                out_specs=pl.BlockSpec((depth, width), lambda t, w: (0, w[t + first])),
            ),
            out_shape=jax.ShapeDtypeStruct((depth, concat), F32),
            input_output_aliases={5: 0} if out else {},
            compiler_params=params(8),
            cost_estimate=cost(2),
            name="assemble",
        )(where, *pieces, *out)

    def beyond(value):
        for which in range(5, bits):
            value = value + swapped(value, 1 << which)
        return value

    skip_other = swapped(skip_send, 1)
    send_a, keep_a, small, own, below, above = backward(0, small)
    other_a = swapped(send_a, 1)
    s_mine, *s_rest = step_call(skip_core_sum, "s_core", [quarter] * 4, [skip_keep, skip_other], [keep_a])
    s_got = over_plane(s_rest)
    send_b, keep_b, small, own, below, above = backward(1, small, own, below, above, s_mine)
    other_b = swapped(send_b, 1)
    back_below = passed(below, -1)
    back_above = passed(above, 1)
    p_mine, *p_rest = step_call(proj_core_sum, "p_core", [quarter] * 4, [keep_a, keep_b, other_a, other_b])
    p_got = over_plane(p_rest)
    s_mine, *s_rest = share_sum("s_plane", [s_mine, *s_got], 4, [p_mine])
    s_got = over_line(s_rest)
    grad_feats = pl.pallas_call(
        feats_kernel,
        grid=(heads,),
        in_specs=[
            by_head(rows), by_head(halo_pad), by_head(halo_pad), whole(*send_index.shape), by_head(rows),
            by_head(depth), by_head(depth),
        ],
        out_specs=whole(node_rows, depth),
        scratch_shapes=[
            pltpu.VMEM((rows, depth), F32), pltpu.VMEM((rows, 2 * LANES), BF16), pltpu.VMEM((8, 2 * LANES), jnp.int32),
        ],
        out_shape=shape_of((node_rows, depth), BF16),
        compiler_params=params(),
        cost_estimate=cost(6),
        name="features",
    )(own, back_above, back_below, send_index, dskip, w_proj, w_skip)

    s_piece = beyond(share_sum("s_line", [s_mine, *s_got], 1, [grad_feats])[0])
    s_got = over_line([s_piece] * 3)
    p_mine, *p_rest = share_sum("p_plane", [p_mine, *p_got], 4, [s_piece])
    p_got = over_line(p_rest)
    s_share = join("s_join", [s_piece, *s_got], [p_mine])
    s_got = over_plane([s_share] * 3)
    p_piece = beyond(share_sum("p_line", [p_mine, *p_got], 1, [s_share])[0])
    p_got = over_line([p_piece] * 3)
    p_share = join("p_join", [p_piece, *p_got], [])
    p_got = [p_share, *over_plane([p_share] * 3)]
    s_half = join("s_half", [s_share, *s_got], [p_share])
    s_other = swapped(s_half, 1)
    grad_skip = assemble([s_other] * 4, 0, assemble([s_half] * 4, 2))
    grad_proj = assemble([swapped(share, 1) for share in p_got], 0, assemble(p_got, 2))

    for which in range(bits):
        small = small + swapped(small, 1 << which)
    return (
        output,
        grad_feats,
        grad_proj,
        grad_skip,
        small[:, 0],
        small[:, 1],
        small[:, 2].reshape(concat),
        norm_grad[0],
        norm_grad[1],
    )


def solution(mesh):
    rows = P(AXES, None)
    in_specs = (rows,) + (P(),) * 7 + (rows, rows, rows, P(AXES), P(AXES, None, None))
    out_specs = (rows, rows) + (P(),) * 7
    return jax.shard_map(per_device, mesh=mesh, in_specs=in_specs, out_specs=out_specs, check_vma=False)
```

```python
import functools

import jax
import jax.numpy as jnp
from jax import lax
from jax.experimental import pallas as pl
from jax.experimental.pallas import tpu as pltpu
from jax.sharding import PartitionSpec as P

AXES = ("dom", "sub")
F32 = jnp.float32
BF16 = jnp.bfloat16
NEG = -1e30
LN2 = 0.6931471805599453
STEP = 64
SHARDS = 16
CHUNK = 32
LANES = 128
MIB = 1024 * 1024


def params(mib=24):
    return pltpu.CompilerParams(vmem_limit_bytes=mib * MIB)


def cost(us):
    return pl.CostEstimate(flops=int(us * 1.1e9), bytes_accessed=int(us * 1e6), transcendentals=0)


def mm(a, b, contract):
    return lax.dot_general(a, b, ((contract[:1], contract[1:]), ((), ())), preferred_element_type=F32)


def pad_rows(value, rows):
    extra = rows - value.shape[0]
    if extra == 0:
        return value
    return jnp.concatenate([value, jnp.zeros((extra,) + value.shape[1:], value.dtype)], axis=0)


def three_parts(value):
    high = value.astype(BF16)
    rest = value - high.astype(F32)
    middle = rest.astype(BF16)
    low = (rest - middle.astype(F32)).astype(BF16)
    return high, middle, low


def two_parts(value):
    high = value.astype(BF16).astype(F32)
    return jnp.concatenate([high, value - high], axis=0).astype(BF16)


def whole_of(parts):
    parts = parts.astype(F32)
    return parts[:8] + parts[8:]


def repeat_lanes(value, columns):
    return jnp.concatenate([value] * (columns // value.shape[1]), axis=1)


def fold_rows(value):
    return value.reshape(value.shape[0] // 8, 8, value.shape[1])


def real_rows(mask_ref, rows, columns):
    count = jnp.sum(mask_ref[...].astype(F32), axis=1, keepdims=True)
    real = lax.broadcasted_iota(jnp.int32, (rows, columns), 0).astype(F32) < count
    return count, real


def one_hot(rows, index_ref, scratch, odd):
    halo = index_ref.shape[2]
    down, up = index_ref[0, 0:1, :], index_ref[0, 1:2, :]
    scratch[...] = jnp.full(scratch.shape, -1, jnp.int32)
    scratch[0:1, 0:halo] = jnp.where(odd, down, up)
    scratch[0:1, LANES : LANES + halo] = jnp.where(odd, up, down)
    wanted = scratch[0:1, :]
    return (lax.broadcasted_iota(jnp.int32, (rows, 2 * LANES), 0) == wanted).astype(BF16)


def own_index():
    return lax.axis_index(AXES[0]) * lax.axis_size(AXES[1]) + lax.axis_index(AXES[1])


def is_odd():
    return lax.axis_index(AXES[1]) % 2 == 1


def own_place():
    me = own_index()
    return (me // 2 % 4) * 4 + me // 8 % 4


def head_at(step):
    core = lax.axis_index(AXES[1]) % 2
    return (2 - 2 * core if step < 2 else 2 * core) + step % 2


def halo_rows_kernel(feats_ref, index_ref, near_ref, far_ref, scratch):
    picked = one_hot(feats_ref.shape[0], index_ref, scratch, is_odd())
    rows = mm(picked, feats_ref[...], (0, 0)).astype(BF16)
    near_ref[...] = rows[: near_ref.shape[0]]
    far_ref[...] = rows[LANES : LANES + far_ref.shape[0]]


def project_kernel(
    feats_ref, proj_ref, skip_w_ref, neighbours_ref, mask_ref, zq_ref, skip_ref, count_ref, flipped_ref, padded,
    *, halo,
):
    node_rows = feats_ref.shape[0]
    columns, rows = count_ref.shape

    @pl.when(pl.program_id(0) == 0)
    def _():
        feats = pad_rows(feats_ref[...].astype(F32), rows).astype(BF16)
        padded[...] = feats
        flipped_ref[...] = feats.T

    zq_ref[...] = mm(padded[...], proj_ref[...], (1, 0)).astype(BF16)
    skip_ref[...] = mm(padded[...], skip_w_ref[...], (1, 0))

    names = neighbours_ref[...]
    names = names + jnp.where(names >= node_rows, rows - node_rows, 0)
    names = names + jnp.where(names >= rows + halo, STEP - halo, 0)
    names = jnp.where(mask_ref[...] > 0, names, -1)
    names = jnp.concatenate([names, jnp.full((names.shape[0], rows - node_rows), -1, jnp.int32)], axis=1)
    own = lax.broadcasted_iota(jnp.int32, (8, rows), 1)
    share = columns // 4

    def chunk(index, carry):
        start = pl.multiple_of(pl.program_id(0) * share + index * 8, 8)
        source = lax.broadcasted_iota(jnp.int32, (8, rows), 0) + start
        total = (source == own).astype(F32)
        for slot in range(names.shape[0]):
            total += jnp.where(source == names[slot : slot + 1, :], 1.0, 0.0)
        count_ref[pl.ds(start, 8), :] = jnp.where(total > 0, jnp.log(jnp.maximum(total, 1.0)) * (1.0 / LN2), NEG)
        return carry

    lax.fori_loop(0, share // 8, chunk, 0, unroll=2)


def attend_kernel(
    zq_ref, near_ref, far_ref, proj_ref, skip_ref, count_ref, src_ref, dst_ref, bias_ref, cot_ref, mask_ref,
    ext_ref, weight_ref, source_ref, target_ref, scale_ref, pre_ref, stats_ref, flipped_ref, halo_scr, score_scr,
):
    columns, rows = count_ref.shape
    half = (columns - rows) // 2
    head = pl.program_id(0)

    @pl.when(head == 0)
    def _():
        halo_scr[...] = jnp.zeros_like(halo_scr)
        near_at = jnp.where(is_odd(), 0, half)
        halo_scr[pl.ds(pl.multiple_of(near_at, 16), near_ref.shape[0]), :] = near_ref[...]
        halo_scr[pl.ds(pl.multiple_of(half - near_at, 16), far_ref.shape[0]), :] = far_ref[...]
        flipped_ref[...] = halo_scr[...].T

    ext_ref[0:rows, :] = zq_ref[...]
    ext_ref[rows:columns, :] = mm(halo_scr[...], proj_ref[...], (1, 0)).astype(BF16)
    ext = ext_ref[...]
    width = ext.shape[1]
    parts = three_parts(src_ref[pl.ds(head, 1), :] * (1.0 / LN2))
    vectors = jnp.concatenate([jnp.broadcast_to(part, (LANES, width)) for part in parts], axis=0)
    source = mm(ext, vectors, (1, 1))
    source_ref[0] = source[:, :LANES] + source[:, LANES : 2 * LANES] + source[:, 2 * LANES :]
    parts = three_parts(dst_ref[pl.ds(head, 1), :] * (1.0 / LN2))
    vectors = jnp.concatenate([jnp.broadcast_to(part, (16, width)) for part in parts], axis=0)
    target = mm(vectors, zq_ref[...], (1, 1))
    target = target[0:8] + target[16:24] + target[32:40]
    target_ref[0] = target
    target = target[0:1]

    def score(index, highest):
        where = pl.ds(pl.multiple_of(index * CHUNK, CHUNK), CHUNK)
        value = repeat_lanes(source_ref[0, where, :], rows) + target
        small = jnp.exp2(-jnp.abs(value))
        result = jnp.maximum(value, 0.2 * value) + (0.8 / LN2) * jnp.log(1.0 + small) + count_ref[where, :]
        score_scr[where, :] = result
        return jnp.maximum(highest, jnp.max(fold_rows(result), axis=0))

    highest = lax.fori_loop(0, columns // CHUNK, score, jnp.full((8, rows), NEG, F32), unroll=2)
    highest = jnp.max(highest, axis=0, keepdims=True)

    def weigh(index, carry):
        where = pl.ds(pl.multiple_of(index * CHUNK, CHUNK), CHUNK)
        weight_ref[0, where, :] = jnp.exp2(score_scr[where, :] - highest).astype(BF16)
        return carry

    lax.fori_loop(0, columns // CHUNK, weigh, 0, unroll=2)
    weights = weight_ref[0]
    wide = jnp.concatenate([ext, jnp.ones((columns, LANES), BF16)], axis=1)
    summed = mm(weights, wide, (0, 0))
    scale = 1.0 / summed[:, width:]
    scale_ref[0] = scale
    pre = summed[:, :width] * repeat_lanes(scale, width) + skip_ref[...] + bias_ref[...]
    pre_ref[...] = pre
    act = jnp.where(pre > 0, pre, jnp.exp(jnp.minimum(pre, 0.0)) - 1.0)
    nodes, real = real_rows(mask_ref, rows, width)
    cot = jnp.where(real, pad_rows(cot_ref[...].astype(F32), rows), 0.0)
    mean = jnp.sum(jnp.where(real, act, 0.0), axis=0, keepdims=True) / nodes
    centred = jnp.where(real, act - mean, 0.0)
    stats_ref[...] = jnp.zeros_like(stats_ref)
    stats_ref[0:1, :] = jnp.broadcast_to(nodes, mean.shape)
    stats_ref[1:2, :] = mean
    stats_ref[2:3, :] = jnp.sum(centred * centred, axis=0, keepdims=True)
    stats_ref[3:4, :] = jnp.sum(cot, axis=0, keepdims=True)
    stats_ref[4:5, :] = jnp.sum(cot * centred, axis=0, keepdims=True)


def merged(first, second):
    nodes = first[0:1] + second[0:1]
    gap = second[1:2] - first[1:2]
    part = second[0:1] / nodes
    mean = first[1:2] + gap * part
    spread = first[2:3] + second[2:3] + gap * gap * first[0:1] * part
    shift = first[3:4] + second[3:4]
    gain = first[4:5] + second[4:5] - (mean - first[1:2]) * first[3:4] - (mean - second[1:2]) * second[3:4]
    return nodes, mean, spread, shift, gain


def in_order(mine, other, bit):
    mine_first = bit == 0
    return jnp.where(mine_first, mine, other), jnp.where(mine_first, other, mine)


def merge_kernel(mine_ref, other_ref, out_ref, *, which):
    bit = own_index() // 2**which % 2
    lines = merged(*in_order(mine_ref[...], other_ref[...], bit))
    out_ref[...] = jnp.zeros_like(out_ref)
    for line, value in enumerate(lines):
        out_ref[line : line + 1, :] = value


def place_blocks(out_ref, value, me):
    size = value.shape[0] // SHARDS
    for block in range(SHARDS):
        at = pl.multiple_of((block ^ me) * size, size)
        out_ref[pl.ds(at, size), :] = value[block * size : (block + 1) * size, :]


def core_shares_kernel(keep_ref, other_ref, *outs):
    size = keep_ref.shape[1] // 4 - 4
    for head in range(2):
        vectors = two_parts(whole_of(keep_ref[head, 4 * size :, :]) + whole_of(other_ref[head, 4 * size :, :]))
        for index, out_ref in enumerate(outs):
            rows = slice(index * size, (index + 1) * size)
            out_ref[head, :size, :] = (keep_ref[head, rows, :].astype(F32) + other_ref[head, rows, :].astype(F32)).astype(BF16)
            out_ref[head, size:, :] = vectors


def sum_of_four(refs, head, rows):
    first, second, third, fourth = (ref[head, rows, :].astype(F32) for ref in refs)
    return (first + second + third + fourth).astype(BF16)


def ordered_sum(refs, start, me, scratch):
    for index, ref in enumerate(refs):
        for head in range(2):
            scratch[index ^ me, head] = whole_of(ref[head, start:, :])
    return [scratch[0, head] + scratch[1, head] + scratch[2, head] + scratch[3, head] for head in range(2)]


def plane_sum_kernel(*refs, deps):
    ins, outs, scratch = refs[:4], refs[4 + deps : -1], refs[-1]
    size = outs[0].shape[1] - 16
    vectors = ordered_sum(ins, 4 * size, own_place() // 4, scratch)
    for head in range(2):
        for index, out_ref in enumerate(outs):
            out_ref[head, :size, :] = sum_of_four(ins, head, slice(index * size, (index + 1) * size))
            out_ref[head, size:, :] = two_parts(vectors[head])


def line_sum_kernel(*refs, deps):
    ins, (out_ref, small_ref, scratch) = refs[:4], refs[4 + deps :]
    size = out_ref.shape[1]
    vectors = ordered_sum(ins, size, own_place() % 4, scratch)
    for head in range(2):
        out_ref[head] = sum_of_four(ins, head, slice(0, size))
        small_ref[head] = vectors[head]


def vectors_kernel(mine_ref, other_ref, src_ref, dst_ref, bias_ref):
    odd = is_odd()
    width = src_ref.shape[1]
    for head in range(4):
        mine, other = mine_ref[head % 2], other_ref[head % 2]
        value = jnp.where(odd == (head >= 2), mine, other)
        src_ref[head : head + 1, :] = value[0:1]
        dst_ref[head : head + 1, :] = value[1:2]
        bias_ref[:, head * width : (head + 1) * width] = value[2:3]


def share_sum_kernel(*refs, deps):
    ins, outs = refs[:4], refs[4 + deps :]
    size = outs[0].shape[1]
    for head in range(2):
        for index, out_ref in enumerate(outs):
            out_ref[head] = sum_of_four(ins, head, slice(index * size, (index + 1) * size))


def join_kernel(*refs):
    out_ref = refs[-1]
    size = refs[0].shape[1]
    for piece in range(4):
        out_ref[:, piece * size : (piece + 1) * size, :] = refs[piece][...]


def two_sum_kernel(mine_ref, other_ref, *outs, deps=0):
    outs = outs[deps:]
    size = outs[0].shape[1]
    for piece, out_ref in enumerate(outs):
        rows = slice(piece * size, (piece + 1) * size)
        out_ref[...] = (mine_ref[:, rows, :].astype(F32) + other_ref[:, rows, :].astype(F32)).astype(BF16)


def norm_kernel(
    pre_ref, stats_ref, other_ref, cot_ref, mask_ref, gain_ref, shift_ref, flipped_ref,
    out_ref, dskip_ref, send_ref, keep_ref, small_ref, gain_grad_ref, shift_grad_ref, out_scr, done, *, last_bit,
):
    rows = pre_ref.shape[0]
    node_rows, width = out_scr.shape[1:]
    real = real_rows(mask_ref, rows, width)[1]
    copies = []
    for step in range(4):
        head = head_at(step)
        lanes = pl.ds(pl.multiple_of(head * width, width), width)
        pre = pre_ref[:, lanes]
        steep = jnp.exp(jnp.minimum(pre, 0.0))
        act = jnp.where(pre > 0, pre, steep - 1.0)
        first, second = in_order(stats_ref[:, lanes], other_ref[:, lanes], own_index() // 2**last_bit % 2)
        nodes, mean, spread, total, cross = merged(first, second)
        inverse = lax.rsqrt(spread / nodes + 1e-05)
        normed = (act - mean) * inverse
        gain = gain_ref[:, lanes]
        out_scr[step] = jnp.where(real, gain * normed + shift_ref[:, lanes], 0.0)[:node_rows].astype(BF16)
        copies.append(pltpu.make_async_copy(out_scr.at[step], out_ref.at[:, lanes], done.at[step]))
        copies[-1].start()
        gain_grad_ref[:, lanes] = cross * inverse
        shift_grad_ref[:, lanes] = total
        grad = pad_rows(cot_ref[:, lanes].astype(F32), rows) - total / nodes - normed * (cross * inverse / nodes)
        grad_pre = jnp.where(real, grad * (inverse * gain) * steep, 0.0)
        small_ref[head] = jnp.broadcast_to(jnp.sum(grad_pre, axis=0, keepdims=True), small_ref.shape[1:])
        dskip = grad_pre.astype(BF16)
        dskip_ref[:, lanes] = dskip
        grads = mm(flipped_ref[...], dskip, (1, 0)).astype(BF16)
        place_blocks((send_ref if step < 2 else keep_ref).at[step % 2], grads, own_place())
    for copy in copies:
        copy.wait()


def back_kernel(
    weight_ref, source_ref, target_ref, scale_ref, ext_ref, dskip_ref, src_ref, dst_ref, flipped_ref, halo_ref,
    small_in, *rest, part,
):
    grad_ref, own_ref, near_ref, far_ref, dal_scr, sum_scr = rest[-6:]
    columns, rows = weight_ref.shape[1:]
    half = (columns - rows) // 2
    width = src_ref.shape[1]
    depth = flipped_ref.shape[0]
    count = near_ref.shape[0]
    if part:
        near_ref[:, : 2 * width] = rest[0][...]
        far_ref[:, : 2 * width] = rest[1][...]
    for step in range(2):
        head = head_at(part + step)
        lanes = pl.ds(pl.multiple_of(head * width, width), width)
        target = target_ref[head, 0:1, :]
        dskip = dskip_ref[:, lanes]
        dal_scr[...] = mm(ext_ref[:, lanes], dskip, (1, 1))

        def average(index, carry):
            total, mean = carry
            where = pl.ds(pl.multiple_of(index * CHUNK, CHUNK), CHUNK)
            weight = weight_ref[head, where, :].astype(F32)
            return total + jnp.sum(fold_rows(weight), axis=0), mean + jnp.sum(fold_rows(weight * dal_scr[where, :]), axis=0)

        nothing = jnp.zeros((8, rows), F32)
        total, mean = lax.fori_loop(0, columns // CHUNK, average, (nothing, nothing), unroll=2)
        scale = 1.0 / jnp.sum(total, axis=0, keepdims=True)
        mean = jnp.sum(mean, axis=0, keepdims=True) * scale

        def slopes(index, by_target):
            where = pl.ds(pl.multiple_of(index * CHUNK, CHUNK), CHUNK)
            value = repeat_lanes(source_ref[head, where, :], rows) + target
            slope = (0.6 + 0.4 * jnp.tanh(value * (0.5 * LN2))) * scale
            du = weight_ref[head, where, :].astype(F32) * slope * (dal_scr[where, :] - mean)
            sum_scr[where, :] = sum(du[:, at : at + LANES] for at in range(0, rows, LANES))
            return by_target + jnp.sum(fold_rows(du), axis=0)

        by_target = lax.fori_loop(0, columns // CHUNK, slopes, nothing, unroll=2)
        by_target = jnp.sum(by_target, axis=0, keepdims=True)
        by_source = jnp.sum(sum_scr[...], axis=1, keepdims=True)
        ext = ext_ref[:, lanes]
        scaled = (dskip.astype(F32) * repeat_lanes(scale_ref[head], width)).astype(BF16)
        dz = mm(weight_ref[head], scaled, (1, 0)) + by_source * src_ref[pl.ds(head, 1), :]
        high, middle, low = three_parts(by_target)
        row = lax.broadcasted_iota(jnp.int32, (16, rows), 0)
        lines = jnp.where(row == 1, middle.astype(F32), jnp.where(row == 3, low.astype(F32), high.astype(F32)))
        lines = jnp.where(row < 4, lines, 0.0).astype(BF16)
        dst_high, dst_middle, _ = three_parts(dst_ref[pl.ds(head, 1), :])
        row = lax.broadcasted_iota(jnp.int32, (16, width), 0)
        vectors = jnp.where(row == 2, dst_middle.astype(F32), dst_high.astype(F32)).astype(BF16)
        dz_own = dz[:rows] + mm(lines, vectors, (0, 0))
        mine = slice(step * width, (step + 1) * width)
        dz_own = dz_own.astype(BF16)
        own_ref[:, mine] = dz_own
        dz_halo = dz[rows:].astype(BF16)
        below, above = dz[rows : rows + count], dz[rows + half : rows + half + count]
        odd = is_odd()
        at = part * width + step * width
        near_ref[:, at : at + width] = jnp.where(odd, below, above).astype(BF16)
        far_ref[:, at : at + width] = jnp.where(odd, above, below).astype(BF16)
        sums = mm(lines, ext[:rows], (1, 0))
        source_sum = jnp.sum(by_source * ext.astype(F32), axis=0, keepdims=True)
        row = lax.broadcasted_iota(jnp.int32, (8, width), 0)
        lines = jnp.where(row == 0, source_sum, jnp.where(row == 1, sums[0:1] + sums[1:2] + sums[3:4], small_in[head]))
        grad_ref[step, depth:, :] = two_parts(jnp.where(row < 3, lines, 0.0))
        grads = mm(flipped_ref[...], dz_own, (1, 0)) + mm(halo_ref[...], dz_halo, (1, 0))
        place_blocks(grad_ref.at[step], grads.astype(BF16), own_place())


def feats_kernel(own_one, own_two, dskip_ref, proj_ref, skip_ref, total_ref):
    width = own_one.shape[1] // 2
    total = mm(dskip_ref[...], skip_ref[...], (1, 1))
    for step in range(4):
        lanes = pl.ds(pl.multiple_of(head_at(step) * width, width), width)
        own = (own_one if step < 2 else own_two)[:, step % 2 * width : (step % 2 + 1) * width]
        total += mm(own, proj_ref[:, lanes], (1, 1))
    total_ref[...] = total


def feats_halo_kernel(total_ref, near_ref, far_ref, index_ref, proj_ref, out_ref, scratch):
    rows = total_ref.shape[0]
    count = near_ref.shape[0]
    width = near_ref.shape[1] // 4
    picks = one_hot(rows, index_ref, scratch, is_odd())
    picks = jnp.concatenate([picks[:, :count], picks[:, LANES : LANES + count]], axis=1)
    sent = jnp.concatenate([near_ref[...], far_ref[...]], axis=0)
    product = jnp.zeros((2 * count, proj_ref.shape[0]), F32)
    for step in range(4):
        lanes = pl.ds(pl.multiple_of(head_at(step) * width, width), width)
        other = (step + 2) % 4 * width
        product += mm(sent[:, other : other + width], proj_ref[:, lanes], (1, 1))
    high, middle, _ = three_parts(product)
    total = total_ref[...] + mm(picks, high, (1, 0)) + mm(picks, middle, (1, 0))
    out_ref[...] = total[: out_ref.shape[0]].astype(BF16)


def assemble_kernel(*refs, first, pieces):
    out_ref, scratch, done = refs[-3:]
    size, width = scratch.shape[2:]
    me = own_place()
    each = SHARDS // pieces
    copies = []
    for step in range(2):
        lanes = pl.ds(pl.multiple_of(head_at(first + step) * width, width), width)
        for block in range(SHARDS):
            at = pl.multiple_of((block ^ me) * size, size)
            rows = slice(block % each * size, (block % each + 1) * size)
            scratch[step, block] = refs[block // each][step, rows, :].astype(F32)
            copies.append(pltpu.make_async_copy(scratch.at[step, block], out_ref.at[pl.ds(at, size), lanes], done.at[step, block]))
            copies[-1].start()
    for copy in copies:
        copy.wait()


def per_device(
    feats, w_proj, w_skip, attn_src, attn_dst, bias, gain, shift, cotangent, neighbours, edge_mask, node_mask, send_index,
):
    node_rows, depth = feats.shape
    heads, width = attn_src.shape
    concat = heads * width
    slots = neighbours.shape[1]
    halo = send_index.shape[2]
    devices = lax.axis_size(AXES)
    bits = devices.bit_length() - 1
    rows = -(-node_rows // LANES) * LANES
    columns = rows + 2 * STEP
    halo_pad = -(-halo // 16) * 16

    def far_swapped(value):
        pairs = [(low, low + 1) for low in range(1, devices - 1, 2)]
        return lax.ppermute(value, AXES, pairs + [(high, low) for low, high in pairs])

    def swapped(value, distance):
        return lax.ppermute(value, AXES, [(source, source ^ distance) for source in range(devices)])

    mask = node_mask.reshape(1, node_rows)
    bias2, gain2, shift2 = bias[None], gain[None], shift[None]

    in_hbm = lambda value: pltpu.with_memory_space_constraint(value, pltpu.HBM)
    near, far = pl.pallas_call(
        halo_rows_kernel,
        out_shape=[jax.ShapeDtypeStruct((halo_pad, depth), BF16)] * 2,
        scratch_shapes=[pltpu.VMEM((8, 2 * LANES), jnp.int32)],
        compiler_params=params(8),
        name="halo_rows",
    )(in_hbm(feats), in_hbm(send_index))
    near, far = swapped(near, 1), far_swapped(far)

    def spec(shape, index):
        return pl.BlockSpec(shape, index)

    def whole(*shape):
        return pl.BlockSpec(shape, lambda *_: (0,) * len(shape))

    by_head = lambda n: pl.BlockSpec((n, width), lambda h, *_: (0, h))
    stacked = lambda *shape: pl.BlockSpec((1, *shape), lambda h, *_: (h, 0, 0))
    shape_of = jax.ShapeDtypeStruct
    zq, skip, count, flipped = pl.pallas_call(
        functools.partial(project_kernel, halo=halo),
        grid=(heads,),
        in_specs=[
            whole(node_rows, depth), by_head(depth), by_head(depth), whole(slots, node_rows), whole(slots, node_rows),
        ],
        out_specs=[by_head(rows), by_head(rows), whole(columns, rows), whole(depth, rows)],
        scratch_shapes=[pltpu.VMEM((rows, depth), BF16)],
        out_shape=[
            shape_of((rows, concat), BF16),
            shape_of((rows, concat), F32),
            shape_of((columns, rows), F32),
            shape_of((depth, rows), BF16),
        ],
        compiler_params=params(),
        cost_estimate=cost(5),
        name="project",
    )(in_hbm(feats), in_hbm(w_proj), in_hbm(w_skip), in_hbm(neighbours.T), in_hbm(edge_mask.T))

    ext, weight, source, target, scale, pre, stats, halo_flipped = pl.pallas_call(
        attend_kernel,
        grid=(heads,),
        in_specs=[
            by_head(rows), whole(halo_pad, depth), whole(halo_pad, depth), by_head(depth), by_head(rows),
            whole(columns, rows), whole(heads, width), whole(heads, width), by_head(1), by_head(node_rows),
            whole(1, node_rows),
        ],
        out_specs=[
            by_head(columns), stacked(columns, rows), stacked(columns, LANES), stacked(8, rows), stacked(rows, LANES),
            by_head(rows), by_head(8), whole(depth, columns - rows),
        ],
        out_shape=[
            shape_of((columns, concat), BF16),
            shape_of((heads, columns, rows), BF16),
            shape_of((heads, columns, LANES), F32),
            shape_of((heads, 8, rows), F32),
            shape_of((heads, rows, LANES), F32),
            shape_of((rows, concat), F32),
            shape_of((8, concat), F32),
            shape_of((depth, columns - rows), BF16),
        ],
        scratch_shapes=[pltpu.VMEM((columns - rows, depth), BF16), pltpu.VMEM((columns, rows), F32)],
        compiler_params=params(),
        cost_estimate=cost(8),
        name="attend",
    )(zq, near, far, in_hbm(w_proj), skip, count, attn_src, attn_dst, bias2, in_hbm(cotangent), mask)

    for which in range(bits - 1):
        stats = pl.pallas_call(
            functools.partial(merge_kernel, which=which),
            in_specs=[pl.BlockSpec(memory_space=pltpu.VMEM)] * 2,
            out_shape=shape_of(stats.shape, F32),
            compiler_params=params(1),
            name="merge",
        )(stats, swapped(stats, 1 << which))
    other = swapped(stats, 1 << (bits - 1))

    vmem = pl.BlockSpec(memory_space=pltpu.VMEM)
    anywhere = pl.BlockSpec(memory_space=pl.ANY)
    half_grad = shape_of((2, depth, width), BF16)
    output, dskip, skip_send, skip_keep, small, gain_grad, shift_grad = pl.pallas_call(
        functools.partial(norm_kernel, last_bit=bits - 1),
        in_specs=[vmem] * 8,
        out_specs=[anywhere] + [vmem] * 6,
        out_shape=[
            pltpu.HBM((node_rows, concat), BF16),
            shape_of((rows, concat), BF16),
            half_grad,
            half_grad,
            shape_of((heads, 8, width), F32),
            jax.ShapeDtypeStruct((1, concat), F32),
            jax.ShapeDtypeStruct((1, concat), F32),
        ],
        scratch_shapes=[pltpu.VMEM((heads, node_rows, width), BF16), pltpu.SemaphoreType.DMA((heads,))],
        compiler_params=params(16),
        cost_estimate=cost(0.1),
        name="norm",
    )(pre, stats, other, cotangent, mask, gain2, shift2, flipped)

    def backward(part, arrays=(), deps=()):
        return pl.pallas_call(
            functools.partial(back_kernel, part=part),
            in_specs=[vmem] * (11 + len(arrays)) + [anywhere] * len(deps),
            out_shape=[
                shape_of((2, depth + 16, width), BF16),
                shape_of((rows, 2 * width), BF16),
                shape_of((halo_pad, (2 + part) * width), BF16),
                shape_of((halo_pad, (2 + part) * width), BF16),
            ],
            scratch_shapes=[pltpu.VMEM((columns, rows), F32), pltpu.VMEM((columns, LANES), F32)],
            compiler_params=params(8),
            cost_estimate=cost(0.1),
            name="back",
        )(weight, source, target, scale, ext, dskip, attn_src, attn_dst, flipped, halo_flipped, small, *arrays, *deps)

    quarter = (2, depth // 4, width)
    piece = (2, depth // SHARDS, width)
    def step_call(kernel, name, shapes, arrays, deps=()):
        return pl.pallas_call(
            kernel,
            in_specs=[vmem] * len(arrays) + [anywhere] * len(deps),
            out_shape=[shape_of(shape, BF16) for shape in shapes],
            compiler_params=params(1),
            cost_estimate=cost(0.1),
            name=name,
        )(*arrays, *deps)

    def over_plane(shares):
        return [swapped(share, distance << 1) for distance, share in zip((1, 2, 3), shares)]

    def over_line(shares):
        return [swapped(share, distance << 3) for distance, share in zip((1, 2, 3), shares)]

    def ordered_call(kernel, name, shapes, arrays, deps):
        return pl.pallas_call(
            functools.partial(kernel, deps=len(deps)),
            in_specs=[vmem] * len(arrays) + [anywhere] * len(deps),
            out_shape=shapes,
            scratch_shapes=[pltpu.VMEM((4, 2, 8, width), F32)],
            compiler_params=params(1),
            cost_estimate=cost(0.1),
            name=name,
        )(*arrays, *deps)

    def plane_sum(arrays, deps):
        shapes = [shape_of((2, depth // SHARDS + 16, width), BF16)] * 4
        return ordered_call(plane_sum_kernel, "p_plane", shapes, arrays, deps)

    def line_sum(arrays, deps):
        shapes = [shape_of(piece, BF16), shape_of((2, 8, width), F32)]
        return ordered_call(line_sum_kernel, "p_line", shapes, arrays, deps)

    def share_sum(name, arrays, count, deps):
        shapes = [(2, arrays[0].shape[1] // count, width)] * count
        return step_call(functools.partial(share_sum_kernel, deps=len(deps)), name, shapes, arrays, deps)

    def join(name, arrays, deps):
        return step_call(join_kernel, name, [(2, 4 * arrays[0].shape[1], width)], arrays, deps)[0]

    def assemble(pieces, first, *out):
        return pl.pallas_call(
            functools.partial(assemble_kernel, first=first, pieces=len(pieces)),
            in_specs=[vmem] * len(pieces) + [anywhere] * len(out),
            out_specs=anywhere,
            out_shape=pltpu.HBM((depth, concat), F32),
            scratch_shapes=[pltpu.VMEM((2, SHARDS, depth // SHARDS, width), F32), pltpu.SemaphoreType.DMA((2, SHARDS))],
            input_output_aliases={len(pieces): 0} if out else {},
            compiler_params=params(8),
            cost_estimate=cost(0.1),
            name="assemble",
        )(*pieces, *out)

    def beyond(value):
        for which in range(5, bits):
            value = value + swapped(value, 1 << which)
        return value

    def after(value, *others):
        return lax.optimization_barrier((value, *others))[0]

    skip_other = swapped(skip_send, 1)
    proj_send, own_send, near_send, far_send = backward(0)
    proj_other = swapped(proj_send, 1)
    s_mine, *s_rest = step_call(
        functools.partial(two_sum_kernel, deps=1), "s_core", [quarter] * 4, [skip_keep, skip_other], [proj_send]
    )
    s_got = over_plane(s_rest)
    proj_keep, own_keep, back_near, back_far = backward(2, [near_send, far_send], [s_mine])
    p_mine, *p_rest = step_call(core_shares_kernel, "p_core", [(2, depth // 4 + 16, width)] * 4, [proj_keep, proj_other])
    p_got = over_plane(p_rest)
    s_mine, *s_rest = share_sum("s_plane", [s_mine, *s_got], 4, [p_mine])
    s_got = over_line(s_rest)
    s_piece = beyond(share_sum("s_line", [s_mine, *s_got], 1, [])[0])
    s_got = over_line([s_piece] * 3)
    p_mine, *p_rest = plane_sum([p_mine, *p_got], [])
    p_got = over_line(p_rest)
    s_share = join("s_join", [s_piece, *s_got], [p_mine])
    s_got = [s_share, *over_plane([s_share] * 3)]
    p_piece, small = line_sum([p_mine, *p_got], [s_share])
    p_piece, small = beyond(p_piece), beyond(small)
    p_got = over_line([p_piece] * 3)
    small_other = swapped(small, 1)
    p_share = join("p_join", [p_piece, *p_got], [])
    p_got = over_plane([p_share] * 3)
    s_half = join("s_half", s_got, [p_share])
    grad_skip = assemble([swapped(s_half, 1)], 0, assemble([s_half], 2))
    back_near, back_far = swapped(after(back_near, p_share), 1), far_swapped(after(back_far, p_share))
    feats_total = pl.pallas_call(
        feats_kernel,
        in_specs=[vmem] * 5,
        out_specs=vmem,
        out_shape=shape_of((rows, depth), F32),
        compiler_params=params(8),
        cost_estimate=cost(0.1),
        name="features",
    )(own_send, own_keep, dskip, w_proj, w_skip)
    grad_src, grad_dst, grad_bias = pl.pallas_call(
        vectors_kernel,
        out_shape=[
            jax.ShapeDtypeStruct((heads, width), F32),
            jax.ShapeDtypeStruct((heads, width), F32),
            jax.ShapeDtypeStruct((1, concat), F32),
        ],
        compiler_params=params(1),
        cost_estimate=cost(0.1),
        name="vectors",
    )(small, small_other)
    p_got = [p_share, *(after(share, grad_skip, grad_src, back_near, back_far, feats_total) for share in p_got)]
    p_other = [swapped(share, 1) for share in p_got]
    grad_proj = assemble(p_other, 0, assemble(p_got, 2))

    grad_feats = pl.pallas_call(
        feats_halo_kernel,
        in_specs=[vmem] * 5,
        out_specs=vmem,
        scratch_shapes=[pltpu.VMEM((8, 2 * LANES), jnp.int32)],
        out_shape=jax.ShapeDtypeStruct((node_rows, depth), BF16),
        compiler_params=params(8),
        cost_estimate=cost(0.1),
        name="features_halo",
    )(feats_total, back_near, back_far, send_index, w_proj)

    return (
        output,
        grad_feats,
        grad_proj,
        grad_skip,
        grad_src,
        grad_dst,
        grad_bias.reshape(concat),
        gain_grad.reshape(concat),
        shift_grad.reshape(concat),
    )


def solution(mesh):
    rows = P(AXES, None)
    in_specs = (rows,) + (P(),) * 7 + (rows, rows, rows, P(AXES), P(AXES, None, None))
    out_specs = (rows, rows) + (P(),) * 7
    return jax.shard_map(per_device, mesh=mesh, in_specs=in_specs, out_specs=out_specs, check_vma=False)
```

```python
import functools

import jax
import jax.numpy as jnp
from jax import lax
from jax.experimental import pallas as pl
from jax.experimental.pallas import tpu as pltpu
from jax.sharding import PartitionSpec as P

AXES = ("dom", "sub")
F32 = jnp.float32
BF16 = jnp.bfloat16
NEG = -1e30
LN2 = 0.6931471805599453
STEP = 64
SHARDS = 16
CHUNK = 32
LANES = 128
MIB = 1024 * 1024


def params(mib=24):
    return pltpu.CompilerParams(vmem_limit_bytes=mib * MIB)


def cost(us):
    return pl.CostEstimate(flops=int(us * 1.1e9), bytes_accessed=int(us * 1e6), transcendentals=0)


def mm(a, b, contract):
    return lax.dot_general(a, b, ((contract[:1], contract[1:]), ((), ())), preferred_element_type=F32)


def pad_rows(value, rows):
    extra = rows - value.shape[0]
    if extra == 0:
        return value
    return jnp.concatenate([value, jnp.zeros((extra,) + value.shape[1:], value.dtype)], axis=0)


def three_parts(value):
    high = value.astype(BF16)
    rest = value - high.astype(F32)
    middle = rest.astype(BF16)
    low = (rest - middle.astype(F32)).astype(BF16)
    return high, middle, low


def two_parts(value):
    high = value.astype(BF16).astype(F32)
    return jnp.concatenate([high, value - high], axis=0).astype(BF16)


def whole_of(parts):
    parts = parts.astype(F32)
    return parts[:8] + parts[8:]


def repeat_lanes(value, columns):
    return jnp.concatenate([value] * (columns // value.shape[1]), axis=1)


def fold_rows(value):
    return value.reshape(value.shape[0] // 8, 8, value.shape[1])


def real_rows(mask_ref, rows, columns):
    count = jnp.sum(mask_ref[...].astype(F32), axis=1, keepdims=True)
    real = lax.broadcasted_iota(jnp.int32, (rows, columns), 0).astype(F32) < count
    return count, real


def one_hot(rows, index_ref, scratch, odd):
    halo = index_ref.shape[2]
    down, up = index_ref[0, 0:1, :], index_ref[0, 1:2, :]
    scratch[...] = jnp.full(scratch.shape, -1, jnp.int32)
    scratch[0:1, 0:halo] = jnp.where(odd, down, up)
    scratch[0:1, LANES : LANES + halo] = jnp.where(odd, up, down)
    wanted = scratch[0:1, :]
    return (lax.broadcasted_iota(jnp.int32, (rows, 2 * LANES), 0) == wanted).astype(BF16)


def own_index():
    return lax.axis_index(AXES[0]) * lax.axis_size(AXES[1]) + lax.axis_index(AXES[1])


def is_odd():
    return lax.axis_index(AXES[1]) % 2 == 1


def own_place():
    me = own_index()
    return (me // 2 % 4) * 4 + (me // 8 % 2) * 2 + me // 16 % 2


def head_at(step):
    core = lax.axis_index(AXES[1]) % 2
    return (2 - 2 * core if step < 2 else 2 * core) + step % 2


def halo_rows_kernel(feats_ref, index_ref, near_ref, far_ref, scratch):
    picked = one_hot(feats_ref.shape[0], index_ref, scratch, is_odd())
    rows = mm(picked, feats_ref[...], (0, 0)).astype(BF16)
    near_ref[...] = rows[: near_ref.shape[0]]
    far_ref[...] = rows[LANES : LANES + far_ref.shape[0]]


def project_kernel(
    feats_ref, proj_ref, skip_w_ref, neighbours_ref, mask_ref, zq_ref, skip_ref, count_ref, flipped_ref, padded,
    *, halo,
):
    node_rows = feats_ref.shape[0]
    columns, rows = count_ref.shape

    @pl.when(pl.program_id(0) == 0)
    def _():
        feats = pad_rows(feats_ref[...].astype(F32), rows).astype(BF16)
        padded[...] = feats
        flipped_ref[...] = feats.T

    zq_ref[...] = mm(padded[...], proj_ref[...], (1, 0)).astype(BF16)
    skip_ref[...] = mm(padded[...], skip_w_ref[...], (1, 0))

    names = neighbours_ref[...]
    names = names + jnp.where(names >= node_rows, rows - node_rows, 0)
    names = names + jnp.where(names >= rows + halo, STEP - halo, 0)
    names = jnp.where(mask_ref[...] > 0, names, -1)
    names = jnp.concatenate([names, jnp.full((names.shape[0], rows - node_rows), -1, jnp.int32)], axis=1)
    own = lax.broadcasted_iota(jnp.int32, (8, rows), 1)
    share = columns // 4

    def chunk(index, carry):
        start = pl.multiple_of(pl.program_id(0) * share + index * 8, 8)
        source = lax.broadcasted_iota(jnp.int32, (8, rows), 0) + start
        total = (source == own).astype(F32)
        for slot in range(names.shape[0]):
            total += jnp.where(source == names[slot : slot + 1, :], 1.0, 0.0)
        count_ref[pl.ds(start, 8), :] = jnp.where(total > 0, jnp.log(jnp.maximum(total, 1.0)) * (1.0 / LN2), NEG)
        return carry

    lax.fori_loop(0, share // 8, chunk, 0, unroll=2)


def attend_kernel(
    zq_ref, near_ref, far_ref, proj_ref, skip_ref, count_ref, src_ref, dst_ref, bias_ref, cot_ref, mask_ref,
    ext_ref, weight_ref, source_ref, target_ref, scale_ref, pre_ref, stats_ref, flipped_ref, halo_scr, score_scr,
):
    columns, rows = count_ref.shape
    half = (columns - rows) // 2
    head = pl.program_id(0)

    @pl.when(head == 0)
    def _():
        halo_scr[...] = jnp.zeros_like(halo_scr)
        near_at = jnp.where(is_odd(), 0, half)
        halo_scr[pl.ds(pl.multiple_of(near_at, 16), near_ref.shape[0]), :] = near_ref[...]
        halo_scr[pl.ds(pl.multiple_of(half - near_at, 16), far_ref.shape[0]), :] = far_ref[...]
        flipped_ref[...] = halo_scr[...].T

    ext_ref[0:rows, :] = zq_ref[...]
    ext_ref[rows:columns, :] = mm(halo_scr[...], proj_ref[...], (1, 0)).astype(BF16)
    ext = ext_ref[...]
    width = ext.shape[1]
    parts = three_parts(src_ref[pl.ds(head, 1), :] * (1.0 / LN2))
    vectors = jnp.concatenate([jnp.broadcast_to(part, (LANES, width)) for part in parts], axis=0)
    source = mm(ext, vectors, (1, 1))
    source_ref[0] = source[:, :LANES] + source[:, LANES : 2 * LANES] + source[:, 2 * LANES :]
    parts = three_parts(dst_ref[pl.ds(head, 1), :] * (1.0 / LN2))
    vectors = jnp.concatenate([jnp.broadcast_to(part, (16, width)) for part in parts], axis=0)
    target = mm(vectors, zq_ref[...], (1, 1))
    target = target[0:8] + target[16:24] + target[32:40]
    target_ref[0] = target
    target = target[0:1]

    def score(index, highest):
        where = pl.ds(pl.multiple_of(index * CHUNK, CHUNK), CHUNK)
        value = repeat_lanes(source_ref[0, where, :], rows) + target
        small = jnp.exp2(-jnp.abs(value))
        result = jnp.maximum(value, 0.2 * value) + (0.8 / LN2) * jnp.log(1.0 + small) + count_ref[where, :]
        score_scr[where, :] = result
        return jnp.maximum(highest, jnp.max(fold_rows(result), axis=0))

    highest = lax.fori_loop(0, columns // CHUNK, score, jnp.full((8, rows), NEG, F32), unroll=2)
    highest = jnp.max(highest, axis=0, keepdims=True)

    def weigh(index, carry):
        where = pl.ds(pl.multiple_of(index * CHUNK, CHUNK), CHUNK)
        weight_ref[0, where, :] = jnp.exp2(score_scr[where, :] - highest).astype(BF16)
        return carry

    lax.fori_loop(0, columns // CHUNK, weigh, 0, unroll=2)
    weights = weight_ref[0]
    wide = jnp.concatenate([ext, jnp.ones((columns, LANES), BF16)], axis=1)
    summed = mm(weights, wide, (0, 0))
    scale = 1.0 / summed[:, width:]
    scale_ref[0] = scale
    pre = summed[:, :width] * repeat_lanes(scale, width) + skip_ref[...] + bias_ref[...]
    pre_ref[...] = pre
    act = jnp.where(pre > 0, pre, jnp.exp(jnp.minimum(pre, 0.0)) - 1.0)
    nodes, real = real_rows(mask_ref, rows, width)
    cot = jnp.where(real, pad_rows(cot_ref[...].astype(F32), rows), 0.0)
    mean = jnp.sum(jnp.where(real, act, 0.0), axis=0, keepdims=True) / nodes
    centred = jnp.where(real, act - mean, 0.0)
    stats_ref[...] = jnp.zeros_like(stats_ref)
    stats_ref[0:1, :] = jnp.broadcast_to(nodes, mean.shape)
    stats_ref[1:2, :] = mean
    stats_ref[2:3, :] = jnp.sum(centred * centred, axis=0, keepdims=True)
    stats_ref[3:4, :] = jnp.sum(cot, axis=0, keepdims=True)
    stats_ref[4:5, :] = jnp.sum(cot * centred, axis=0, keepdims=True)


def merged(first, second):
    nodes = first[0:1] + second[0:1]
    gap = second[1:2] - first[1:2]
    part = second[0:1] / nodes
    mean = first[1:2] + gap * part
    spread = first[2:3] + second[2:3] + gap * gap * first[0:1] * part
    shift = first[3:4] + second[3:4]
    gain = first[4:5] + second[4:5] - (mean - first[1:2]) * first[3:4] - (mean - second[1:2]) * second[3:4]
    return nodes, mean, spread, shift, gain


def in_order(mine, other, bit):
    mine_first = bit == 0
    return jnp.where(mine_first, mine, other), jnp.where(mine_first, other, mine)


def merge_kernel(mine_ref, other_ref, out_ref, *, which):
    bit = own_index() // 2**which % 2
    lines = merged(*in_order(mine_ref[...], other_ref[...], bit))
    out_ref[...] = jnp.zeros_like(out_ref)
    for line, value in enumerate(lines):
        out_ref[line : line + 1, :] = value


def place_blocks(out_ref, value, me):
    size = value.shape[0] // SHARDS
    for block in range(SHARDS):
        at = pl.multiple_of((block ^ me) * size, size)
        out_ref[pl.ds(at, size), :] = value[block * size : (block + 1) * size, :]


def core_shares_kernel(keep_ref, other_ref, *outs):
    size = keep_ref.shape[1] // 4 - 4
    for head in range(2):
        vectors = two_parts(whole_of(keep_ref[head, 4 * size :, :]) + whole_of(other_ref[head, 4 * size :, :]))
        for index, out_ref in enumerate(outs):
            rows = slice(index * size, (index + 1) * size)
            out_ref[head, :size, :] = (keep_ref[head, rows, :].astype(F32) + other_ref[head, rows, :].astype(F32)).astype(BF16)
            out_ref[head, size:, :] = vectors


def sum_of_four(refs, head, rows):
    first, second, third, fourth = (ref[head, rows, :].astype(F32) for ref in refs)
    return (first + second + third + fourth).astype(BF16)


def ordered_sum(refs, start, me, scratch):
    for index, ref in enumerate(refs):
        for head in range(2):
            scratch[index ^ me, head] = whole_of(ref[head, start:, :])
    return [scratch[0, head] + scratch[1, head] + scratch[2, head] + scratch[3, head] for head in range(2)]


def plane_sum_kernel(*refs, deps):
    ins, outs, scratch = refs[:4], refs[4 + deps : -1], refs[-1]
    size = outs[0].shape[1] - 16
    vectors = ordered_sum(ins, 4 * size, own_place() // 4, scratch)
    for head in range(2):
        for index, out_ref in enumerate(outs):
            out_ref[head, :size, :] = sum_of_four(ins, head, slice(index * size, (index + 1) * size))
            out_ref[head, size:, :] = two_parts(vectors[head])


def line_sum_kernel(*refs, deps):
    ins, (out_ref, small_ref, scratch) = refs[:4], refs[4 + deps :]
    size = out_ref.shape[1]
    vectors = ordered_sum(ins, size, own_place() % 4, scratch)
    for head in range(2):
        out_ref[head] = sum_of_four(ins, head, slice(0, size))
        small_ref[head] = vectors[head]


def vectors_kernel(mine_ref, other_ref, src_ref, dst_ref, bias_ref):
    odd = is_odd()
    width = src_ref.shape[1]
    for head in range(4):
        mine, other = mine_ref[head % 2], other_ref[head % 2]
        value = jnp.where(odd == (head >= 2), mine, other)
        src_ref[head : head + 1, :] = value[0:1]
        dst_ref[head : head + 1, :] = value[1:2]
        bias_ref[:, head * width : (head + 1) * width] = value[2:3]


def share_sum_kernel(*refs, deps):
    ins, outs = refs[:4], refs[4 + deps :]
    size = outs[0].shape[1]
    for head in range(2):
        for index, out_ref in enumerate(outs):
            out_ref[head] = sum_of_four(ins, head, slice(index * size, (index + 1) * size))


def pair_join_kernel(mine_ref, other_ref, *rest):
    size = mine_ref.shape[1]
    rest[-1][:, :size, :] = mine_ref[...]
    rest[-1][:, size:, :] = other_ref[...]


def heads_join_kernel(mine_ref, other_ref, *outs):
    size = mine_ref.shape[1]
    for head, out_ref in enumerate(outs):
        out_ref[:size, :] = mine_ref[head]
        out_ref[size:, :] = other_ref[head]


def half_join_kernel(*refs):
    for share, near, out_ref in zip(refs[:2], refs[2:4], refs[4:]):
        size = share.shape[0]
        out_ref[:size, :] = share[...]
        out_ref[size:, :] = near[...]


def plane_join_kernel(half_one, half_two, far_one, far_two, low_ref, high_ref):
    size = half_one.shape[0] // 2
    low_ref[0] = half_one[...]
    high_ref[0] = far_one[...]
    for part, out_ref in ((slice(0, size), low_ref), (slice(size, 2 * size), high_ref)):
        out_ref[1, :size, :] = half_two[part, :]
        out_ref[1, size:, :] = far_two[part, :]


def two_sum_kernel(mine_ref, other_ref, *outs, deps=0):
    outs = outs[deps:]
    size = outs[0].shape[1]
    for piece, out_ref in enumerate(outs):
        rows = slice(piece * size, (piece + 1) * size)
        out_ref[...] = (mine_ref[:, rows, :].astype(F32) + other_ref[:, rows, :].astype(F32)).astype(BF16)


def norm_kernel(
    pre_ref, stats_ref, other_ref, cot_ref, mask_ref, gain_ref, shift_ref, flipped_ref,
    out_ref, dskip_ref, send_ref, keep_ref, small_ref, gain_grad_ref, shift_grad_ref, out_scr, done, *, last_bit,
):
    rows = pre_ref.shape[0]
    node_rows, width = out_scr.shape[1:]
    real = real_rows(mask_ref, rows, width)[1]
    copies = []
    for step in range(4):
        head = head_at(step)
        lanes = pl.ds(pl.multiple_of(head * width, width), width)
        pre = pre_ref[:, lanes]
        steep = jnp.exp(jnp.minimum(pre, 0.0))
        act = jnp.where(pre > 0, pre, steep - 1.0)
        first, second = in_order(stats_ref[:, lanes], other_ref[:, lanes], own_index() // 2**last_bit % 2)
        nodes, mean, spread, total, cross = merged(first, second)
        inverse = lax.rsqrt(spread / nodes + 1e-05)
        normed = (act - mean) * inverse
        gain = gain_ref[:, lanes]
        out_scr[step] = jnp.where(real, gain * normed + shift_ref[:, lanes], 0.0)[:node_rows].astype(BF16)
        copies.append(pltpu.make_async_copy(out_scr.at[step], out_ref.at[:, lanes], done.at[step]))
        copies[-1].start()
        gain_grad_ref[:, lanes] = cross * inverse
        shift_grad_ref[:, lanes] = total
        grad = pad_rows(cot_ref[:, lanes].astype(F32), rows) - total / nodes - normed * (cross * inverse / nodes)
        grad_pre = jnp.where(real, grad * (inverse * gain) * steep, 0.0)
        small_ref[head] = jnp.broadcast_to(jnp.sum(grad_pre, axis=0, keepdims=True), small_ref.shape[1:])
        dskip = grad_pre.astype(BF16)
        dskip_ref[:, lanes] = dskip
        grads = mm(flipped_ref[...], dskip, (1, 0)).astype(BF16)
        place_blocks((send_ref if step < 2 else keep_ref).at[step % 2], grads, own_place())
    for copy in copies:
        copy.wait()


def back_kernel(
    weight_ref, source_ref, target_ref, scale_ref, ext_ref, dskip_ref, src_ref, dst_ref, flipped_ref, halo_ref,
    small_in, *rest, part,
):
    grad_ref, own_ref, near_ref, far_ref, dal_scr, sum_scr = rest[-6:]
    columns, rows = weight_ref.shape[1:]
    half = (columns - rows) // 2
    width = src_ref.shape[1]
    depth = flipped_ref.shape[0]
    count = near_ref.shape[0]
    if part:
        near_ref[:, : 2 * width] = rest[0][...]
        far_ref[:, : 2 * width] = rest[1][...]
    for step in range(2):
        head = head_at(part + step)
        lanes = pl.ds(pl.multiple_of(head * width, width), width)
        target = target_ref[head, 0:1, :]
        dskip = dskip_ref[:, lanes]
        dal_scr[...] = mm(ext_ref[:, lanes], dskip, (1, 1))

        def average(index, carry):
            total, mean = carry
            where = pl.ds(pl.multiple_of(index * CHUNK, CHUNK), CHUNK)
            weight = weight_ref[head, where, :].astype(F32)
            return total + jnp.sum(fold_rows(weight), axis=0), mean + jnp.sum(fold_rows(weight * dal_scr[where, :]), axis=0)

        nothing = jnp.zeros((8, rows), F32)
        total, mean = lax.fori_loop(0, columns // CHUNK, average, (nothing, nothing), unroll=2)
        scale = 1.0 / jnp.sum(total, axis=0, keepdims=True)
        mean = jnp.sum(mean, axis=0, keepdims=True) * scale

        def slopes(index, by_target):
            where = pl.ds(pl.multiple_of(index * CHUNK, CHUNK), CHUNK)
            value = repeat_lanes(source_ref[head, where, :], rows) + target
            slope = (0.6 + 0.4 * jnp.tanh(value * (0.5 * LN2))) * scale
            du = weight_ref[head, where, :].astype(F32) * slope * (dal_scr[where, :] - mean)
            sum_scr[where, :] = sum(du[:, at : at + LANES] for at in range(0, rows, LANES))
            return by_target + jnp.sum(fold_rows(du), axis=0)

        by_target = lax.fori_loop(0, columns // CHUNK, slopes, nothing, unroll=2)
        by_target = jnp.sum(by_target, axis=0, keepdims=True)
        by_source = jnp.sum(sum_scr[...], axis=1, keepdims=True)
        ext = ext_ref[:, lanes]
        scaled = (dskip.astype(F32) * repeat_lanes(scale_ref[head], width)).astype(BF16)
        dz = mm(weight_ref[head], scaled, (1, 0)) + by_source * src_ref[pl.ds(head, 1), :]
        high, middle, low = three_parts(by_target)
        row = lax.broadcasted_iota(jnp.int32, (16, rows), 0)
        lines = jnp.where(row == 1, middle.astype(F32), jnp.where(row == 3, low.astype(F32), high.astype(F32)))
        lines = jnp.where(row < 4, lines, 0.0).astype(BF16)
        dst_high, dst_middle, _ = three_parts(dst_ref[pl.ds(head, 1), :])
        row = lax.broadcasted_iota(jnp.int32, (16, width), 0)
        vectors = jnp.where(row == 2, dst_middle.astype(F32), dst_high.astype(F32)).astype(BF16)
        dz_own = dz[:rows] + mm(lines, vectors, (0, 0))
        mine = slice(step * width, (step + 1) * width)
        dz_own = dz_own.astype(BF16)
        own_ref[:, mine] = dz_own
        dz_halo = dz[rows:].astype(BF16)
        below, above = dz[rows : rows + count], dz[rows + half : rows + half + count]
        odd = is_odd()
        at = part * width + step * width
        near_ref[:, at : at + width] = jnp.where(odd, below, above).astype(BF16)
        far_ref[:, at : at + width] = jnp.where(odd, above, below).astype(BF16)
        sums = mm(lines, ext[:rows], (1, 0))
        source_sum = jnp.sum(by_source * ext.astype(F32), axis=0, keepdims=True)
        row = lax.broadcasted_iota(jnp.int32, (8, width), 0)
        lines = jnp.where(row == 0, source_sum, jnp.where(row == 1, sums[0:1] + sums[1:2] + sums[3:4], small_in[head]))
        grad_ref[step, depth:, :] = two_parts(jnp.where(row < 3, lines, 0.0))
        grads = mm(flipped_ref[...], dz_own, (1, 0)) + mm(halo_ref[...], dz_halo, (1, 0))
        place_blocks(grad_ref.at[step], grads.astype(BF16), own_place())


def feats_kernel(own_one, own_two, dskip_ref, proj_ref, skip_ref, total_ref):
    width = own_one.shape[1] // 2
    total = mm(dskip_ref[...], skip_ref[...], (1, 1))
    for step in range(4):
        lanes = pl.ds(pl.multiple_of(head_at(step) * width, width), width)
        own = (own_one if step < 2 else own_two)[:, step % 2 * width : (step % 2 + 1) * width]
        total += mm(own, proj_ref[:, lanes], (1, 1))
    total_ref[...] = total


def feats_halo_kernel(total_ref, near_ref, far_ref, index_ref, proj_ref, out_ref, scratch):
    rows = total_ref.shape[0]
    count = near_ref.shape[0]
    width = near_ref.shape[1] // 4
    picks = one_hot(rows, index_ref, scratch, is_odd())
    picks = jnp.concatenate([picks[:, :count], picks[:, LANES : LANES + count]], axis=1)
    sent = jnp.concatenate([near_ref[...], far_ref[...]], axis=0)
    product = jnp.zeros((2 * count, proj_ref.shape[0]), F32)
    for step in range(4):
        lanes = pl.ds(pl.multiple_of(head_at(step) * width, width), width)
        other = (step + 2) % 4 * width
        product += mm(sent[:, other : other + width], proj_ref[:, lanes], (1, 1))
    high, middle, _ = three_parts(product)
    total = total_ref[...] + mm(picks, high, (1, 0)) + mm(picks, middle, (1, 0))
    out_ref[...] = total[: out_ref.shape[0]].astype(BF16)


def assemble_kernel(*refs, first, pieces):
    out_ref, scratch, done = refs[-3:]
    size, width = scratch.shape[2:]
    me = own_place()
    each = SHARDS // pieces
    copies = []
    for step in range(2):
        lanes = pl.ds(pl.multiple_of(head_at(first + step) * width, width), width)
        for block in range(SHARDS):
            at = pl.multiple_of((block ^ me) * size, size)
            rows = slice(block % each * size, (block % each + 1) * size)
            scratch[step, block] = refs[block // each][step, rows, :].astype(F32)
            copies.append(pltpu.make_async_copy(scratch.at[step, block], out_ref.at[pl.ds(at, size), lanes], done.at[step, block]))
            copies[-1].start()
    for copy in copies:
        copy.wait()


def per_device(
    feats, w_proj, w_skip, attn_src, attn_dst, bias, gain, shift, cotangent, neighbours, edge_mask, node_mask, send_index,
):
    node_rows, depth = feats.shape
    heads, width = attn_src.shape
    concat = heads * width
    slots = neighbours.shape[1]
    halo = send_index.shape[2]
    devices = lax.axis_size(AXES)
    bits = devices.bit_length() - 1
    rows = -(-node_rows // LANES) * LANES
    columns = rows + 2 * STEP
    halo_pad = -(-halo // 16) * 16

    def far_swapped(value):
        pairs = [(low, low + 1) for low in range(1, devices - 1, 2)]
        return lax.ppermute(value, AXES, pairs + [(high, low) for low, high in pairs])

    def swapped(value, distance):
        return lax.ppermute(value, AXES, [(source, source ^ distance) for source in range(devices)])

    mask = node_mask.reshape(1, node_rows)
    bias2, gain2, shift2 = bias[None], gain[None], shift[None]

    in_hbm = lambda value: pltpu.with_memory_space_constraint(value, pltpu.HBM)
    near, far = pl.pallas_call(
        halo_rows_kernel,
        out_shape=[jax.ShapeDtypeStruct((halo_pad, depth), BF16)] * 2,
        scratch_shapes=[pltpu.VMEM((8, 2 * LANES), jnp.int32)],
        compiler_params=params(8),
        name="halo_rows",
    )(in_hbm(feats), in_hbm(send_index))
    near, far = swapped(near, 1), far_swapped(far)

    def spec(shape, index):
        return pl.BlockSpec(shape, index)

    def whole(*shape):
        return pl.BlockSpec(shape, lambda *_: (0,) * len(shape))

    by_head = lambda n: pl.BlockSpec((n, width), lambda h, *_: (0, h))
    stacked = lambda *shape: pl.BlockSpec((1, *shape), lambda h, *_: (h, 0, 0))
    shape_of = jax.ShapeDtypeStruct
    zq, skip, count, flipped = pl.pallas_call(
        functools.partial(project_kernel, halo=halo),
        grid=(heads,),
        in_specs=[
            whole(node_rows, depth), by_head(depth), by_head(depth), whole(slots, node_rows), whole(slots, node_rows),
        ],
        out_specs=[by_head(rows), by_head(rows), whole(columns, rows), whole(depth, rows)],
        scratch_shapes=[pltpu.VMEM((rows, depth), BF16)],
        out_shape=[
            shape_of((rows, concat), BF16),
            shape_of((rows, concat), F32),
            shape_of((columns, rows), F32),
            shape_of((depth, rows), BF16),
        ],
        compiler_params=params(),
        cost_estimate=cost(5),
        name="project",
    )(in_hbm(feats), in_hbm(w_proj), in_hbm(w_skip), in_hbm(neighbours.T), in_hbm(edge_mask.T))

    ext, weight, source, target, scale, pre, stats, halo_flipped = pl.pallas_call(
        attend_kernel,
        grid=(heads,),
        in_specs=[
            by_head(rows), whole(halo_pad, depth), whole(halo_pad, depth), by_head(depth), by_head(rows),
            whole(columns, rows), whole(heads, width), whole(heads, width), by_head(1), by_head(node_rows),
            whole(1, node_rows),
        ],
        out_specs=[
            by_head(columns), stacked(columns, rows), stacked(columns, LANES), stacked(8, rows), stacked(rows, LANES),
            by_head(rows), by_head(8), whole(depth, columns - rows),
        ],
        out_shape=[
            shape_of((columns, concat), BF16),
            shape_of((heads, columns, rows), BF16),
            shape_of((heads, columns, LANES), F32),
            shape_of((heads, 8, rows), F32),
            shape_of((heads, rows, LANES), F32),
            shape_of((rows, concat), F32),
            shape_of((8, concat), F32),
            shape_of((depth, columns - rows), BF16),
        ],
        scratch_shapes=[pltpu.VMEM((columns - rows, depth), BF16), pltpu.VMEM((columns, rows), F32)],
        compiler_params=params(),
        cost_estimate=cost(8),
        name="attend",
    )(zq, near, far, in_hbm(w_proj), skip, count, attn_src, attn_dst, bias2, in_hbm(cotangent), mask)

    for which in range(bits - 1):
        stats = pl.pallas_call(
            functools.partial(merge_kernel, which=which),
            in_specs=[pl.BlockSpec(memory_space=pltpu.VMEM)] * 2,
            out_shape=shape_of(stats.shape, F32),
            compiler_params=params(1),
            name="merge",
        )(stats, swapped(stats, 1 << which))
    other = swapped(stats, 1 << (bits - 1))

    vmem = pl.BlockSpec(memory_space=pltpu.VMEM)
    anywhere = pl.BlockSpec(memory_space=pl.ANY)
    half_grad = shape_of((2, depth, width), BF16)
    output, dskip, skip_send, skip_keep, small, gain_grad, shift_grad = pl.pallas_call(
        functools.partial(norm_kernel, last_bit=bits - 1),
        in_specs=[vmem] * 8,
        out_specs=[anywhere] + [vmem] * 6,
        out_shape=[
            pltpu.HBM((node_rows, concat), BF16),
            shape_of((rows, concat), BF16),
            half_grad,
            half_grad,
            shape_of((heads, 8, width), F32),
            jax.ShapeDtypeStruct((1, concat), F32),
            jax.ShapeDtypeStruct((1, concat), F32),
        ],
        scratch_shapes=[pltpu.VMEM((heads, node_rows, width), BF16), pltpu.SemaphoreType.DMA((heads,))],
        compiler_params=params(16),
        cost_estimate=cost(0.1),
        name="norm",
    )(pre, stats, other, cotangent, mask, gain2, shift2, flipped)

    def backward(part, arrays=(), deps=()):
        return pl.pallas_call(
            functools.partial(back_kernel, part=part),
            in_specs=[vmem] * (11 + len(arrays)) + [anywhere] * len(deps),
            out_shape=[
                shape_of((2, depth + 16, width), BF16),
                shape_of((rows, 2 * width), BF16),
                shape_of((halo_pad, (2 + part) * width), BF16),
                shape_of((halo_pad, (2 + part) * width), BF16),
            ],
            scratch_shapes=[pltpu.VMEM((columns, rows), F32), pltpu.VMEM((columns, LANES), F32)],
            compiler_params=params(8),
            cost_estimate=cost(0.1),
            name="back",
        )(weight, source, target, scale, ext, dskip, attn_src, attn_dst, flipped, halo_flipped, small, *arrays, *deps)

    quarter = (2, depth // 4, width)
    piece = (2, depth // SHARDS, width)
    def step_call(kernel, name, shapes, arrays, deps=()):
        return pl.pallas_call(
            kernel,
            in_specs=[vmem] * len(arrays) + [anywhere] * len(deps),
            out_shape=[shape_of(shape, BF16) for shape in shapes],
            compiler_params=params(1),
            cost_estimate=cost(0.1),
            name=name,
        )(*arrays, *deps)

    def over_plane(shares):
        return [swapped(share, distance << 1) for distance, share in zip((1, 2, 3), shares)]

    def over_line(shares):
        return [swapped(share, distance) for distance, share in zip((16, 8, 24), shares)]

    def ordered_call(kernel, name, shapes, arrays, deps):
        return pl.pallas_call(
            functools.partial(kernel, deps=len(deps)),
            in_specs=[vmem] * len(arrays) + [anywhere] * len(deps),
            out_shape=shapes,
            scratch_shapes=[pltpu.VMEM((4, 2, 8, width), F32)],
            compiler_params=params(1),
            cost_estimate=cost(0.1),
            name=name,
        )(*arrays, *deps)

    def plane_sum(arrays, deps):
        shapes = [shape_of((2, depth // SHARDS + 16, width), BF16)] * 4
        return ordered_call(plane_sum_kernel, "p_plane", shapes, arrays, deps)

    def line_sum(arrays, deps):
        shapes = [shape_of(piece, BF16), shape_of((2, 8, width), F32)]
        return ordered_call(line_sum_kernel, "p_line", shapes, arrays, deps)

    def two_sum(name, arrays, count, deps=()):
        shapes = [(2, arrays[0].shape[1] // count, width)] * count
        return step_call(functools.partial(two_sum_kernel, deps=len(deps)), name, shapes, arrays, deps)

    def pair_join(name, mine, other, deps=()):
        return step_call(pair_join_kernel, name, [(2, 2 * mine.shape[1], width)], [mine, other], deps)[0]

    def share_sum(name, arrays, count, deps):
        shapes = [(2, arrays[0].shape[1] // count, width)] * count
        return step_call(functools.partial(share_sum_kernel, deps=len(deps)), name, shapes, arrays, deps)

    def assemble(pieces, first, *out):
        return pl.pallas_call(
            functools.partial(assemble_kernel, first=first, pieces=len(pieces)),
            in_specs=[vmem] * len(pieces) + [anywhere] * len(out),
            out_specs=anywhere,
            out_shape=pltpu.HBM((depth, concat), F32),
            scratch_shapes=[pltpu.VMEM((2, SHARDS, depth // SHARDS, width), F32), pltpu.SemaphoreType.DMA((2, SHARDS))],
            input_output_aliases={len(pieces): 0} if out else {},
            compiler_params=params(8),
            cost_estimate=cost(0.1),
            name="assemble",
        )(*pieces, *out)

    def beyond(value):
        for which in range(5, bits):
            value = value + swapped(value, 1 << which)
        return value

    def after(value, *others):
        return lax.optimization_barrier((value, *others))[0]

    skip_other = swapped(skip_send, 1)
    proj_send, own_send, near_send, far_send = backward(0)
    proj_other = swapped(proj_send, 1)
    s_mine, *s_rest = step_call(
        functools.partial(two_sum_kernel, deps=1), "s_core", [quarter] * 4, [skip_keep, skip_other], [proj_send]
    )
    s_got = over_plane(s_rest)
    proj_keep, own_keep, back_near, back_far = backward(2, [near_send, far_send], [s_mine])
    p_mine, *p_rest = step_call(core_shares_kernel, "p_core", [(2, depth // 4 + 16, width)] * 4, [proj_keep, proj_other])
    p_got = over_plane(p_rest)
    s_mine, s_rest = share_sum("s_plane", [s_mine, *s_got], 2, [p_mine])
    s_mine, s_rest = two_sum("s_line", [s_mine, swapped(s_rest, 8)], 2)
    p_mine, *p_rest = plane_sum([p_mine, *p_got], [])
    p_got = over_line(p_rest)
    s_piece = beyond(two_sum("s_line", [s_mine, swapped(s_rest, 16)], 1, [p_mine])[0])
    s_piece = pair_join("s_join", s_piece, swapped(s_piece, 16))
    s_share = step_call(heads_join_kernel, "s_share", [(depth // 4, width)] * 2, [s_piece, swapped(s_piece, 8)])
    s_near = (swapped(s_share[0], 2), swapped(s_share[1], 4))
    s_sent = step_call(half_join_kernel, "s_near", [(depth // 2, width)] * 2, [*s_share, *s_near])
    s_far = (swapped(s_sent[0], 4), swapped(s_sent[1], 2))
    back_near, back_far = swapped(after(back_near, p_mine), 1), far_swapped(after(back_far, p_mine))
    p_piece, small = line_sum([p_mine, *p_got], [back_near, back_far])
    p_piece, small = beyond(p_piece), beyond(small)
    small_other = swapped(small, 1)
    p_piece = pair_join("p_join", p_piece, swapped(p_piece, 16))
    p_share = pair_join("p_join", p_piece, swapped(p_piece, 8), [small_other])
    p_got = over_plane([p_share] * 3)
    feats_total = pl.pallas_call(
        feats_kernel,
        in_specs=[vmem] * 5,
        out_specs=vmem,
        out_shape=shape_of((rows, depth), F32),
        compiler_params=params(8),
        cost_estimate=cost(0.1),
        name="features",
    )(own_send, own_keep, dskip, w_proj, w_skip)
    grad_src, grad_dst, grad_bias = pl.pallas_call(
        vectors_kernel,
        out_shape=[
            jax.ShapeDtypeStruct((heads, width), F32),
            jax.ShapeDtypeStruct((heads, width), F32),
            jax.ShapeDtypeStruct((1, concat), F32),
        ],
        compiler_params=params(1),
        cost_estimate=cost(0.1),
        name="vectors",
    )(small, small_other)
    p_got = [p_share, *(after(share, grad_src, back_near, back_far, feats_total) for share in p_got)]
    p_other = [swapped(share, 1) for share in p_got]
    s_halves = step_call(plane_join_kernel, "s_half", [(2, depth // 2, width)] * 2, [*s_sent, *s_far])
    s_other = [swapped(half, 1) for half in s_halves]
    grad_skip = assemble(s_other, 0, assemble(s_halves, 2))
    grad_proj = assemble(p_other, 0, assemble(p_got, 2))

    grad_feats = pl.pallas_call(
        feats_halo_kernel,
        in_specs=[vmem] * 5,
        out_specs=vmem,
        scratch_shapes=[pltpu.VMEM((8, 2 * LANES), jnp.int32)],
        out_shape=jax.ShapeDtypeStruct((node_rows, depth), BF16),
        compiler_params=params(8),
        cost_estimate=cost(0.1),
        name="features_halo",
    )(feats_total, back_near, back_far, send_index, w_proj)

    return (
        output,
        grad_feats,
        grad_proj,
        grad_skip,
        grad_src,
        grad_dst,
        grad_bias.reshape(concat),
        gain_grad.reshape(concat),
        shift_grad.reshape(concat),
    )


def solution(mesh):
    rows = P(AXES, None)
    in_specs = (rows,) + (P(),) * 7 + (rows, rows, rows, P(AXES), P(AXES, None, None))
    out_specs = (rows, rows) + (P(),) * 7
    return jax.shard_map(per_device, mesh=mesh, in_specs=in_specs, out_specs=out_specs, check_vma=False)
```

```python
import functools

import jax
import jax.numpy as jnp
from jax import lax
from jax.experimental import pallas as pl
from jax.experimental.pallas import tpu as pltpu
from jax.sharding import PartitionSpec as P

AXES = ("dom", "sub")
F32 = jnp.float32
BF16 = jnp.bfloat16
NEG = -1e30
LN2 = 0.6931471805599453
STEP = 64
SHARDS = 16
CHUNK = 32
LANES = 128
MIB = 1024 * 1024


def params(mib=24):
    return pltpu.CompilerParams(vmem_limit_bytes=mib * MIB)


def cost(us):
    return pl.CostEstimate(flops=int(us * 1.1e9), bytes_accessed=int(us * 1e6), transcendentals=0)


def mm(a, b, contract):
    return lax.dot_general(a, b, ((contract[:1], contract[1:]), ((), ())), preferred_element_type=F32)


def pad_rows(value, rows):
    extra = rows - value.shape[0]
    if extra == 0:
        return value
    return jnp.concatenate([value, jnp.zeros((extra,) + value.shape[1:], value.dtype)], axis=0)


def three_parts(value):
    high = value.astype(BF16)
    rest = value - high.astype(F32)
    middle = rest.astype(BF16)
    low = (rest - middle.astype(F32)).astype(BF16)
    return high, middle, low


def two_parts(value):
    high = value.astype(BF16).astype(F32)
    return jnp.concatenate([high, value - high], axis=0).astype(BF16)


def whole_of(parts):
    parts = parts.astype(F32)
    return parts[:8] + parts[8:]


def repeat_lanes(value, columns):
    return jnp.concatenate([value] * (columns // value.shape[1]), axis=1)


def fold_rows(value):
    return value.reshape(value.shape[0] // 8, 8, value.shape[1])


def real_rows(mask_ref, rows, columns):
    count = jnp.sum(mask_ref[...].astype(F32), axis=1, keepdims=True)
    real = lax.broadcasted_iota(jnp.int32, (rows, columns), 0).astype(F32) < count
    return count, real


def one_hot(rows, index_ref, scratch, odd):
    halo = index_ref.shape[2]
    down, up = index_ref[0, 0:1, :], index_ref[0, 1:2, :]
    scratch[...] = jnp.full(scratch.shape, -1, jnp.int32)
    scratch[0:1, 0:halo] = jnp.where(odd, down, up)
    scratch[0:1, LANES : LANES + halo] = jnp.where(odd, up, down)
    wanted = scratch[0:1, :]
    return (lax.broadcasted_iota(jnp.int32, (rows, 2 * LANES), 0) == wanted).astype(BF16)


def own_index():
    return lax.axis_index(AXES[0]) * lax.axis_size(AXES[1]) + lax.axis_index(AXES[1])


def is_odd():
    return lax.axis_index(AXES[1]) % 2 == 1


def own_place():
    me = own_index()
    return (me // 2 % 4) * 4 + (me // 8 % 2) * 2 + me // 16 % 2


def head_at(step):
    core = lax.axis_index(AXES[1]) % 2
    return (2 - 2 * core if step < 2 else 2 * core) + step % 2


def halo_rows_kernel(feats_ref, index_ref, near_ref, far_ref, scratch):
    picked = one_hot(feats_ref.shape[0], index_ref, scratch, is_odd())
    rows = mm(picked, feats_ref[...], (0, 0)).astype(BF16)
    near_ref[...] = rows[: near_ref.shape[0]]
    far_ref[...] = rows[LANES : LANES + far_ref.shape[0]]


def project_kernel(
    feats_ref, proj_ref, skip_w_ref, neighbours_ref, mask_ref, zq_ref, skip_ref, count_ref, flipped_ref, padded,
    *, halo,
):
    node_rows = feats_ref.shape[0]
    columns, rows = count_ref.shape

    @pl.when(pl.program_id(0) == 0)
    def _():
        feats = pad_rows(feats_ref[...].astype(F32), rows).astype(BF16)
        padded[...] = feats
        flipped_ref[...] = feats.T

    zq_ref[...] = mm(padded[...], proj_ref[...], (1, 0)).astype(BF16)
    skip_ref[...] = mm(padded[...], skip_w_ref[...], (1, 0))

    names = neighbours_ref[...]
    names = names + jnp.where(names >= node_rows, rows - node_rows, 0)
    names = names + jnp.where(names >= rows + halo, STEP - halo, 0)
    names = jnp.where(mask_ref[...] > 0, names, -1)
    names = jnp.concatenate([names, jnp.full((names.shape[0], rows - node_rows), -1, jnp.int32)], axis=1)
    own = lax.broadcasted_iota(jnp.int32, (8, rows), 1)
    share = columns // 4

    def chunk(index, carry):
        start = pl.multiple_of(pl.program_id(0) * share + index * 8, 8)
        source = lax.broadcasted_iota(jnp.int32, (8, rows), 0) + start
        total = (source == own).astype(F32)
        for slot in range(names.shape[0]):
            total += jnp.where(source == names[slot : slot + 1, :], 1.0, 0.0)
        count_ref[pl.ds(start, 8), :] = jnp.where(total > 0, jnp.log(jnp.maximum(total, 1.0)) * (1.0 / LN2), NEG)
        return carry

    lax.fori_loop(0, share // 8, chunk, 0, unroll=2)


def attend_kernel(
    zq_ref, near_ref, far_ref, proj_ref, skip_ref, count_ref, src_ref, dst_ref, bias_ref, cot_ref, mask_ref,
    ext_ref, weight_ref, source_ref, target_ref, scale_ref, pre_ref, stats_ref, flipped_ref, halo_scr, score_scr,
):
    columns, rows = count_ref.shape
    half = (columns - rows) // 2
    heads, width = src_ref.shape
    halo_scr[...] = jnp.zeros_like(halo_scr)
    near_at = jnp.where(is_odd(), 0, half)
    halo_scr[pl.ds(pl.multiple_of(near_at, 16), near_ref.shape[0]), :] = near_ref[...]
    halo_scr[pl.ds(pl.multiple_of(half - near_at, 16), far_ref.shape[0]), :] = far_ref[...]
    flipped_ref[...] = halo_scr[...].T
    stats_ref[...] = jnp.zeros_like(stats_ref)
    nodes, real = real_rows(mask_ref, rows, width)
    for head in range(heads):
        lanes = slice(head * width, (head + 1) * width)
        own = zq_ref[:, lanes]
        ext_ref[0:rows, lanes] = own
        ext_ref[rows:columns, lanes] = mm(halo_scr[...], proj_ref[:, lanes], (1, 0)).astype(BF16)
        ext = ext_ref[:, lanes]
        parts = three_parts(src_ref[head : head + 1, :] * (1.0 / LN2))
        vectors = jnp.concatenate([jnp.broadcast_to(part, (LANES, width)) for part in parts], axis=0)
        source = mm(ext, vectors, (1, 1))
        source_ref[head] = source[:, :LANES] + source[:, LANES : 2 * LANES] + source[:, 2 * LANES :]
        parts = three_parts(dst_ref[head : head + 1, :] * (1.0 / LN2))
        vectors = jnp.concatenate([jnp.broadcast_to(part, (16, width)) for part in parts], axis=0)
        target = mm(vectors, own, (1, 1))
        target = target[0:8] + target[16:24] + target[32:40]
        target_ref[head] = target
        target = target[0:1]

        def score(index, highest, head=head, target=target):
            where = pl.ds(pl.multiple_of(index * CHUNK, CHUNK), CHUNK)
            value = repeat_lanes(source_ref[head, where, :], rows) + target
            small = jnp.exp2(-jnp.abs(value))
            result = jnp.maximum(value, 0.2 * value) + (0.8 / LN2) * jnp.log(1.0 + small) + count_ref[where, :]
            score_scr[where, :] = result
            return jnp.maximum(highest, jnp.max(fold_rows(result), axis=0))

        highest = lax.fori_loop(0, columns // CHUNK, score, jnp.full((8, rows), NEG, F32), unroll=2)
        highest = jnp.max(highest, axis=0, keepdims=True)

        def weigh(index, carry, head=head, highest=highest):
            where = pl.ds(pl.multiple_of(index * CHUNK, CHUNK), CHUNK)
            weight_ref[head, where, :] = jnp.exp2(score_scr[where, :] - highest).astype(BF16)
            return carry

        lax.fori_loop(0, columns // CHUNK, weigh, 0, unroll=2)
        wide = jnp.concatenate([ext, jnp.ones((columns, LANES), BF16)], axis=1)
        summed = mm(weight_ref[head], wide, (0, 0))
        scale = 1.0 / summed[:, width:]
        scale_ref[head] = scale
        pre = summed[:, :width] * repeat_lanes(scale, width) + skip_ref[:, lanes] + bias_ref[:, lanes]
        pre_ref[:, lanes] = pre
        act = jnp.where(pre > 0, pre, jnp.exp(jnp.minimum(pre, 0.0)) - 1.0)
        cot = jnp.where(real, pad_rows(cot_ref[:, lanes].astype(F32), rows), 0.0)
        mean = jnp.sum(jnp.where(real, act, 0.0), axis=0, keepdims=True) / nodes
        centred = jnp.where(real, act - mean, 0.0)
        stats_ref[0:1, lanes] = jnp.broadcast_to(nodes, mean.shape)
        stats_ref[1:2, lanes] = mean
        stats_ref[2:3, lanes] = jnp.sum(centred * centred, axis=0, keepdims=True)
        stats_ref[3:4, lanes] = jnp.sum(cot, axis=0, keepdims=True)
        stats_ref[4:5, lanes] = jnp.sum(cot * centred, axis=0, keepdims=True)


def merged(first, second):
    nodes = first[0:1] + second[0:1]
    gap = second[1:2] - first[1:2]
    part = second[0:1] / nodes
    mean = first[1:2] + gap * part
    spread = first[2:3] + second[2:3] + gap * gap * first[0:1] * part
    shift = first[3:4] + second[3:4]
    gain = first[4:5] + second[4:5] - (mean - first[1:2]) * first[3:4] - (mean - second[1:2]) * second[3:4]
    return nodes, mean, spread, shift, gain


def in_order(mine, other, bit):
    mine_first = bit == 0
    return jnp.where(mine_first, mine, other), jnp.where(mine_first, other, mine)


def merge_kernel(mine_ref, other_ref, out_ref, *, which):
    bit = own_index() // 2**which % 2
    lines = merged(*in_order(mine_ref[...], other_ref[...], bit))
    out_ref[...] = jnp.zeros_like(out_ref)
    for line, value in enumerate(lines):
        out_ref[line : line + 1, :] = value


def place_blocks(out_ref, value, me):
    size = value.shape[0] // SHARDS
    for block in range(SHARDS):
        at = pl.multiple_of((block ^ me) * size, size)
        out_ref[pl.ds(at, size), :] = value[block * size : (block + 1) * size, :]


def core_shares_kernel(keep_ref, other_ref, *outs):
    size = keep_ref.shape[1] // 4 - 4
    for head in range(2):
        vectors = two_parts(whole_of(keep_ref[head, 4 * size :, :]) + whole_of(other_ref[head, 4 * size :, :]))
        for index, out_ref in enumerate(outs):
            rows = slice(index * size, (index + 1) * size)
            out_ref[head, :size, :] = (keep_ref[head, rows, :].astype(F32) + other_ref[head, rows, :].astype(F32)).astype(BF16)
            out_ref[head, size:, :] = vectors


def sum_of_four(refs, head, rows):
    first, second, third, fourth = (ref[head, rows, :].astype(F32) for ref in refs)
    return (first + second + third + fourth).astype(BF16)


def ordered_sum(refs, start, me, scratch):
    for index, ref in enumerate(refs):
        for head in range(2):
            scratch[index ^ me, head] = whole_of(ref[head, start:, :])
    return [scratch[0, head] + scratch[1, head] + scratch[2, head] + scratch[3, head] for head in range(2)]


def plane_sum_kernel(*refs, deps):
    ins, outs, scratch = refs[:4], refs[4 + deps : -1], refs[-1]
    size = outs[0].shape[1] - 16
    vectors = ordered_sum(ins, 4 * size, own_place() // 4, scratch)
    for head in range(2):
        for index, out_ref in enumerate(outs):
            out_ref[head, :size, :] = sum_of_four(ins, head, slice(index * size, (index + 1) * size))
            out_ref[head, size:, :] = two_parts(vectors[head])


def line_sum_kernel(*refs, deps):
    ins, (out_ref, small_ref, scratch) = refs[:4], refs[4 + deps :]
    size = out_ref.shape[1]
    vectors = ordered_sum(ins, size, own_place() % 4, scratch)
    for head in range(2):
        out_ref[head] = sum_of_four(ins, head, slice(0, size))
        small_ref[head] = vectors[head]


def vectors_kernel(mine_ref, other_ref, src_ref, dst_ref, bias_ref):
    odd = is_odd()
    width = src_ref.shape[1]
    for head in range(4):
        mine, other = mine_ref[head % 2], other_ref[head % 2]
        value = jnp.where(odd == (head >= 2), mine, other)
        src_ref[head : head + 1, :] = value[0:1]
        dst_ref[head : head + 1, :] = value[1:2]
        bias_ref[:, head * width : (head + 1) * width] = value[2:3]


def share_sum_kernel(*refs, deps):
    ins, outs = refs[:4], refs[4 + deps :]
    size = outs[0].shape[1]
    for head in range(2):
        for index, out_ref in enumerate(outs):
            out_ref[head] = sum_of_four(ins, head, slice(index * size, (index + 1) * size))


def pair_join_kernel(mine_ref, other_ref, *rest):
    size = mine_ref.shape[1]
    rest[-1][:, :size, :] = mine_ref[...]
    rest[-1][:, size:, :] = other_ref[...]


def heads_join_kernel(mine_ref, other_ref, *outs):
    size = mine_ref.shape[1]
    for head, out_ref in enumerate(outs):
        out_ref[:size, :] = mine_ref[head]
        out_ref[size:, :] = other_ref[head]


def half_join_kernel(*refs):
    for share, near, out_ref in zip(refs[:2], refs[2:4], refs[4:]):
        size = share.shape[0]
        out_ref[:size, :] = share[...]
        out_ref[size:, :] = near[...]


def plane_join_kernel(half_one, half_two, far_one, far_two, low_ref, high_ref):
    size = half_one.shape[0] // 2
    low_ref[0] = half_one[...]
    high_ref[0] = far_one[...]
    for part, out_ref in ((slice(0, size), low_ref), (slice(size, 2 * size), high_ref)):
        out_ref[1, :size, :] = half_two[part, :]
        out_ref[1, size:, :] = far_two[part, :]


def two_sum_kernel(mine_ref, other_ref, *outs, deps=0):
    outs = outs[deps:]
    size = outs[0].shape[1]
    for piece, out_ref in enumerate(outs):
        rows = slice(piece * size, (piece + 1) * size)
        out_ref[...] = (mine_ref[:, rows, :].astype(F32) + other_ref[:, rows, :].astype(F32)).astype(BF16)


def norm_kernel(
    pre_ref, stats_ref, other_ref, cot_ref, mask_ref, gain_ref, shift_ref, flipped_ref,
    out_ref, dskip_ref, send_ref, keep_ref, small_ref, gain_grad_ref, shift_grad_ref, out_scr, done, *, last_bit,
):
    rows = pre_ref.shape[0]
    node_rows, width = out_scr.shape[1:]
    real = real_rows(mask_ref, rows, width)[1]
    copies = []
    for step in range(4):
        head = head_at(step)
        lanes = pl.ds(pl.multiple_of(head * width, width), width)
        pre = pre_ref[:, lanes]
        steep = jnp.exp(jnp.minimum(pre, 0.0))
        act = jnp.where(pre > 0, pre, steep - 1.0)
        first, second = in_order(stats_ref[:, lanes], other_ref[:, lanes], own_index() // 2**last_bit % 2)
        nodes, mean, spread, total, cross = merged(first, second)
        inverse = lax.rsqrt(spread / nodes + 1e-05)
        normed = (act - mean) * inverse
        gain = gain_ref[:, lanes]
        out_scr[step] = jnp.where(real, gain * normed + shift_ref[:, lanes], 0.0)[:node_rows].astype(BF16)
        copies.append(pltpu.make_async_copy(out_scr.at[step], out_ref.at[:, lanes], done.at[step]))
        copies[-1].start()
        gain_grad_ref[:, lanes] = cross * inverse
        shift_grad_ref[:, lanes] = total
        grad = pad_rows(cot_ref[:, lanes].astype(F32), rows) - total / nodes - normed * (cross * inverse / nodes)
        grad_pre = jnp.where(real, grad * (inverse * gain) * steep, 0.0)
        small_ref[head] = jnp.broadcast_to(jnp.sum(grad_pre, axis=0, keepdims=True), small_ref.shape[1:])
        dskip = grad_pre.astype(BF16)
        dskip_ref[:, lanes] = dskip
        grads = mm(flipped_ref[...], dskip, (1, 0)).astype(BF16)
        place_blocks((send_ref if step < 2 else keep_ref).at[step % 2], grads, own_place())
    for copy in copies:
        copy.wait()


def back_kernel(
    weight_ref, source_ref, target_ref, scale_ref, ext_ref, dskip_ref, src_ref, dst_ref, flipped_ref, halo_ref,
    small_in, *rest, part,
):
    grad_ref, own_ref, near_ref, far_ref, dal_scr, sum_scr = rest[-6:]
    columns, rows = weight_ref.shape[1:]
    half = (columns - rows) // 2
    width = src_ref.shape[1]
    depth = flipped_ref.shape[0]
    count = near_ref.shape[0]
    if part:
        near_ref[:, : 2 * width] = rest[0][...]
        far_ref[:, : 2 * width] = rest[1][...]
    for step in range(2):
        head = head_at(part + step)
        lanes = pl.ds(pl.multiple_of(head * width, width), width)
        target = target_ref[head, 0:1, :]
        dskip = dskip_ref[:, lanes]
        dal_scr[...] = mm(ext_ref[:, lanes], dskip, (1, 1))

        def average(index, carry):
            total, mean = carry
            where = pl.ds(pl.multiple_of(index * CHUNK, CHUNK), CHUNK)
            weight = weight_ref[head, where, :].astype(F32)
            return total + jnp.sum(fold_rows(weight), axis=0), mean + jnp.sum(fold_rows(weight * dal_scr[where, :]), axis=0)

        nothing = jnp.zeros((8, rows), F32)
        total, mean = lax.fori_loop(0, columns // CHUNK, average, (nothing, nothing), unroll=2)
        scale = 1.0 / jnp.sum(total, axis=0, keepdims=True)
        mean = jnp.sum(mean, axis=0, keepdims=True) * scale

        def slopes(index, by_target):
            where = pl.ds(pl.multiple_of(index * CHUNK, CHUNK), CHUNK)
            value = repeat_lanes(source_ref[head, where, :], rows) + target
            slope = (0.6 + 0.4 * jnp.tanh(value * (0.5 * LN2))) * scale
            du = weight_ref[head, where, :].astype(F32) * slope * (dal_scr[where, :] - mean)
            sum_scr[where, :] = sum(du[:, at : at + LANES] for at in range(0, rows, LANES))
            return by_target + jnp.sum(fold_rows(du), axis=0)

        by_target = lax.fori_loop(0, columns // CHUNK, slopes, nothing, unroll=2)
        by_target = jnp.sum(by_target, axis=0, keepdims=True)
        by_source = jnp.sum(sum_scr[...], axis=1, keepdims=True)
        ext = ext_ref[:, lanes]
        scaled = (dskip.astype(F32) * repeat_lanes(scale_ref[head], width)).astype(BF16)
        dz = mm(weight_ref[head], scaled, (1, 0)) + by_source * src_ref[pl.ds(head, 1), :]
        high, middle, low = three_parts(by_target)
        row = lax.broadcasted_iota(jnp.int32, (16, rows), 0)
        lines = jnp.where(row == 1, middle.astype(F32), jnp.where(row == 3, low.astype(F32), high.astype(F32)))
        lines = jnp.where(row < 4, lines, 0.0).astype(BF16)
        dst_high, dst_middle, _ = three_parts(dst_ref[pl.ds(head, 1), :])
        row = lax.broadcasted_iota(jnp.int32, (16, width), 0)
        vectors = jnp.where(row == 2, dst_middle.astype(F32), dst_high.astype(F32)).astype(BF16)
        dz_own = dz[:rows] + mm(lines, vectors, (0, 0))
        mine = slice(step * width, (step + 1) * width)
        dz_own = dz_own.astype(BF16)
        own_ref[:, mine] = dz_own
        dz_halo = dz[rows:].astype(BF16)
        below, above = dz[rows : rows + count], dz[rows + half : rows + half + count]
        odd = is_odd()
        at = part * width + step * width
        near_ref[:, at : at + width] = jnp.where(odd, below, above).astype(BF16)
        far_ref[:, at : at + width] = jnp.where(odd, above, below).astype(BF16)
        sums = mm(lines, ext[:rows], (1, 0))
        source_sum = jnp.sum(by_source * ext.astype(F32), axis=0, keepdims=True)
        row = lax.broadcasted_iota(jnp.int32, (8, width), 0)
        lines = jnp.where(row == 0, source_sum, jnp.where(row == 1, sums[0:1] + sums[1:2] + sums[3:4], small_in[head]))
        grad_ref[step, depth:, :] = two_parts(jnp.where(row < 3, lines, 0.0))
        grads = mm(flipped_ref[...], dz_own, (1, 0)) + mm(halo_ref[...], dz_halo, (1, 0))
        place_blocks(grad_ref.at[step], grads.astype(BF16), own_place())


def feats_kernel(own_one, own_two, dskip_ref, proj_ref, skip_ref, total_ref):
    width = own_one.shape[1] // 2
    total = mm(dskip_ref[...], skip_ref[...], (1, 1))
    for step in range(4):
        lanes = pl.ds(pl.multiple_of(head_at(step) * width, width), width)
        own = (own_one if step < 2 else own_two)[:, step % 2 * width : (step % 2 + 1) * width]
        total += mm(own, proj_ref[:, lanes], (1, 1))
    total_ref[...] = total


def feats_halo_kernel(total_ref, near_ref, far_ref, index_ref, proj_ref, out_ref, scratch):
    rows = total_ref.shape[0]
    count = near_ref.shape[0]
    width = near_ref.shape[1] // 4
    picks = one_hot(rows, index_ref, scratch, is_odd())
    picks = jnp.concatenate([picks[:, :count], picks[:, LANES : LANES + count]], axis=1)
    sent = jnp.concatenate([near_ref[...], far_ref[...]], axis=0)
    product = jnp.zeros((2 * count, proj_ref.shape[0]), F32)
    for step in range(4):
        lanes = pl.ds(pl.multiple_of(head_at(step) * width, width), width)
        other = (step + 2) % 4 * width
        product += mm(sent[:, other : other + width], proj_ref[:, lanes], (1, 1))
    high, middle, _ = three_parts(product)
    total = total_ref[...] + mm(picks, high, (1, 0)) + mm(picks, middle, (1, 0))
    out_ref[...] = total[: out_ref.shape[0]].astype(BF16)


def assemble_kernel(*refs, first, pieces):
    out_ref, scratch, done = refs[-3:]
    size, width = scratch.shape[2:]
    me = own_place()
    each = SHARDS // pieces
    copies = []
    for step in range(2):
        lanes = pl.ds(pl.multiple_of(head_at(first + step) * width, width), width)
        for block in range(SHARDS):
            at = pl.multiple_of((block ^ me) * size, size)
            rows = slice(block % each * size, (block % each + 1) * size)
            scratch[step, block] = refs[block // each][step, rows, :].astype(F32)
            copies.append(pltpu.make_async_copy(scratch.at[step, block], out_ref.at[pl.ds(at, size), lanes], done.at[step, block]))
            copies[-1].start()
    for copy in copies:
        copy.wait()


def per_device(
    feats, w_proj, w_skip, attn_src, attn_dst, bias, gain, shift, cotangent, neighbours, edge_mask, node_mask, send_index,
):
    node_rows, depth = feats.shape
    heads, width = attn_src.shape
    concat = heads * width
    slots = neighbours.shape[1]
    halo = send_index.shape[2]
    devices = lax.axis_size(AXES)
    bits = devices.bit_length() - 1
    rows = -(-node_rows // LANES) * LANES
    columns = rows + 2 * STEP
    halo_pad = -(-halo // 16) * 16

    def far_swapped(value):
        pairs = [(low, low + 1) for low in range(1, devices - 1, 2)]
        return lax.ppermute(value, AXES, pairs + [(high, low) for low, high in pairs])

    def swapped(value, distance):
        return lax.ppermute(value, AXES, [(source, source ^ distance) for source in range(devices)])

    mask = node_mask.reshape(1, node_rows)
    bias2, gain2, shift2 = bias[None], gain[None], shift[None]

    in_hbm = lambda value: pltpu.with_memory_space_constraint(value, pltpu.HBM)
    near, far = pl.pallas_call(
        halo_rows_kernel,
        out_shape=[jax.ShapeDtypeStruct((halo_pad, depth), BF16)] * 2,
        scratch_shapes=[pltpu.VMEM((8, 2 * LANES), jnp.int32)],
        compiler_params=params(8),
        name="halo_rows",
    )(in_hbm(feats), in_hbm(send_index))
    near, far = swapped(near, 1), far_swapped(far)

    def spec(shape, index):
        return pl.BlockSpec(shape, index)

    def whole(*shape):
        return pl.BlockSpec(shape, lambda *_: (0,) * len(shape))

    by_head = lambda n: pl.BlockSpec((n, width), lambda h, *_: (0, h))
    stacked = lambda *shape: pl.BlockSpec((1, *shape), lambda h, *_: (h, 0, 0))
    shape_of = jax.ShapeDtypeStruct
    zq, skip, count, flipped = pl.pallas_call(
        functools.partial(project_kernel, halo=halo),
        grid=(heads,),
        in_specs=[
            whole(node_rows, depth), by_head(depth), by_head(depth), whole(slots, node_rows), whole(slots, node_rows),
        ],
        out_specs=[by_head(rows), by_head(rows), whole(columns, rows), whole(depth, rows)],
        scratch_shapes=[pltpu.VMEM((rows, depth), BF16)],
        out_shape=[
            shape_of((rows, concat), BF16),
            shape_of((rows, concat), F32),
            shape_of((columns, rows), F32),
            shape_of((depth, rows), BF16),
        ],
        compiler_params=params(),
        cost_estimate=cost(5),
        name="project",
    )(in_hbm(feats), in_hbm(w_proj), in_hbm(w_skip), in_hbm(neighbours.T), in_hbm(edge_mask.T))

    vmem = pl.BlockSpec(memory_space=pltpu.VMEM)
    anywhere = pl.BlockSpec(memory_space=pl.ANY)
    ext, weight, source, target, scale, pre, stats, halo_flipped = pl.pallas_call(
        attend_kernel,
        in_specs=[vmem] * 11,
        out_shape=[
            shape_of((columns, concat), BF16),
            shape_of((heads, columns, rows), BF16),
            shape_of((heads, columns, LANES), F32),
            shape_of((heads, 8, rows), F32),
            shape_of((heads, rows, LANES), F32),
            shape_of((rows, concat), F32),
            shape_of((8, concat), F32),
            shape_of((depth, columns - rows), BF16),
        ],
        scratch_shapes=[pltpu.VMEM((columns - rows, depth), BF16), pltpu.VMEM((columns, rows), F32)],
        compiler_params=params(8),
        cost_estimate=cost(8),
        name="attend",
    )(zq, near, far, w_proj, skip, count, attn_src, attn_dst, bias2, cotangent, mask)

    for which in range(bits - 1):
        stats = pl.pallas_call(
            functools.partial(merge_kernel, which=which),
            in_specs=[pl.BlockSpec(memory_space=pltpu.VMEM)] * 2,
            out_shape=shape_of(stats.shape, F32),
            compiler_params=params(1),
            name="merge",
        )(stats, swapped(stats, 1 << which))
    other = swapped(stats, 1 << (bits - 1))

    half_grad = shape_of((2, depth, width), BF16)
    output, dskip, skip_send, skip_keep, small, gain_grad, shift_grad = pl.pallas_call(
        functools.partial(norm_kernel, last_bit=bits - 1),
        in_specs=[vmem] * 8,
        out_specs=[anywhere] + [vmem] * 6,
        out_shape=[
            pltpu.HBM((node_rows, concat), BF16),
            shape_of((rows, concat), BF16),
            half_grad,
            half_grad,
            shape_of((heads, 8, width), F32),
            jax.ShapeDtypeStruct((1, concat), F32),
            jax.ShapeDtypeStruct((1, concat), F32),
        ],
        scratch_shapes=[pltpu.VMEM((heads, node_rows, width), BF16), pltpu.SemaphoreType.DMA((heads,))],
        compiler_params=params(16),
        cost_estimate=cost(0.1),
        name="norm",
    )(pre, stats, other, cotangent, mask, gain2, shift2, flipped)

    def backward(part, arrays=(), deps=()):
        return pl.pallas_call(
            functools.partial(back_kernel, part=part),
            in_specs=[vmem] * (11 + len(arrays)) + [anywhere] * len(deps),
            out_shape=[
                shape_of((2, depth + 16, width), BF16),
                shape_of((rows, 2 * width), BF16),
                shape_of((halo_pad, (2 + part) * width), BF16),
                shape_of((halo_pad, (2 + part) * width), BF16),
            ],
            scratch_shapes=[pltpu.VMEM((columns, rows), F32), pltpu.VMEM((columns, LANES), F32)],
            compiler_params=params(8),
            cost_estimate=cost(0.1),
            name="back",
        )(weight, source, target, scale, ext, dskip, attn_src, attn_dst, flipped, halo_flipped, small, *arrays, *deps)

    quarter = (2, depth // 4, width)
    piece = (2, depth // SHARDS, width)
    def step_call(kernel, name, shapes, arrays, deps=()):
        return pl.pallas_call(
            kernel,
            in_specs=[vmem] * len(arrays) + [anywhere] * len(deps),
            out_shape=[shape_of(shape, BF16) for shape in shapes],
            compiler_params=params(1),
            cost_estimate=cost(0.1),
            name=name,
        )(*arrays, *deps)

    def over_plane(shares):
        return [swapped(share, distance << 1) for distance, share in zip((1, 2, 3), shares)]

    def over_line(shares):
        return [swapped(share, distance) for distance, share in zip((16, 8, 24), shares)]

    def ordered_call(kernel, name, shapes, arrays, deps):
        return pl.pallas_call(
            functools.partial(kernel, deps=len(deps)),
            in_specs=[vmem] * len(arrays) + [anywhere] * len(deps),
            out_shape=shapes,
            scratch_shapes=[pltpu.VMEM((4, 2, 8, width), F32)],
            compiler_params=params(1),
            cost_estimate=cost(0.1),
            name=name,
        )(*arrays, *deps)

    def plane_sum(arrays, deps):
        shapes = [shape_of((2, depth // SHARDS + 16, width), BF16)] * 4
        return ordered_call(plane_sum_kernel, "p_plane", shapes, arrays, deps)

    def line_sum(arrays, deps):
        shapes = [shape_of(piece, BF16), shape_of((2, 8, width), F32)]
        return ordered_call(line_sum_kernel, "p_line", shapes, arrays, deps)

    def two_sum(name, arrays, count, deps=()):
        shapes = [(2, arrays[0].shape[1] // count, width)] * count
        return step_call(functools.partial(two_sum_kernel, deps=len(deps)), name, shapes, arrays, deps)

    def pair_join(name, mine, other, deps=()):
        return step_call(pair_join_kernel, name, [(2, 2 * mine.shape[1], width)], [mine, other], deps)[0]

    def share_sum(name, arrays, count, deps):
        shapes = [(2, arrays[0].shape[1] // count, width)] * count
        return step_call(functools.partial(share_sum_kernel, deps=len(deps)), name, shapes, arrays, deps)

    def assemble(pieces, first, *out):
        return pl.pallas_call(
            functools.partial(assemble_kernel, first=first, pieces=len(pieces)),
            in_specs=[vmem] * len(pieces) + [anywhere] * len(out),
            out_specs=anywhere,
            out_shape=pltpu.HBM((depth, concat), F32),
            scratch_shapes=[pltpu.VMEM((2, SHARDS, depth // SHARDS, width), F32), pltpu.SemaphoreType.DMA((2, SHARDS))],
            input_output_aliases={len(pieces): 0} if out else {},
            compiler_params=params(8),
            cost_estimate=cost(0.1),
            name="assemble",
        )(*pieces, *out)

    def beyond(value):
        for which in range(5, bits):
            value = value + swapped(value, 1 << which)
        return value

    def after(value, *others):
        return lax.optimization_barrier((value, *others))[0]

    skip_other = swapped(skip_send, 1)
    proj_send, own_send, near_send, far_send = backward(0)
    proj_other = swapped(proj_send, 1)
    s_mine, *s_rest = step_call(
        functools.partial(two_sum_kernel, deps=1), "s_core", [quarter] * 4, [skip_keep, skip_other], [proj_send]
    )
    s_got = over_plane(s_rest)
    proj_keep, own_keep, back_near, back_far = backward(2, [near_send, far_send], [s_mine])
    p_mine, *p_rest = step_call(core_shares_kernel, "p_core", [(2, depth // 4 + 16, width)] * 4, [proj_keep, proj_other])
    p_got = over_plane(p_rest)
    s_mine, s_rest = share_sum("s_plane", [s_mine, *s_got], 2, [p_mine])
    s_mine, s_rest = two_sum("s_line", [s_mine, swapped(s_rest, 8)], 2)
    p_mine, *p_rest = plane_sum([p_mine, *p_got], [])
    p_got = over_line(p_rest)
    s_piece = beyond(two_sum("s_line", [s_mine, swapped(s_rest, 16)], 1, [p_mine])[0])
    s_piece = pair_join("s_join", s_piece, swapped(s_piece, 16))
    s_share = step_call(heads_join_kernel, "s_share", [(depth // 4, width)] * 2, [s_piece, swapped(s_piece, 8)])
    s_near = (swapped(s_share[0], 2), swapped(s_share[1], 4))
    s_sent = step_call(half_join_kernel, "s_near", [(depth // 2, width)] * 2, [*s_share, *s_near])
    s_far = (swapped(s_sent[0], 4), swapped(s_sent[1], 2))
    back_near, back_far = swapped(after(back_near, p_mine), 1), far_swapped(after(back_far, p_mine))
    p_piece, small = line_sum([p_mine, *p_got], [back_near, back_far])
    p_piece, small = beyond(p_piece), beyond(small)
    small_other = swapped(small, 1)
    p_piece = pair_join("p_join", p_piece, swapped(p_piece, 16))
    p_share = pair_join("p_join", p_piece, swapped(p_piece, 8), [small_other])
    p_got = over_plane([p_share] * 3)
    feats_total = pl.pallas_call(
        feats_kernel,
        in_specs=[vmem] * 5,
        out_specs=vmem,
        out_shape=shape_of((rows, depth), F32),
        compiler_params=params(8),
        cost_estimate=cost(0.1),
        name="features",
    )(own_send, own_keep, dskip, w_proj, w_skip)
    grad_src, grad_dst, grad_bias = pl.pallas_call(
        vectors_kernel,
        out_shape=[
            jax.ShapeDtypeStruct((heads, width), F32),
            jax.ShapeDtypeStruct((heads, width), F32),
            jax.ShapeDtypeStruct((1, concat), F32),
        ],
        compiler_params=params(1),
        cost_estimate=cost(0.1),
        name="vectors",
    )(small, small_other)
    p_got = [p_share, *(after(share, grad_src, back_near, back_far, feats_total) for share in p_got)]
    p_other = [swapped(share, 1) for share in p_got]
    s_halves = step_call(plane_join_kernel, "s_half", [(2, depth // 2, width)] * 2, [*s_sent, *s_far])
    s_other = [swapped(half, 1) for half in s_halves]
    grad_skip = assemble(s_other, 0, assemble(s_halves, 2))
    grad_proj = assemble(p_other, 0, assemble(p_got, 2))

    grad_feats = pl.pallas_call(
        feats_halo_kernel,
        in_specs=[vmem] * 5,
        out_specs=vmem,
        scratch_shapes=[pltpu.VMEM((8, 2 * LANES), jnp.int32)],
        out_shape=jax.ShapeDtypeStruct((node_rows, depth), BF16),
        compiler_params=params(8),
        cost_estimate=cost(0.1),
        name="features_halo",
    )(feats_total, back_near, back_far, send_index, w_proj)

    return (
        output,
        grad_feats,
        grad_proj,
        grad_skip,
        grad_src,
        grad_dst,
        grad_bias.reshape(concat),
        gain_grad.reshape(concat),
        shift_grad.reshape(concat),
    )


def solution(mesh):
    rows = P(AXES, None)
    in_specs = (rows,) + (P(),) * 7 + (rows, rows, rows, P(AXES), P(AXES, None, None))
    out_specs = (rows, rows) + (P(),) * 7
    return jax.shard_map(per_device, mesh=mesh, in_specs=in_specs, out_specs=out_specs, check_vma=False)
```

```python
import functools

import jax
import jax.numpy as jnp
from jax import lax
from jax.experimental import pallas as pl
from jax.experimental.pallas import tpu as pltpu
from jax.sharding import PartitionSpec as P

AXES = ("dom", "sub")
F32 = jnp.float32
BF16 = jnp.bfloat16
NEG = -1e30
LN2 = 0.6931471805599453
STEP = 64
SHARDS = 16
CHUNK = 32
LANES = 128
MIB = 1024 * 1024
COSTS = {"p_plane": 0.1, "p_line": 0.5, "p_join": 0.5}


def params(mib=24):
    return pltpu.CompilerParams(vmem_limit_bytes=mib * MIB)


def cost(us):
    return pl.CostEstimate(flops=int(us * 1.1e9), bytes_accessed=int(us * 1e6), transcendentals=0)


def mm(a, b, contract):
    return lax.dot_general(a, b, ((contract[:1], contract[1:]), ((), ())), preferred_element_type=F32)


def pad_rows(value, rows):
    extra = rows - value.shape[0]
    if extra == 0:
        return value
    return jnp.concatenate([value, jnp.zeros((extra,) + value.shape[1:], value.dtype)], axis=0)


def three_parts(value):
    high = value.astype(BF16)
    rest = value - high.astype(F32)
    middle = rest.astype(BF16)
    low = (rest - middle.astype(F32)).astype(BF16)
    return high, middle, low


def two_parts(value):
    high = value.astype(BF16).astype(F32)
    return jnp.concatenate([high, value - high], axis=0).astype(BF16)


def whole_of(parts):
    parts = parts.astype(F32)
    return parts[:8] + parts[8:]


def repeat_lanes(value, columns):
    return jnp.concatenate([value] * (columns // value.shape[1]), axis=1)


def fold_rows(value):
    return value.reshape(value.shape[0] // 8, 8, value.shape[1])


def real_rows(mask_ref, rows, columns):
    count = jnp.sum(mask_ref[...].astype(F32), axis=1, keepdims=True)
    real = lax.broadcasted_iota(jnp.int32, (rows, columns), 0).astype(F32) < count
    return count, real


def one_hot(rows, index_ref, scratch, odd):
    halo = index_ref.shape[2]
    down, up = index_ref[0, 0:1, :], index_ref[0, 1:2, :]
    scratch[...] = jnp.full(scratch.shape, -1, jnp.int32)
    scratch[0:1, 0:halo] = jnp.where(odd, down, up)
    scratch[0:1, LANES : LANES + halo] = jnp.where(odd, up, down)
    wanted = scratch[0:1, :]
    return (lax.broadcasted_iota(jnp.int32, (rows, 2 * LANES), 0) == wanted).astype(BF16)


def own_index():
    return lax.axis_index(AXES[0]) * lax.axis_size(AXES[1]) + lax.axis_index(AXES[1])


def is_odd():
    return lax.axis_index(AXES[1]) % 2 == 1


def own_place():
    me = own_index()
    return (me // 2 % 4) * 4 + (me // 8 % 2) * 2 + me // 16 % 2


def head_at(step):
    core = lax.axis_index(AXES[1]) % 2
    return (2 - 2 * core if step < 2 else 2 * core) + step % 2


def halo_rows_kernel(feats_ref, index_ref, near_ref, far_ref, scratch):
    picked = one_hot(feats_ref.shape[0], index_ref, scratch, is_odd())
    rows = mm(picked, feats_ref[...], (0, 0)).astype(BF16)
    near_ref[...] = rows[: near_ref.shape[0]]
    far_ref[...] = rows[LANES : LANES + far_ref.shape[0]]


def project_kernel(
    feats_ref, proj_ref, skip_w_ref, neighbours_ref, mask_ref, zq_ref, skip_ref, count_ref, flipped_ref, padded,
    *, halo,
):
    node_rows = feats_ref.shape[0]
    columns, rows = count_ref.shape

    @pl.when(pl.program_id(0) == 0)
    def _():
        feats = pad_rows(feats_ref[...].astype(F32), rows).astype(BF16)
        padded[...] = feats
        flipped_ref[...] = feats.T

    zq_ref[...] = mm(padded[...], proj_ref[...], (1, 0)).astype(BF16)
    skip_ref[...] = mm(padded[...], skip_w_ref[...], (1, 0))

    names = neighbours_ref[...]
    names = names + jnp.where(names >= node_rows, rows - node_rows, 0)
    names = names + jnp.where(names >= rows + halo, STEP - halo, 0)
    names = jnp.where(mask_ref[...] > 0, names, -1)
    names = jnp.concatenate([names, jnp.full((names.shape[0], rows - node_rows), -1, jnp.int32)], axis=1)
    own = lax.broadcasted_iota(jnp.int32, (8, rows), 1)
    share = columns // 4

    def chunk(index, carry):
        start = pl.multiple_of(pl.program_id(0) * share + index * 8, 8)
        source = lax.broadcasted_iota(jnp.int32, (8, rows), 0) + start
        total = (source == own).astype(F32)
        for slot in range(names.shape[0]):
            total += jnp.where(source == names[slot : slot + 1, :], 1.0, 0.0)
        count_ref[pl.ds(start, 8), :] = jnp.where(total > 0, jnp.log(jnp.maximum(total, 1.0)) * (1.0 / LN2), NEG)
        return carry

    lax.fori_loop(0, share // 8, chunk, 0, unroll=2)


def attend_kernel(
    zq_ref, near_ref, far_ref, proj_ref, skip_ref, count_ref, src_ref, dst_ref, bias_ref, cot_ref, mask_ref,
    ext_ref, weight_ref, source_ref, target_ref, scale_ref, pre_ref, stats_ref, flipped_ref, halo_scr, score_scr,
):
    columns, rows = count_ref.shape
    half = (columns - rows) // 2
    heads, width = src_ref.shape
    halo_scr[...] = jnp.zeros_like(halo_scr)
    near_at = jnp.where(is_odd(), 0, half)
    halo_scr[pl.ds(pl.multiple_of(near_at, 16), near_ref.shape[0]), :] = near_ref[...]
    halo_scr[pl.ds(pl.multiple_of(half - near_at, 16), far_ref.shape[0]), :] = far_ref[...]
    flipped_ref[...] = halo_scr[...].T
    stats_ref[...] = jnp.zeros_like(stats_ref)
    nodes, real = real_rows(mask_ref, rows, width)
    for head in range(heads):
        lanes = slice(head * width, (head + 1) * width)
        own = zq_ref[:, lanes]
        ext_ref[0:rows, lanes] = own
        ext_ref[rows:columns, lanes] = mm(halo_scr[...], proj_ref[:, lanes], (1, 0)).astype(BF16)
        ext = ext_ref[:, lanes]
        parts = three_parts(src_ref[head : head + 1, :] * (1.0 / LN2))
        vectors = jnp.concatenate([jnp.broadcast_to(part, (LANES, width)) for part in parts], axis=0)
        source = mm(ext, vectors, (1, 1))
        source_ref[head] = source[:, :LANES] + source[:, LANES : 2 * LANES] + source[:, 2 * LANES :]
        parts = three_parts(dst_ref[head : head + 1, :] * (1.0 / LN2))
        vectors = jnp.concatenate([jnp.broadcast_to(part, (16, width)) for part in parts], axis=0)
        target = mm(vectors, own, (1, 1))
        target = target[0:8] + target[16:24] + target[32:40]
        target_ref[head] = target
        target = target[0:1]

        def score(index, highest, head=head, target=target):
            where = pl.ds(pl.multiple_of(index * CHUNK, CHUNK), CHUNK)
            value = repeat_lanes(source_ref[head, where, :], rows) + target
            small = jnp.exp2(-jnp.abs(value))
            result = jnp.maximum(value, 0.2 * value) + (0.8 / LN2) * jnp.log(1.0 + small) + count_ref[where, :]
            score_scr[where, :] = result
            return jnp.maximum(highest, jnp.max(fold_rows(result), axis=0))

        highest = lax.fori_loop(0, columns // CHUNK, score, jnp.full((8, rows), NEG, F32), unroll=2)
        highest = jnp.max(highest, axis=0, keepdims=True)

        def weigh(index, carry, head=head, highest=highest):
            where = pl.ds(pl.multiple_of(index * CHUNK, CHUNK), CHUNK)
            weight_ref[head, where, :] = jnp.exp2(score_scr[where, :] - highest).astype(BF16)
            return carry

        lax.fori_loop(0, columns // CHUNK, weigh, 0, unroll=2)
        wide = jnp.concatenate([ext, jnp.ones((columns, LANES), BF16)], axis=1)
        summed = mm(weight_ref[head], wide, (0, 0))
        scale = 1.0 / summed[:, width:]
        scale_ref[head] = scale
        pre = summed[:, :width] * repeat_lanes(scale, width) + skip_ref[:, lanes] + bias_ref[:, lanes]
        pre_ref[:, lanes] = pre
        act = jnp.where(pre > 0, pre, jnp.exp(jnp.minimum(pre, 0.0)) - 1.0)
        cot = jnp.where(real, pad_rows(cot_ref[:, lanes].astype(F32), rows), 0.0)
        mean = jnp.sum(jnp.where(real, act, 0.0), axis=0, keepdims=True) / nodes
        centred = jnp.where(real, act - mean, 0.0)
        stats_ref[0:1, lanes] = jnp.broadcast_to(nodes, mean.shape)
        stats_ref[1:2, lanes] = mean
        stats_ref[2:3, lanes] = jnp.sum(centred * centred, axis=0, keepdims=True)
        stats_ref[3:4, lanes] = jnp.sum(cot, axis=0, keepdims=True)
        stats_ref[4:5, lanes] = jnp.sum(cot * centred, axis=0, keepdims=True)


def merged(first, second):
    nodes = first[0:1] + second[0:1]
    gap = second[1:2] - first[1:2]
    part = second[0:1] / nodes
    mean = first[1:2] + gap * part
    spread = first[2:3] + second[2:3] + gap * gap * first[0:1] * part
    shift = first[3:4] + second[3:4]
    gain = first[4:5] + second[4:5] - (mean - first[1:2]) * first[3:4] - (mean - second[1:2]) * second[3:4]
    return nodes, mean, spread, shift, gain


def in_order(mine, other, bit):
    mine_first = bit == 0
    return jnp.where(mine_first, mine, other), jnp.where(mine_first, other, mine)


def merge_kernel(mine_ref, other_ref, out_ref, *, which):
    bit = own_index() // 2**which % 2
    lines = merged(*in_order(mine_ref[...], other_ref[...], bit))
    out_ref[...] = jnp.zeros_like(out_ref)
    for line, value in enumerate(lines):
        out_ref[line : line + 1, :] = value


def place_blocks(out_ref, value, me):
    size = value.shape[0] // SHARDS
    for block in range(SHARDS):
        at = pl.multiple_of((block ^ me) * size, size)
        out_ref[pl.ds(at, size), :] = value[block * size : (block + 1) * size, :]


def core_shares_kernel(keep_ref, other_ref, *outs):
    size = keep_ref.shape[1] // 4 - 4
    for head in range(2):
        vectors = two_parts(whole_of(keep_ref[head, 4 * size :, :]) + whole_of(other_ref[head, 4 * size :, :]))
        for index, out_ref in enumerate(outs):
            rows = slice(index * size, (index + 1) * size)
            out_ref[head, :size, :] = (keep_ref[head, rows, :].astype(F32) + other_ref[head, rows, :].astype(F32)).astype(BF16)
            out_ref[head, size:, :] = vectors


def sum_of_four(refs, head, rows):
    first, second, third, fourth = (ref[head, rows, :].astype(F32) for ref in refs)
    return (first + second + third + fourth).astype(BF16)


def ordered_sum(refs, start, me, scratch):
    for index, ref in enumerate(refs):
        for head in range(2):
            scratch[index ^ me, head] = whole_of(ref[head, start:, :])
    return [scratch[0, head] + scratch[1, head] + scratch[2, head] + scratch[3, head] for head in range(2)]


def plane_sum_kernel(*refs, deps):
    ins, outs, scratch = refs[:4], refs[4 + deps : -1], refs[-1]
    size = outs[0].shape[1] - 16
    vectors = ordered_sum(ins, 4 * size, own_place() // 4, scratch)
    for head in range(2):
        for index, out_ref in enumerate(outs):
            out_ref[head, :size, :] = sum_of_four(ins, head, slice(index * size, (index + 1) * size))
            out_ref[head, size:, :] = two_parts(vectors[head])


def line_sum_kernel(*refs, deps):
    ins, (out_ref, small_ref, scratch) = refs[:4], refs[4 + deps :]
    size = out_ref.shape[1]
    vectors = ordered_sum(ins, size, own_place() % 4, scratch)
    for head in range(2):
        out_ref[head] = sum_of_four(ins, head, slice(0, size))
        small_ref[head] = vectors[head]


def vectors_kernel(mine_ref, other_ref, dep_ref, src_ref, dst_ref, bias_ref):
    odd = is_odd()
    width = src_ref.shape[1]
    for head in range(4):
        mine, other = mine_ref[head % 2], other_ref[head % 2]
        value = jnp.where(odd == (head >= 2), mine, other)
        src_ref[head : head + 1, :] = value[0:1]
        dst_ref[head : head + 1, :] = value[1:2]
        bias_ref[:, head * width : (head + 1) * width] = value[2:3]


def share_sum_kernel(*refs, deps):
    ins, outs = refs[:4], refs[4 + deps :]
    size = outs[0].shape[1]
    for head in range(2):
        for index, out_ref in enumerate(outs):
            out_ref[head] = sum_of_four(ins, head, slice(index * size, (index + 1) * size))


def pair_join_kernel(mine_ref, other_ref, *rest):
    size = mine_ref.shape[1]
    rest[-1][:, :size, :] = mine_ref[...]
    rest[-1][:, size:, :] = other_ref[...]


def heads_join_kernel(mine_ref, other_ref, *outs):
    size = mine_ref.shape[1]
    for head, out_ref in enumerate(outs):
        out_ref[:size, :] = mine_ref[head]
        out_ref[size:, :] = other_ref[head]


def half_join_kernel(*refs):
    for share, near, out_ref in zip(refs[:2], refs[2:4], refs[4:]):
        size = share.shape[0]
        out_ref[:size, :] = share[...]
        out_ref[size:, :] = near[...]


def plane_join_kernel(half_one, half_two, far_one, far_two, *rest):
    low_ref, high_ref = rest[-2:]
    size = half_one.shape[0] // 2
    low_ref[0] = half_one[...]
    high_ref[0] = far_one[...]
    for part, out_ref in ((slice(0, size), low_ref), (slice(size, 2 * size), high_ref)):
        out_ref[1, :size, :] = half_two[part, :]
        out_ref[1, size:, :] = far_two[part, :]


def two_sum_kernel(mine_ref, other_ref, *outs, deps=0):
    outs = outs[deps:]
    size = outs[0].shape[1]
    for piece, out_ref in enumerate(outs):
        rows = slice(piece * size, (piece + 1) * size)
        out_ref[...] = (mine_ref[:, rows, :].astype(F32) + other_ref[:, rows, :].astype(F32)).astype(BF16)


def norm_kernel(
    pre_ref, stats_ref, other_ref, cot_ref, mask_ref, gain_ref, shift_ref, flipped_ref,
    out_ref, dskip_ref, send_ref, keep_ref, small_ref, gain_grad_ref, shift_grad_ref, out_scr, done, *, last_bit,
):
    rows = pre_ref.shape[0]
    node_rows, width = out_scr.shape[1:]
    real = real_rows(mask_ref, rows, width)[1]
    copies = []
    for step in range(4):
        head = head_at(step)
        lanes = pl.ds(pl.multiple_of(head * width, width), width)
        pre = pre_ref[:, lanes]
        steep = jnp.exp(jnp.minimum(pre, 0.0))
        act = jnp.where(pre > 0, pre, steep - 1.0)
        first, second = in_order(stats_ref[:, lanes], other_ref[:, lanes], own_index() // 2**last_bit % 2)
        nodes, mean, spread, total, cross = merged(first, second)
        inverse = lax.rsqrt(spread / nodes + 1e-05)
        normed = (act - mean) * inverse
        gain = gain_ref[:, lanes]
        out_scr[step] = jnp.where(real, gain * normed + shift_ref[:, lanes], 0.0)[:node_rows].astype(BF16)
        copies.append(pltpu.make_async_copy(out_scr.at[step], out_ref.at[:, lanes], done.at[step]))
        copies[-1].start()
        gain_grad_ref[:, lanes] = cross * inverse
        shift_grad_ref[:, lanes] = total
        grad = pad_rows(cot_ref[:, lanes].astype(F32), rows) - total / nodes - normed * (cross * inverse / nodes)
        grad_pre = jnp.where(real, grad * (inverse * gain) * steep, 0.0)
        small_ref[head] = jnp.broadcast_to(jnp.sum(grad_pre, axis=0, keepdims=True), small_ref.shape[1:])
        dskip = grad_pre.astype(BF16)
        dskip_ref[:, lanes] = dskip
        grads = mm(flipped_ref[...], dskip, (1, 0)).astype(BF16)
        place_blocks((send_ref if step < 2 else keep_ref).at[step % 2], grads, own_place())
    for copy in copies:
        copy.wait()


def back_kernel(
    weight_ref, source_ref, target_ref, scale_ref, ext_ref, dskip_ref, src_ref, dst_ref, flipped_ref, halo_ref,
    small_in, *rest, part,
):
    grad_ref, own_ref, near_ref, far_ref, dal_scr, sum_scr = rest[-6:]
    columns, rows = weight_ref.shape[1:]
    half = (columns - rows) // 2
    width = src_ref.shape[1]
    depth = flipped_ref.shape[0]
    count = near_ref.shape[0]
    if part:
        near_ref[:, : 2 * width] = rest[0][...]
        far_ref[:, : 2 * width] = rest[1][...]
    for step in range(2):
        head = head_at(part + step)
        lanes = pl.ds(pl.multiple_of(head * width, width), width)
        target = target_ref[head, 0:1, :]
        dskip = dskip_ref[:, lanes]
        dal_scr[...] = mm(ext_ref[:, lanes], dskip, (1, 1))

        def average(index, carry):
            total, mean = carry
            where = pl.ds(pl.multiple_of(index * CHUNK, CHUNK), CHUNK)
            weight = weight_ref[head, where, :].astype(F32)
            return total + jnp.sum(fold_rows(weight), axis=0), mean + jnp.sum(fold_rows(weight * dal_scr[where, :]), axis=0)

        nothing = jnp.zeros((8, rows), F32)
        total, mean = lax.fori_loop(0, columns // CHUNK, average, (nothing, nothing), unroll=2)
        scale = 1.0 / jnp.sum(total, axis=0, keepdims=True)
        mean = jnp.sum(mean, axis=0, keepdims=True) * scale

        def slopes(index, by_target):
            where = pl.ds(pl.multiple_of(index * CHUNK, CHUNK), CHUNK)
            value = repeat_lanes(source_ref[head, where, :], rows) + target
            slope = (0.6 + 0.4 * jnp.tanh(value * (0.5 * LN2))) * scale
            du = weight_ref[head, where, :].astype(F32) * slope * (dal_scr[where, :] - mean)
            sum_scr[where, :] = sum(du[:, at : at + LANES] for at in range(0, rows, LANES))
            return by_target + jnp.sum(fold_rows(du), axis=0)

        by_target = lax.fori_loop(0, columns // CHUNK, slopes, nothing, unroll=2)
        by_target = jnp.sum(by_target, axis=0, keepdims=True)
        by_source = jnp.sum(sum_scr[...], axis=1, keepdims=True)
        ext = ext_ref[:, lanes]
        scaled = (dskip.astype(F32) * repeat_lanes(scale_ref[head], width)).astype(BF16)
        dz = mm(weight_ref[head], scaled, (1, 0)) + by_source * src_ref[pl.ds(head, 1), :]
        high, middle, low = three_parts(by_target)
        row = lax.broadcasted_iota(jnp.int32, (16, rows), 0)
        lines = jnp.where(row == 1, middle.astype(F32), jnp.where(row == 3, low.astype(F32), high.astype(F32)))
        lines = jnp.where(row < 4, lines, 0.0).astype(BF16)
        dst_high, dst_middle, _ = three_parts(dst_ref[pl.ds(head, 1), :])
        row = lax.broadcasted_iota(jnp.int32, (16, width), 0)
        vectors = jnp.where(row == 2, dst_middle.astype(F32), dst_high.astype(F32)).astype(BF16)
        dz_own = dz[:rows] + mm(lines, vectors, (0, 0))
        mine = slice(step * width, (step + 1) * width)
        dz_own = dz_own.astype(BF16)
        own_ref[:, mine] = dz_own
        dz_halo = dz[rows:].astype(BF16)
        below, above = dz[rows : rows + count], dz[rows + half : rows + half + count]
        odd = is_odd()
        at = part * width + step * width
        near_ref[:, at : at + width] = jnp.where(odd, below, above).astype(BF16)
        far_ref[:, at : at + width] = jnp.where(odd, above, below).astype(BF16)
        sums = mm(lines, ext[:rows], (1, 0))
        source_sum = jnp.sum(by_source * ext.astype(F32), axis=0, keepdims=True)
        row = lax.broadcasted_iota(jnp.int32, (8, width), 0)
        lines = jnp.where(row == 0, source_sum, jnp.where(row == 1, sums[0:1] + sums[1:2] + sums[3:4], small_in[head]))
        grad_ref[step, depth:, :] = two_parts(jnp.where(row < 3, lines, 0.0))
        grads = mm(flipped_ref[...], dz_own, (1, 0)) + mm(halo_ref[...], dz_halo, (1, 0))
        place_blocks(grad_ref.at[step], grads.astype(BF16), own_place())


def feats_kernel(own_one, own_two, dskip_ref, proj_ref, skip_ref, dep_ref, total_ref):
    width = own_one.shape[1] // 2
    total = mm(dskip_ref[...], skip_ref[...], (1, 1))
    for step in range(4):
        lanes = pl.ds(pl.multiple_of(head_at(step) * width, width), width)
        own = (own_one if step < 2 else own_two)[:, step % 2 * width : (step % 2 + 1) * width]
        total += mm(own, proj_ref[:, lanes], (1, 1))
    total_ref[...] = total


def feats_halo_kernel(total_ref, near_ref, far_ref, index_ref, proj_ref, out_ref, scratch):
    rows = total_ref.shape[0]
    count = near_ref.shape[0]
    width = near_ref.shape[1] // 4
    picks = one_hot(rows, index_ref, scratch, is_odd())
    picks = jnp.concatenate([picks[:, :count], picks[:, LANES : LANES + count]], axis=1)
    sent = jnp.concatenate([near_ref[...], far_ref[...]], axis=0)
    product = jnp.zeros((2 * count, proj_ref.shape[0]), F32)
    for step in range(4):
        lanes = pl.ds(pl.multiple_of(head_at(step) * width, width), width)
        other = (step + 2) % 4 * width
        product += mm(sent[:, other : other + width], proj_ref[:, lanes], (1, 1))
    high, middle, _ = three_parts(product)
    total = total_ref[...] + mm(picks, high, (1, 0)) + mm(picks, middle, (1, 0))
    out_ref[...] = total[: out_ref.shape[0]].astype(BF16)


def assemble_kernel(*refs, first, pieces):
    out_ref, scratch, done = refs[-3:]
    size, width = scratch.shape[2:]
    me = own_place()
    each = SHARDS // pieces
    copies = []
    for step in range(2):
        lanes = pl.ds(pl.multiple_of(head_at(first + step) * width, width), width)
        for block in range(SHARDS):
            at = pl.multiple_of((block ^ me) * size, size)
            rows = slice(block % each * size, (block % each + 1) * size)
            scratch[step, block] = refs[block // each][step, rows, :].astype(F32)
            copies.append(pltpu.make_async_copy(scratch.at[step, block], out_ref.at[pl.ds(at, size), lanes], done.at[step, block]))
            copies[-1].start()
    for copy in copies:
        copy.wait()


def per_device(
    feats, w_proj, w_skip, attn_src, attn_dst, bias, gain, shift, cotangent, neighbours, edge_mask, node_mask, send_index,
):
    node_rows, depth = feats.shape
    heads, width = attn_src.shape
    concat = heads * width
    slots = neighbours.shape[1]
    halo = send_index.shape[2]
    devices = lax.axis_size(AXES)
    bits = devices.bit_length() - 1
    rows = -(-node_rows // LANES) * LANES
    columns = rows + 2 * STEP
    halo_pad = -(-halo // 16) * 16

    def far_swapped(value):
        pairs = [(low, low + 1) for low in range(1, devices - 1, 2)]
        return lax.ppermute(value, AXES, pairs + [(high, low) for low, high in pairs])

    def swapped(value, distance):
        return lax.ppermute(value, AXES, [(source, source ^ distance) for source in range(devices)])

    mask = node_mask.reshape(1, node_rows)
    bias2, gain2, shift2 = bias[None], gain[None], shift[None]

    in_hbm = lambda value: pltpu.with_memory_space_constraint(value, pltpu.HBM)
    near, far = pl.pallas_call(
        halo_rows_kernel,
        out_shape=[jax.ShapeDtypeStruct((halo_pad, depth), BF16)] * 2,
        scratch_shapes=[pltpu.VMEM((8, 2 * LANES), jnp.int32)],
        compiler_params=params(8),
        name="halo_rows",
    )(in_hbm(feats), in_hbm(send_index))
    near, far = swapped(near, 1), far_swapped(far)

    def spec(shape, index):
        return pl.BlockSpec(shape, index)

    def whole(*shape):
        return pl.BlockSpec(shape, lambda *_: (0,) * len(shape))

    by_head = lambda n: pl.BlockSpec((n, width), lambda h, *_: (0, h))
    stacked = lambda *shape: pl.BlockSpec((1, *shape), lambda h, *_: (h, 0, 0))
    shape_of = jax.ShapeDtypeStruct
    zq, skip, count, flipped = pl.pallas_call(
        functools.partial(project_kernel, halo=halo),
        grid=(heads,),
        in_specs=[
            whole(node_rows, depth), by_head(depth), by_head(depth), whole(slots, node_rows), whole(slots, node_rows),
        ],
        out_specs=[by_head(rows), by_head(rows), whole(columns, rows), whole(depth, rows)],
        scratch_shapes=[pltpu.VMEM((rows, depth), BF16)],
        out_shape=[
            shape_of((rows, concat), BF16),
            shape_of((rows, concat), F32),
            shape_of((columns, rows), F32),
            shape_of((depth, rows), BF16),
        ],
        compiler_params=params(),
        cost_estimate=cost(5),
        name="project",
    )(in_hbm(feats), in_hbm(w_proj), in_hbm(w_skip), in_hbm(neighbours.T), in_hbm(edge_mask.T))

    vmem = pl.BlockSpec(memory_space=pltpu.VMEM)
    anywhere = pl.BlockSpec(memory_space=pl.ANY)
    ext, weight, source, target, scale, pre, stats, halo_flipped = pl.pallas_call(
        attend_kernel,
        in_specs=[vmem] * 11,
        out_shape=[
            shape_of((columns, concat), BF16),
            shape_of((heads, columns, rows), BF16),
            shape_of((heads, columns, LANES), F32),
            shape_of((heads, 8, rows), F32),
            shape_of((heads, rows, LANES), F32),
            shape_of((rows, concat), F32),
            shape_of((8, concat), F32),
            shape_of((depth, columns - rows), BF16),
        ],
        scratch_shapes=[pltpu.VMEM((columns - rows, depth), BF16), pltpu.VMEM((columns, rows), F32)],
        compiler_params=params(8),
        cost_estimate=cost(8),
        name="attend",
    )(zq, near, far, w_proj, skip, count, attn_src, attn_dst, bias2, cotangent, mask)

    for which in range(bits - 1):
        stats = pl.pallas_call(
            functools.partial(merge_kernel, which=which),
            in_specs=[pl.BlockSpec(memory_space=pltpu.VMEM)] * 2,
            out_shape=shape_of(stats.shape, F32),
            compiler_params=params(1),
            name="merge",
        )(stats, swapped(stats, 1 << which))
    other = swapped(stats, 1 << (bits - 1))

    half_grad = shape_of((2, depth, width), BF16)
    output, dskip, skip_send, skip_keep, small, gain_grad, shift_grad = pl.pallas_call(
        functools.partial(norm_kernel, last_bit=bits - 1),
        in_specs=[vmem] * 8,
        out_specs=[anywhere] + [vmem] * 6,
        out_shape=[
            pltpu.HBM((node_rows, concat), BF16),
            shape_of((rows, concat), BF16),
            half_grad,
            half_grad,
            shape_of((heads, 8, width), F32),
            jax.ShapeDtypeStruct((1, concat), F32),
            jax.ShapeDtypeStruct((1, concat), F32),
        ],
        scratch_shapes=[pltpu.VMEM((heads, node_rows, width), BF16), pltpu.SemaphoreType.DMA((heads,))],
        compiler_params=params(16),
        cost_estimate=cost(0.1),
        name="norm",
    )(pre, stats, other, cotangent, mask, gain2, shift2, flipped)

    def backward(part, arrays=(), deps=()):
        return pl.pallas_call(
            functools.partial(back_kernel, part=part),
            in_specs=[vmem] * (11 + len(arrays)) + [anywhere] * len(deps),
            out_shape=[
                shape_of((2, depth + 16, width), BF16),
                shape_of((rows, 2 * width), BF16),
                shape_of((halo_pad, (2 + part) * width), BF16),
                shape_of((halo_pad, (2 + part) * width), BF16),
            ],
            scratch_shapes=[pltpu.VMEM((columns, rows), F32), pltpu.VMEM((columns, LANES), F32)],
            compiler_params=params(8),
            cost_estimate=cost(0.1),
            name="back",
        )(weight, source, target, scale, ext, dskip, attn_src, attn_dst, flipped, halo_flipped, small, *arrays, *deps)

    quarter = (2, depth // 4, width)
    piece = (2, depth // SHARDS, width)
    def step_call(kernel, name, shapes, arrays, deps=()):
        return pl.pallas_call(
            kernel,
            in_specs=[vmem] * len(arrays) + [anywhere] * len(deps),
            out_shape=[shape_of(shape, BF16) for shape in shapes],
            compiler_params=params(1),
            cost_estimate=cost(COSTS.get(name, 0.1)),
            name=name,
        )(*arrays, *deps)

    def over_plane(shares):
        return [swapped(share, distance << 1) for distance, share in zip((1, 2, 3), shares)]

    def over_line(shares):
        return [swapped(share, distance) for distance, share in zip((16, 8, 24), shares)]

    def ordered_call(kernel, name, shapes, arrays, deps):
        return pl.pallas_call(
            functools.partial(kernel, deps=len(deps)),
            in_specs=[vmem] * len(arrays) + [anywhere] * len(deps),
            out_shape=shapes,
            scratch_shapes=[pltpu.VMEM((4, 2, 8, width), F32)],
            compiler_params=params(1),
            cost_estimate=cost(COSTS.get(name, 0.1)),
            name=name,
        )(*arrays, *deps)

    def plane_sum(arrays, deps):
        shapes = [shape_of((2, depth // SHARDS + 16, width), BF16)] * 4
        return ordered_call(plane_sum_kernel, "p_plane", shapes, arrays, deps)

    def line_sum(arrays, deps):
        shapes = [shape_of(piece, BF16), shape_of((2, 8, width), F32)]
        return ordered_call(line_sum_kernel, "p_line", shapes, arrays, deps)

    def two_sum(name, arrays, count, deps=()):
        shapes = [(2, arrays[0].shape[1] // count, width)] * count
        return step_call(functools.partial(two_sum_kernel, deps=len(deps)), name, shapes, arrays, deps)

    def pair_join(name, mine, other, deps=()):
        return step_call(pair_join_kernel, name, [(2, 2 * mine.shape[1], width)], [mine, other], deps)[0]

    def share_sum(name, arrays, count, deps):
        shapes = [(2, arrays[0].shape[1] // count, width)] * count
        return step_call(functools.partial(share_sum_kernel, deps=len(deps)), name, shapes, arrays, deps)

    def assemble(pieces, first, *out):
        return pl.pallas_call(
            functools.partial(assemble_kernel, first=first, pieces=len(pieces)),
            in_specs=[vmem] * len(pieces) + [anywhere] * len(out),
            out_specs=anywhere,
            out_shape=pltpu.HBM((depth, concat), F32),
            scratch_shapes=[pltpu.VMEM((2, SHARDS, depth // SHARDS, width), F32), pltpu.SemaphoreType.DMA((2, SHARDS))],
            input_output_aliases={len(pieces): 0} if out else {},
            compiler_params=params(8),
            cost_estimate=cost(0.1),
            name="assemble",
        )(*pieces, *out)

    def beyond(value):
        for which in range(5, bits):
            value = value + swapped(value, 1 << which)
        return value

    def after(value, *others):
        return lax.optimization_barrier((value, *others))[0]

    skip_other = swapped(skip_send, 1)
    proj_send, own_send, near_send, far_send = backward(0)
    proj_other = swapped(proj_send, 1)
    s_mine, *s_rest = step_call(
        functools.partial(two_sum_kernel, deps=1), "s_core", [quarter] * 4, [skip_keep, skip_other], [proj_send]
    )
    s_got = over_plane(s_rest)
    proj_keep, own_keep, back_near, back_far = backward(2, [near_send, far_send], [s_mine])
    p_mine, *p_rest = step_call(core_shares_kernel, "p_core", [(2, depth // 4 + 16, width)] * 4, [proj_keep, proj_other])
    p_got = over_plane(p_rest)
    s_mine, s_rest = share_sum("s_plane", [s_mine, *s_got], 2, [p_mine])
    s_mine, s_rest = two_sum("s_line", [s_mine, swapped(s_rest, 8)], 2)
    p_mine, *p_rest = plane_sum([p_mine, *p_got], [])
    p_got = over_line(p_rest)
    s_piece = beyond(two_sum("s_line", [s_mine, swapped(s_rest, 16)], 1, [p_mine])[0])
    s_piece = pair_join("s_join", s_piece, swapped(s_piece, 16))
    s_share = step_call(heads_join_kernel, "s_share", [(depth // 4, width)] * 2, [s_piece, swapped(s_piece, 8)])
    s_near = (swapped(s_share[0], 2), swapped(s_share[1], 4))
    s_sent = step_call(half_join_kernel, "s_near", [(depth // 2, width)] * 2, [*s_share, *s_near])
    s_far = (swapped(s_sent[0], 4), swapped(s_sent[1], 2))
    back_near, back_far = swapped(after(back_near, p_mine), 1), far_swapped(after(back_far, p_mine))
    p_piece, small = line_sum([p_mine, *p_got], [back_near, back_far])
    p_piece, small = beyond(p_piece), beyond(small)
    small_other = swapped(small, 1)
    p_piece = pair_join("p_join", p_piece, swapped(p_piece, 16))
    p_share = pair_join("p_join", p_piece, swapped(p_piece, 8), [small_other])
    p_got = over_plane([p_share] * 3)
    feats_total = pl.pallas_call(
        feats_kernel,
        in_specs=[vmem] * 5 + [anywhere],
        out_specs=vmem,
        out_shape=shape_of((rows, depth), F32),
        compiler_params=params(8),
        cost_estimate=cost(0.1),
        name="features",
    )(own_send, own_keep, dskip, w_proj, w_skip, s_far[0])
    grad_src, grad_dst, grad_bias = pl.pallas_call(
        vectors_kernel,
        in_specs=[vmem] * 2 + [anywhere],
        out_shape=[
            jax.ShapeDtypeStruct((heads, width), F32),
            jax.ShapeDtypeStruct((heads, width), F32),
            jax.ShapeDtypeStruct((1, concat), F32),
        ],
        compiler_params=params(1),
        cost_estimate=cost(0.1),
        name="vectors",
    )(small, small_other, s_far[0])
    grad_feats = pl.pallas_call(
        feats_halo_kernel,
        in_specs=[vmem] * 5,
        out_specs=vmem,
        scratch_shapes=[pltpu.VMEM((8, 2 * LANES), jnp.int32)],
        out_shape=jax.ShapeDtypeStruct((node_rows, depth), BF16),
        compiler_params=params(8),
        cost_estimate=cost(0.1),
        name="features_halo",
    )(feats_total, back_near, back_far, send_index, w_proj)
    p_got = [p_share, *p_got]
    p_other = [swapped(share, 1) for share in p_got]
    s_halves = step_call(
        plane_join_kernel, "s_half", [(2, depth // 2, width)] * 2, [*s_sent, *s_far], [grad_feats, grad_src]
    )
    s_other = [swapped(half, 1) for half in s_halves]
    grad_skip = assemble(s_other, 0, assemble(s_halves, 2))
    grad_proj = assemble(p_other, 0, assemble(p_got, 2))

    return (
        output,
        grad_feats,
        grad_proj,
        grad_skip,
        grad_src,
        grad_dst,
        grad_bias.reshape(concat),
        gain_grad.reshape(concat),
        shift_grad.reshape(concat),
    )


def solution(mesh):
    rows = P(AXES, None)
    in_specs = (rows,) + (P(),) * 7 + (rows, rows, rows, P(AXES), P(AXES, None, None))
    out_specs = (rows, rows) + (P(),) * 7
    return jax.shard_map(per_device, mesh=mesh, in_specs=in_specs, out_specs=out_specs, check_vma=False)
```

```python
import functools

import jax
import jax.numpy as jnp
from jax import lax
from jax.experimental import pallas as pl
from jax.experimental.pallas import tpu as pltpu
from jax.sharding import PartitionSpec as P

AXES = ("dom", "sub")
F32 = jnp.float32
BF16 = jnp.bfloat16
NEG = -1e30
LN2 = 0.6931471805599453
STEP = 64
SHARDS = 16
CHUNK = 32
LANES = 128
MIB = 1024 * 1024
COSTS = {"p_plane": 0.1, "p_line": 0.5, "p_join": 0.5}


def params(mib=24):
    return pltpu.CompilerParams(vmem_limit_bytes=mib * MIB)


def cost(us):
    return pl.CostEstimate(flops=int(us * 1.1e9), bytes_accessed=int(us * 1e6), transcendentals=0)


def mm(a, b, contract):
    return lax.dot_general(a, b, ((contract[:1], contract[1:]), ((), ())), preferred_element_type=F32)


def pad_rows(value, rows):
    extra = rows - value.shape[0]
    if extra == 0:
        return value
    return jnp.concatenate([value, jnp.zeros((extra,) + value.shape[1:], value.dtype)], axis=0)


def three_parts(value):
    high = value.astype(BF16)
    rest = value - high.astype(F32)
    middle = rest.astype(BF16)
    low = (rest - middle.astype(F32)).astype(BF16)
    return high, middle, low


def two_parts(value):
    high = value.astype(BF16).astype(F32)
    return jnp.concatenate([high, value - high], axis=0).astype(BF16)


def whole_of(parts):
    parts = parts.astype(F32)
    return parts[:8] + parts[8:]


def repeat_lanes(value, columns):
    return jnp.concatenate([value] * (columns // value.shape[1]), axis=1)


def fold_rows(value):
    return value.reshape(value.shape[0] // 8, 8, value.shape[1])


def real_rows(mask_ref, rows, columns):
    count = jnp.sum(mask_ref[...].astype(F32), axis=1, keepdims=True)
    real = lax.broadcasted_iota(jnp.int32, (rows, columns), 0).astype(F32) < count
    return count, real


def one_hot(rows, index_ref, scratch, odd):
    halo = index_ref.shape[2]
    down, up = index_ref[0, 0:1, :], index_ref[0, 1:2, :]
    scratch[...] = jnp.full(scratch.shape, -1, jnp.int32)
    scratch[0:1, 0:halo] = jnp.where(odd, down, up)
    scratch[0:1, LANES : LANES + halo] = jnp.where(odd, up, down)
    wanted = scratch[0:1, :]
    return (lax.broadcasted_iota(jnp.int32, (rows, 2 * LANES), 0) == wanted).astype(BF16)


def own_index():
    return lax.axis_index(AXES[0]) * lax.axis_size(AXES[1]) + lax.axis_index(AXES[1])


def is_odd():
    return lax.axis_index(AXES[1]) % 2 == 1


def own_place():
    me = own_index()
    return (me // 2 % 4) * 4 + (me // 8 % 2) * 2 + me // 16 % 2


def head_at(step):
    core = lax.axis_index(AXES[1]) % 2
    return (2 - 2 * core if step < 2 else 2 * core) + step % 2


def halo_rows_kernel(feats_ref, index_ref, near_ref, far_ref, scratch):
    picked = one_hot(feats_ref.shape[0], index_ref, scratch, is_odd())
    rows = mm(picked, feats_ref[...], (0, 0)).astype(BF16)
    near_ref[...] = rows[: near_ref.shape[0]]
    far_ref[...] = rows[LANES : LANES + far_ref.shape[0]]


def project_kernel(
    feats_ref, proj_ref, skip_w_ref, neighbours_ref, mask_ref, zq_ref, skip_ref, count_ref, flipped_ref, padded,
    *, halo,
):
    node_rows = feats_ref.shape[0]
    columns, rows = count_ref.shape

    @pl.when(pl.program_id(0) == 0)
    def _():
        feats = pad_rows(feats_ref[...].astype(F32), rows).astype(BF16)
        padded[...] = feats
        flipped_ref[...] = feats.T

    zq_ref[...] = mm(padded[...], proj_ref[...], (1, 0)).astype(BF16)
    skip_ref[...] = mm(padded[...], skip_w_ref[...], (1, 0))

    names = neighbours_ref[...]
    names = names + jnp.where(names >= node_rows, rows - node_rows, 0)
    names = names + jnp.where(names >= rows + halo, STEP - halo, 0)
    names = jnp.where(mask_ref[...] > 0, names, -1)
    names = jnp.concatenate([names, jnp.full((names.shape[0], rows - node_rows), -1, jnp.int32)], axis=1)
    own = lax.broadcasted_iota(jnp.int32, (8, rows), 1)
    share = columns // 4

    def chunk(index, carry):
        start = pl.multiple_of(pl.program_id(0) * share + index * 8, 8)
        source = lax.broadcasted_iota(jnp.int32, (8, rows), 0) + start
        total = (source == own).astype(F32)
        for slot in range(names.shape[0]):
            total += jnp.where(source == names[slot : slot + 1, :], 1.0, 0.0)
        count_ref[pl.ds(start, 8), :] = jnp.where(total > 0, jnp.log(jnp.maximum(total, 1.0)) * (1.0 / LN2), NEG)
        return carry

    lax.fori_loop(0, share // 8, chunk, 0, unroll=4)


def attend_kernel(
    zq_ref, near_ref, far_ref, proj_ref, skip_ref, count_ref, src_ref, dst_ref, bias_ref, cot_ref, mask_ref,
    ext_ref, weight_ref, source_ref, target_ref, scale_ref, pre_ref, stats_ref, flipped_ref, halo_scr, score_scr,
):
    columns, rows = count_ref.shape
    half = (columns - rows) // 2
    heads, width = src_ref.shape
    halo_scr[...] = jnp.zeros_like(halo_scr)
    near_at = jnp.where(is_odd(), 0, half)
    halo_scr[pl.ds(pl.multiple_of(near_at, 16), near_ref.shape[0]), :] = near_ref[...]
    halo_scr[pl.ds(pl.multiple_of(half - near_at, 16), far_ref.shape[0]), :] = far_ref[...]
    flipped_ref[...] = halo_scr[...].T
    stats_ref[...] = jnp.zeros_like(stats_ref)
    nodes, real = real_rows(mask_ref, rows, width)
    for head in range(heads):
        lanes = slice(head * width, (head + 1) * width)
        own = zq_ref[:, lanes]
        ext_ref[0:rows, lanes] = own
        ext_ref[rows:columns, lanes] = mm(halo_scr[...], proj_ref[:, lanes], (1, 0)).astype(BF16)
        ext = ext_ref[:, lanes]
        parts = three_parts(src_ref[head : head + 1, :] * (1.0 / LN2))
        vectors = jnp.concatenate([jnp.broadcast_to(part, (LANES, width)) for part in parts], axis=0)
        source = mm(ext, vectors, (1, 1))
        source_ref[head] = source[:, :LANES] + source[:, LANES : 2 * LANES] + source[:, 2 * LANES :]
        parts = three_parts(dst_ref[head : head + 1, :] * (1.0 / LN2))
        vectors = jnp.concatenate([jnp.broadcast_to(part, (16, width)) for part in parts], axis=0)
        target = mm(vectors, own, (1, 1))
        target = target[0:8] + target[16:24] + target[32:40]
        target_ref[head] = target
        target = target[0:1]

        def score(index, highest, head=head, target=target):
            where = pl.ds(pl.multiple_of(index * CHUNK, CHUNK), CHUNK)
            value = repeat_lanes(source_ref[head, where, :], rows) + target
            small = jnp.exp2(-jnp.abs(value))
            result = jnp.maximum(value, 0.2 * value) + (0.8 / LN2) * jnp.log(1.0 + small) + count_ref[where, :]
            score_scr[where, :] = result
            return jnp.maximum(highest, jnp.max(fold_rows(result), axis=0))

        highest = lax.fori_loop(0, columns // CHUNK, score, jnp.full((8, rows), NEG, F32), unroll=4)
        highest = jnp.max(highest, axis=0, keepdims=True)

        def weigh(index, carry, head=head, highest=highest):
            where = pl.ds(pl.multiple_of(index * CHUNK, CHUNK), CHUNK)
            weight_ref[head, where, :] = jnp.exp2(score_scr[where, :] - highest).astype(BF16)
            return carry

        lax.fori_loop(0, columns // CHUNK, weigh, 0, unroll=4)
        wide = jnp.concatenate([ext, jnp.ones((columns, LANES), BF16)], axis=1)
        summed = mm(weight_ref[head], wide, (0, 0))
        scale = 1.0 / summed[:, width:]
        scale_ref[head] = scale
        pre = summed[:, :width] * repeat_lanes(scale, width) + skip_ref[:, lanes] + bias_ref[:, lanes]
        pre_ref[:, lanes] = pre
        act = jnp.where(pre > 0, pre, jnp.exp(jnp.minimum(pre, 0.0)) - 1.0)
        cot = jnp.where(real, pad_rows(cot_ref[:, lanes].astype(F32), rows), 0.0)
        mean = jnp.sum(jnp.where(real, act, 0.0), axis=0, keepdims=True) / nodes
        centred = jnp.where(real, act - mean, 0.0)
        stats_ref[0:1, lanes] = jnp.broadcast_to(nodes, mean.shape)
        stats_ref[1:2, lanes] = mean
        stats_ref[2:3, lanes] = jnp.sum(centred * centred, axis=0, keepdims=True)
        stats_ref[3:4, lanes] = jnp.sum(cot, axis=0, keepdims=True)
        stats_ref[4:5, lanes] = jnp.sum(cot * centred, axis=0, keepdims=True)


def merged(first, second):
    nodes = first[0:1] + second[0:1]
    gap = second[1:2] - first[1:2]
    part = second[0:1] / nodes
    mean = first[1:2] + gap * part
    spread = first[2:3] + second[2:3] + gap * gap * first[0:1] * part
    shift = first[3:4] + second[3:4]
    gain = first[4:5] + second[4:5] - (mean - first[1:2]) * first[3:4] - (mean - second[1:2]) * second[3:4]
    return nodes, mean, spread, shift, gain


def in_order(mine, other, bit):
    mine_first = bit == 0
    return jnp.where(mine_first, mine, other), jnp.where(mine_first, other, mine)


def merge_kernel(mine_ref, other_ref, out_ref, *, which):
    bit = own_index() // 2**which % 2
    lines = merged(*in_order(mine_ref[...], other_ref[...], bit))
    out_ref[...] = jnp.zeros_like(out_ref)
    for line, value in enumerate(lines):
        out_ref[line : line + 1, :] = value


def place_blocks(out_ref, value, me):
    size = value.shape[0] // SHARDS
    for block in range(SHARDS):
        at = pl.multiple_of((block ^ me) * size, size)
        out_ref[pl.ds(at, size), :] = value[block * size : (block + 1) * size, :]


def core_shares_kernel(keep_ref, other_ref, *outs):
    size = keep_ref.shape[1] // 4 - 4
    for head in range(2):
        vectors = two_parts(whole_of(keep_ref[head, 4 * size :, :]) + whole_of(other_ref[head, 4 * size :, :]))
        for index, out_ref in enumerate(outs):
            rows = slice(index * size, (index + 1) * size)
            out_ref[head, :size, :] = (keep_ref[head, rows, :].astype(F32) + other_ref[head, rows, :].astype(F32)).astype(BF16)
            out_ref[head, size:, :] = vectors


def sum_of_four(refs, head, rows):
    first, second, third, fourth = (ref[head, rows, :].astype(F32) for ref in refs)
    return (first + second + third + fourth).astype(BF16)


def ordered_sum(refs, start, me, scratch):
    for index, ref in enumerate(refs):
        for head in range(2):
            scratch[index ^ me, head] = whole_of(ref[head, start:, :])
    return [scratch[0, head] + scratch[1, head] + scratch[2, head] + scratch[3, head] for head in range(2)]


def plane_sum_kernel(*refs, deps):
    ins, outs, scratch = refs[:4], refs[4 + deps : -1], refs[-1]
    size = outs[0].shape[1] - 16
    vectors = ordered_sum(ins, 4 * size, own_place() // 4, scratch)
    for head in range(2):
        for index, out_ref in enumerate(outs):
            out_ref[head, :size, :] = sum_of_four(ins, head, slice(index * size, (index + 1) * size))
            out_ref[head, size:, :] = two_parts(vectors[head])


def line_sum_kernel(*refs, deps):
    ins, (out_ref, small_ref, scratch) = refs[:4], refs[4 + deps :]
    size = out_ref.shape[1]
    vectors = ordered_sum(ins, size, own_place() % 4, scratch)
    for head in range(2):
        out_ref[head] = sum_of_four(ins, head, slice(0, size))
        small_ref[head] = vectors[head]


def vectors_kernel(mine_ref, other_ref, dep_ref, src_ref, dst_ref, bias_ref):
    odd = is_odd()
    width = src_ref.shape[1]
    for head in range(4):
        mine, other = mine_ref[head % 2], other_ref[head % 2]
        value = jnp.where(odd == (head >= 2), mine, other)
        src_ref[head : head + 1, :] = value[0:1]
        dst_ref[head : head + 1, :] = value[1:2]
        bias_ref[:, head * width : (head + 1) * width] = value[2:3]


def share_sum_kernel(*refs, deps):
    ins, outs = refs[:4], refs[4 + deps :]
    size = outs[0].shape[1]
    for head in range(2):
        for index, out_ref in enumerate(outs):
            out_ref[head] = sum_of_four(ins, head, slice(index * size, (index + 1) * size))


def pair_join_kernel(mine_ref, other_ref, *rest):
    size = mine_ref.shape[1]
    rest[-1][:, :size, :] = mine_ref[...]
    rest[-1][:, size:, :] = other_ref[...]


def heads_join_kernel(mine_ref, other_ref, *outs):
    size = mine_ref.shape[1]
    for head, out_ref in enumerate(outs):
        out_ref[:size, :] = mine_ref[head]
        out_ref[size:, :] = other_ref[head]


def half_join_kernel(*refs):
    for share, near, out_ref in zip(refs[:2], refs[2:4], refs[4:]):
        size = share.shape[0]
        out_ref[:size, :] = share[...]
        out_ref[size:, :] = near[...]


def plane_join_kernel(half_one, half_two, far_one, far_two, *rest):
    low_ref, high_ref = rest[-2:]
    size = half_one.shape[0] // 2
    low_ref[0] = half_one[...]
    high_ref[0] = far_one[...]
    for part, out_ref in ((slice(0, size), low_ref), (slice(size, 2 * size), high_ref)):
        out_ref[1, :size, :] = half_two[part, :]
        out_ref[1, size:, :] = far_two[part, :]


def two_sum_kernel(mine_ref, other_ref, *outs, deps=0):
    outs = outs[deps:]
    size = outs[0].shape[1]
    for piece, out_ref in enumerate(outs):
        rows = slice(piece * size, (piece + 1) * size)
        out_ref[...] = (mine_ref[:, rows, :].astype(F32) + other_ref[:, rows, :].astype(F32)).astype(BF16)


def norm_kernel(
    pre_ref, stats_ref, other_ref, cot_ref, mask_ref, gain_ref, shift_ref, flipped_ref,
    out_ref, dskip_ref, send_ref, keep_ref, small_ref, gain_grad_ref, shift_grad_ref, out_scr, done, *, last_bit,
):
    rows = pre_ref.shape[0]
    node_rows, width = out_scr.shape[1:]
    real = real_rows(mask_ref, rows, width)[1]
    copies = []
    for step in range(4):
        head = head_at(step)
        lanes = pl.ds(pl.multiple_of(head * width, width), width)
        pre = pre_ref[:, lanes]
        steep = jnp.exp(jnp.minimum(pre, 0.0))
        act = jnp.where(pre > 0, pre, steep - 1.0)
        first, second = in_order(stats_ref[:, lanes], other_ref[:, lanes], own_index() // 2**last_bit % 2)
        nodes, mean, spread, total, cross = merged(first, second)
        inverse = lax.rsqrt(spread / nodes + 1e-05)
        normed = (act - mean) * inverse
        gain = gain_ref[:, lanes]
        out_scr[step] = jnp.where(real, gain * normed + shift_ref[:, lanes], 0.0)[:node_rows].astype(BF16)
        copies.append(pltpu.make_async_copy(out_scr.at[step], out_ref.at[:, lanes], done.at[step]))
        copies[-1].start()
        gain_grad_ref[:, lanes] = cross * inverse
        shift_grad_ref[:, lanes] = total
        grad = pad_rows(cot_ref[:, lanes].astype(F32), rows) - total / nodes - normed * (cross * inverse / nodes)
        grad_pre = jnp.where(real, grad * (inverse * gain) * steep, 0.0)
        small_ref[head] = jnp.broadcast_to(jnp.sum(grad_pre, axis=0, keepdims=True), small_ref.shape[1:])
        dskip = grad_pre.astype(BF16)
        dskip_ref[:, lanes] = dskip
        grads = mm(flipped_ref[...], dskip, (1, 0)).astype(BF16)
        place_blocks((send_ref if step < 2 else keep_ref).at[step % 2], grads, own_place())
    for copy in copies:
        copy.wait()


def back_kernel(
    weight_ref, source_ref, target_ref, scale_ref, ext_ref, dskip_ref, src_ref, dst_ref, flipped_ref, halo_ref,
    small_in, *rest, part,
):
    grad_ref, own_ref, near_ref, far_ref, dal_scr, sum_scr = rest[-6:]
    columns, rows = weight_ref.shape[1:]
    half = (columns - rows) // 2
    width = src_ref.shape[1]
    depth = flipped_ref.shape[0]
    count = near_ref.shape[0]
    if part:
        near_ref[:, : 2 * width] = rest[0][...]
        far_ref[:, : 2 * width] = rest[1][...]
    for step in range(2):
        head = head_at(part + step)
        lanes = pl.ds(pl.multiple_of(head * width, width), width)
        target = target_ref[head, 0:1, :]
        dskip = dskip_ref[:, lanes]
        dal_scr[...] = mm(ext_ref[:, lanes], dskip, (1, 1))

        def average(index, carry):
            total, mean = carry
            where = pl.ds(pl.multiple_of(index * CHUNK, CHUNK), CHUNK)
            weight = weight_ref[head, where, :].astype(F32)
            return total + jnp.sum(fold_rows(weight), axis=0), mean + jnp.sum(fold_rows(weight * dal_scr[where, :]), axis=0)

        nothing = jnp.zeros((8, rows), F32)
        total, mean = lax.fori_loop(0, columns // CHUNK, average, (nothing, nothing), unroll=4)
        scale = 1.0 / jnp.sum(total, axis=0, keepdims=True)
        mean = jnp.sum(mean, axis=0, keepdims=True) * scale

        def slopes(index, by_target):
            where = pl.ds(pl.multiple_of(index * CHUNK, CHUNK), CHUNK)
            value = repeat_lanes(source_ref[head, where, :], rows) + target
            slope = (0.6 + 0.4 * jnp.tanh(value * (0.5 * LN2))) * scale
            du = weight_ref[head, where, :].astype(F32) * slope * (dal_scr[where, :] - mean)
            sum_scr[where, :] = sum(du[:, at : at + LANES] for at in range(0, rows, LANES))
            return by_target + jnp.sum(fold_rows(du), axis=0)

        by_target = lax.fori_loop(0, columns // CHUNK, slopes, nothing, unroll=4)
        by_target = jnp.sum(by_target, axis=0, keepdims=True)
        by_source = jnp.sum(sum_scr[...], axis=1, keepdims=True)
        ext = ext_ref[:, lanes]
        scaled = (dskip.astype(F32) * repeat_lanes(scale_ref[head], width)).astype(BF16)
        dz = mm(weight_ref[head], scaled, (1, 0)) + by_source * src_ref[pl.ds(head, 1), :]
        high, middle, low = three_parts(by_target)
        row = lax.broadcasted_iota(jnp.int32, (16, rows), 0)
        lines = jnp.where(row == 1, middle.astype(F32), jnp.where(row == 3, low.astype(F32), high.astype(F32)))
        lines = jnp.where(row < 4, lines, 0.0).astype(BF16)
        dst_high, dst_middle, _ = three_parts(dst_ref[pl.ds(head, 1), :])
        row = lax.broadcasted_iota(jnp.int32, (16, width), 0)
        vectors = jnp.where(row == 2, dst_middle.astype(F32), dst_high.astype(F32)).astype(BF16)
        dz_own = dz[:rows] + mm(lines, vectors, (0, 0))
        mine = slice(step * width, (step + 1) * width)
        dz_own = dz_own.astype(BF16)
        own_ref[:, mine] = dz_own
        dz_halo = dz[rows:].astype(BF16)
        below, above = dz[rows : rows + count], dz[rows + half : rows + half + count]
        odd = is_odd()
        at = part * width + step * width
        near_ref[:, at : at + width] = jnp.where(odd, below, above).astype(BF16)
        far_ref[:, at : at + width] = jnp.where(odd, above, below).astype(BF16)
        sums = mm(lines, ext[:rows], (1, 0))
        source_sum = jnp.sum(by_source * ext.astype(F32), axis=0, keepdims=True)
        row = lax.broadcasted_iota(jnp.int32, (8, width), 0)
        lines = jnp.where(row == 0, source_sum, jnp.where(row == 1, sums[0:1] + sums[1:2] + sums[3:4], small_in[head]))
        grad_ref[step, depth:, :] = two_parts(jnp.where(row < 3, lines, 0.0))
        grads = mm(flipped_ref[...], dz_own, (1, 0)) + mm(halo_ref[...], dz_halo, (1, 0))
        place_blocks(grad_ref.at[step], grads.astype(BF16), own_place())


def feats_kernel(own_one, own_two, dskip_ref, proj_ref, skip_ref, dep_ref, total_ref):
    width = own_one.shape[1] // 2
    total = mm(dskip_ref[...], skip_ref[...], (1, 1))
    for step in range(4):
        lanes = pl.ds(pl.multiple_of(head_at(step) * width, width), width)
        own = (own_one if step < 2 else own_two)[:, step % 2 * width : (step % 2 + 1) * width]
        total += mm(own, proj_ref[:, lanes], (1, 1))
    total_ref[...] = total


def feats_halo_kernel(total_ref, near_ref, far_ref, index_ref, proj_ref, out_ref, scratch):
    rows = total_ref.shape[0]
    count = near_ref.shape[0]
    width = near_ref.shape[1] // 4
    picks = one_hot(rows, index_ref, scratch, is_odd())
    picks = jnp.concatenate([picks[:, :count], picks[:, LANES : LANES + count]], axis=1)
    sent = jnp.concatenate([near_ref[...], far_ref[...]], axis=0)
    product = jnp.zeros((2 * count, proj_ref.shape[0]), F32)
    for step in range(4):
        lanes = pl.ds(pl.multiple_of(head_at(step) * width, width), width)
        other = (step + 2) % 4 * width
        product += mm(sent[:, other : other + width], proj_ref[:, lanes], (1, 1))
    high, middle, _ = three_parts(product)
    total = total_ref[...] + mm(picks, high, (1, 0)) + mm(picks, middle, (1, 0))
    out_ref[...] = total[: out_ref.shape[0]].astype(BF16)


def assemble_kernel(*refs, first, pieces):
    out_ref, scratch, done = refs[-3:]
    size, width = scratch.shape[2:]
    me = own_place()
    each = SHARDS // pieces
    copies = []
    for step in range(2):
        lanes = pl.ds(pl.multiple_of(head_at(first + step) * width, width), width)
        for block in range(SHARDS):
            at = pl.multiple_of((block ^ me) * size, size)
            rows = slice(block % each * size, (block % each + 1) * size)
            scratch[step, block] = refs[block // each][step, rows, :].astype(F32)
            copies.append(pltpu.make_async_copy(scratch.at[step, block], out_ref.at[pl.ds(at, size), lanes], done.at[step, block]))
            copies[-1].start()
    for copy in copies:
        copy.wait()


def per_device(
    feats, w_proj, w_skip, attn_src, attn_dst, bias, gain, shift, cotangent, neighbours, edge_mask, node_mask, send_index,
):
    node_rows, depth = feats.shape
    heads, width = attn_src.shape
    concat = heads * width
    slots = neighbours.shape[1]
    halo = send_index.shape[2]
    devices = lax.axis_size(AXES)
    bits = devices.bit_length() - 1
    rows = -(-node_rows // LANES) * LANES
    columns = rows + 2 * STEP
    halo_pad = -(-halo // 16) * 16

    def far_swapped(value):
        pairs = [(low, low + 1) for low in range(1, devices - 1, 2)]
        return lax.ppermute(value, AXES, pairs + [(high, low) for low, high in pairs])

    def swapped(value, distance):
        return lax.ppermute(value, AXES, [(source, source ^ distance) for source in range(devices)])

    mask = node_mask.reshape(1, node_rows)
    bias2, gain2, shift2 = bias[None], gain[None], shift[None]

    in_hbm = lambda value: pltpu.with_memory_space_constraint(value, pltpu.HBM)
    near, far = pl.pallas_call(
        halo_rows_kernel,
        out_shape=[jax.ShapeDtypeStruct((halo_pad, depth), BF16)] * 2,
        scratch_shapes=[pltpu.VMEM((8, 2 * LANES), jnp.int32)],
        compiler_params=params(8),
        name="halo_rows",
    )(in_hbm(feats), in_hbm(send_index))
    near, far = swapped(near, 1), far_swapped(far)

    def spec(shape, index):
        return pl.BlockSpec(shape, index)

    def whole(*shape):
        return pl.BlockSpec(shape, lambda *_: (0,) * len(shape))

    by_head = lambda n: pl.BlockSpec((n, width), lambda h, *_: (0, h))
    stacked = lambda *shape: pl.BlockSpec((1, *shape), lambda h, *_: (h, 0, 0))
    shape_of = jax.ShapeDtypeStruct
    zq, skip, count, flipped = pl.pallas_call(
        functools.partial(project_kernel, halo=halo),
        grid=(heads,),
        in_specs=[
            whole(node_rows, depth), by_head(depth), by_head(depth), whole(slots, node_rows), whole(slots, node_rows),
        ],
        out_specs=[by_head(rows), by_head(rows), whole(columns, rows), whole(depth, rows)],
        scratch_shapes=[pltpu.VMEM((rows, depth), BF16)],
        out_shape=[
            shape_of((rows, concat), BF16),
            shape_of((rows, concat), F32),
            shape_of((columns, rows), F32),
            shape_of((depth, rows), BF16),
        ],
        compiler_params=params(),
        cost_estimate=cost(5),
        name="project",
    )(in_hbm(feats), in_hbm(w_proj), in_hbm(w_skip), in_hbm(neighbours.T), in_hbm(edge_mask.T))

    vmem = pl.BlockSpec(memory_space=pltpu.VMEM)
    anywhere = pl.BlockSpec(memory_space=pl.ANY)
    ext, weight, source, target, scale, pre, stats, halo_flipped = pl.pallas_call(
        attend_kernel,
        in_specs=[vmem] * 11,
        out_shape=[
            shape_of((columns, concat), BF16),
            shape_of((heads, columns, rows), BF16),
            shape_of((heads, columns, LANES), F32),
            shape_of((heads, 8, rows), F32),
            shape_of((heads, rows, LANES), F32),
            shape_of((rows, concat), F32),
            shape_of((8, concat), F32),
            shape_of((depth, columns - rows), BF16),
        ],
        scratch_shapes=[pltpu.VMEM((columns - rows, depth), BF16), pltpu.VMEM((columns, rows), F32)],
        compiler_params=params(8),
        cost_estimate=cost(8),
        name="attend",
    )(zq, near, far, w_proj, skip, count, attn_src, attn_dst, bias2, cotangent, mask)

    for which in range(bits - 1):
        stats = pl.pallas_call(
            functools.partial(merge_kernel, which=which),
            in_specs=[pl.BlockSpec(memory_space=pltpu.VMEM)] * 2,
            out_shape=shape_of(stats.shape, F32),
            compiler_params=params(1),
            name="merge",
        )(stats, swapped(stats, 1 << which))
    other = swapped(stats, 1 << (bits - 1))

    half_grad = shape_of((2, depth, width), BF16)
    output, dskip, skip_send, skip_keep, small, gain_grad, shift_grad = pl.pallas_call(
        functools.partial(norm_kernel, last_bit=bits - 1),
        in_specs=[vmem] * 8,
        out_specs=[anywhere] + [vmem] * 6,
        out_shape=[
            pltpu.HBM((node_rows, concat), BF16),
            shape_of((rows, concat), BF16),
            half_grad,
            half_grad,
            shape_of((heads, 8, width), F32),
            jax.ShapeDtypeStruct((1, concat), F32),
            jax.ShapeDtypeStruct((1, concat), F32),
        ],
        scratch_shapes=[pltpu.VMEM((heads, node_rows, width), BF16), pltpu.SemaphoreType.DMA((heads,))],
        compiler_params=params(16),
        cost_estimate=cost(0.1),
        name="norm",
    )(pre, stats, other, cotangent, mask, gain2, shift2, flipped)

    def backward(part, arrays=(), deps=()):
        return pl.pallas_call(
            functools.partial(back_kernel, part=part),
            in_specs=[vmem] * (11 + len(arrays)) + [anywhere] * len(deps),
            out_shape=[
                shape_of((2, depth + 16, width), BF16),
                shape_of((rows, 2 * width), BF16),
                shape_of((halo_pad, (2 + part) * width), BF16),
                shape_of((halo_pad, (2 + part) * width), BF16),
            ],
            scratch_shapes=[pltpu.VMEM((columns, rows), F32), pltpu.VMEM((columns, LANES), F32)],
            compiler_params=params(8),
            cost_estimate=cost(0.1),
            name="back",
        )(weight, source, target, scale, ext, dskip, attn_src, attn_dst, flipped, halo_flipped, small, *arrays, *deps)

    quarter = (2, depth // 4, width)
    piece = (2, depth // SHARDS, width)
    def step_call(kernel, name, shapes, arrays, deps=()):
        return pl.pallas_call(
            kernel,
            in_specs=[vmem] * len(arrays) + [anywhere] * len(deps),
            out_shape=[shape_of(shape, BF16) for shape in shapes],
            compiler_params=params(1),
            cost_estimate=cost(COSTS.get(name, 0.1)),
            name=name,
        )(*arrays, *deps)

    def over_plane(shares):
        return [swapped(share, distance << 1) for distance, share in zip((1, 2, 3), shares)]

    def over_line(shares):
        return [swapped(share, distance) for distance, share in zip((16, 8, 24), shares)]

    def ordered_call(kernel, name, shapes, arrays, deps):
        return pl.pallas_call(
            functools.partial(kernel, deps=len(deps)),
            in_specs=[vmem] * len(arrays) + [anywhere] * len(deps),
            out_shape=shapes,
            scratch_shapes=[pltpu.VMEM((4, 2, 8, width), F32)],
            compiler_params=params(1),
            cost_estimate=cost(COSTS.get(name, 0.1)),
            name=name,
        )(*arrays, *deps)

    def plane_sum(arrays, deps):
        shapes = [shape_of((2, depth // SHARDS + 16, width), BF16)] * 4
        return ordered_call(plane_sum_kernel, "p_plane", shapes, arrays, deps)

    def line_sum(arrays, deps):
        shapes = [shape_of(piece, BF16), shape_of((2, 8, width), F32)]
        return ordered_call(line_sum_kernel, "p_line", shapes, arrays, deps)

    def two_sum(name, arrays, count, deps=()):
        shapes = [(2, arrays[0].shape[1] // count, width)] * count
        return step_call(functools.partial(two_sum_kernel, deps=len(deps)), name, shapes, arrays, deps)

    def pair_join(name, mine, other, deps=()):
        return step_call(pair_join_kernel, name, [(2, 2 * mine.shape[1], width)], [mine, other], deps)[0]

    def share_sum(name, arrays, count, deps):
        shapes = [(2, arrays[0].shape[1] // count, width)] * count
        return step_call(functools.partial(share_sum_kernel, deps=len(deps)), name, shapes, arrays, deps)

    def assemble(pieces, first, *out):
        return pl.pallas_call(
            functools.partial(assemble_kernel, first=first, pieces=len(pieces)),
            in_specs=[vmem] * len(pieces) + [anywhere] * len(out),
            out_specs=anywhere,
            out_shape=pltpu.HBM((depth, concat), F32),
            scratch_shapes=[pltpu.VMEM((2, SHARDS, depth // SHARDS, width), F32), pltpu.SemaphoreType.DMA((2, SHARDS))],
            input_output_aliases={len(pieces): 0} if out else {},
            compiler_params=params(8),
            cost_estimate=cost(0.1),
            name="assemble",
        )(*pieces, *out)

    def beyond(value):
        for which in range(5, bits):
            value = value + swapped(value, 1 << which)
        return value

    def after(value, *others):
        return lax.optimization_barrier((value, *others))[0]

    skip_other = swapped(skip_send, 1)
    proj_send, own_send, near_send, far_send = backward(0)
    proj_other = swapped(proj_send, 1)
    s_mine, *s_rest = step_call(
        functools.partial(two_sum_kernel, deps=1), "s_core", [quarter] * 4, [skip_keep, skip_other], [proj_send]
    )
    s_got = over_plane(s_rest)
    proj_keep, own_keep, back_near, back_far = backward(2, [near_send, far_send], [s_mine])
    p_mine, *p_rest = step_call(core_shares_kernel, "p_core", [(2, depth // 4 + 16, width)] * 4, [proj_keep, proj_other])
    p_got = over_plane(p_rest)
    s_mine, s_rest = share_sum("s_plane", [s_mine, *s_got], 2, [p_mine])
    s_mine, s_rest = two_sum("s_line", [s_mine, swapped(s_rest, 8)], 2)
    p_mine, *p_rest = plane_sum([p_mine, *p_got], [])
    p_got = over_line(p_rest)
    s_piece = beyond(two_sum("s_line", [s_mine, swapped(s_rest, 16)], 1, [p_mine])[0])
    s_piece = pair_join("s_join", s_piece, swapped(s_piece, 16))
    s_share = step_call(heads_join_kernel, "s_share", [(depth // 4, width)] * 2, [s_piece, swapped(s_piece, 8)])
    s_near = (swapped(s_share[0], 2), swapped(s_share[1], 4))
    s_sent = step_call(half_join_kernel, "s_near", [(depth // 2, width)] * 2, [*s_share, *s_near])
    s_far = (swapped(s_sent[0], 4), swapped(s_sent[1], 2))
    back_near, back_far = swapped(after(back_near, p_mine), 1), far_swapped(after(back_far, p_mine))
    p_piece, small = line_sum([p_mine, *p_got], [back_near, back_far])
    p_piece, small = beyond(p_piece), beyond(small)
    small_other = swapped(small, 1)
    p_piece = pair_join("p_join", p_piece, swapped(p_piece, 16))
    p_share = pair_join("p_join", p_piece, swapped(p_piece, 8), [small_other])
    p_got = over_plane([p_share] * 3)
    feats_total = pl.pallas_call(
        feats_kernel,
        in_specs=[vmem] * 5 + [anywhere],
        out_specs=vmem,
        out_shape=shape_of((rows, depth), F32),
        compiler_params=params(8),
        cost_estimate=cost(0.1),
        name="features",
    )(own_send, own_keep, dskip, w_proj, w_skip, s_far[0])
    grad_src, grad_dst, grad_bias = pl.pallas_call(
        vectors_kernel,
        in_specs=[vmem] * 2 + [anywhere],
        out_shape=[
            jax.ShapeDtypeStruct((heads, width), F32),
            jax.ShapeDtypeStruct((heads, width), F32),
            jax.ShapeDtypeStruct((1, concat), F32),
        ],
        compiler_params=params(1),
        cost_estimate=cost(0.1),
        name="vectors",
    )(small, small_other, s_far[0])
    grad_feats = pl.pallas_call(
        feats_halo_kernel,
        in_specs=[vmem] * 5,
        out_specs=vmem,
        scratch_shapes=[pltpu.VMEM((8, 2 * LANES), jnp.int32)],
        out_shape=jax.ShapeDtypeStruct((node_rows, depth), BF16),
        compiler_params=params(8),
        cost_estimate=cost(0.1),
        name="features_halo",
    )(feats_total, back_near, back_far, send_index, w_proj)
    p_got = [p_share, *p_got]
    p_other = [swapped(share, 1) for share in p_got]
    s_halves = step_call(
        plane_join_kernel, "s_half", [(2, depth // 2, width)] * 2, [*s_sent, *s_far], [grad_feats, grad_src]
    )
    s_other = [swapped(half, 1) for half in s_halves]
    grad_skip = assemble(s_other, 0, assemble(s_halves, 2))
    grad_proj = assemble(p_other, 0, assemble(p_got, 2))

    return (
        output,
        grad_feats,
        grad_proj,
        grad_skip,
        grad_src,
        grad_dst,
        grad_bias.reshape(concat),
        gain_grad.reshape(concat),
        shift_grad.reshape(concat),
    )


def solution(mesh):
    rows = P(AXES, None)
    in_specs = (rows,) + (P(),) * 7 + (rows, rows, rows, P(AXES), P(AXES, None, None))
    out_specs = (rows, rows) + (P(),) * 7
    return jax.shard_map(per_device, mesh=mesh, in_specs=in_specs, out_specs=out_specs, check_vma=False)
```

```python
import functools

import jax
import jax.numpy as jnp
from jax import lax
from jax.experimental import pallas as pl
from jax.experimental.pallas import tpu as pltpu
from jax.sharding import PartitionSpec as P

AXES = ("dom", "sub")
F32 = jnp.float32
BF16 = jnp.bfloat16
NEG = -1e30
LN2 = 0.6931471805599453
STEP = 64
SHARDS = 16
CHUNK = 32
LANES = 128
MIB = 1024 * 1024
COSTS = {"p_plane": 0.1, "p_line": 0.5, "p_join": 0.5}


def params(mib=24):
    return pltpu.CompilerParams(vmem_limit_bytes=mib * MIB)


def cost(us):
    return pl.CostEstimate(flops=int(us * 1.1e9), bytes_accessed=int(us * 1e6), transcendentals=0)


def mm(a, b, contract):
    return lax.dot_general(a, b, ((contract[:1], contract[1:]), ((), ())), preferred_element_type=F32)


def pad_rows(value, rows):
    extra = rows - value.shape[0]
    if extra == 0:
        return value
    return jnp.concatenate([value, jnp.zeros((extra,) + value.shape[1:], value.dtype)], axis=0)


def three_parts(value):
    high = value.astype(BF16)
    rest = value - high.astype(F32)
    middle = rest.astype(BF16)
    low = (rest - middle.astype(F32)).astype(BF16)
    return high, middle, low


def two_parts(value):
    high = value.astype(BF16).astype(F32)
    return jnp.concatenate([high, value - high], axis=0).astype(BF16)


def whole_of(parts):
    parts = parts.astype(F32)
    return parts[:8] + parts[8:]


def repeat_lanes(value, columns):
    return jnp.concatenate([value] * (columns // value.shape[1]), axis=1)


def fold_rows(value):
    return value.reshape(value.shape[0] // 8, 8, value.shape[1])


def real_rows(mask_ref, rows, columns):
    count = jnp.sum(mask_ref[...].astype(F32), axis=1, keepdims=True)
    real = lax.broadcasted_iota(jnp.int32, (rows, columns), 0).astype(F32) < count
    return count, real


def one_hot(rows, index_ref, scratch, odd):
    halo = index_ref.shape[2]
    down, up = index_ref[0, 0:1, :], index_ref[0, 1:2, :]
    scratch[...] = jnp.full(scratch.shape, -1, jnp.int32)
    scratch[0:1, 0:halo] = jnp.where(odd, down, up)
    scratch[0:1, LANES : LANES + halo] = jnp.where(odd, up, down)
    wanted = scratch[0:1, :]
    return (lax.broadcasted_iota(jnp.int32, (rows, 2 * LANES), 0) == wanted).astype(BF16)


def own_index():
    return lax.axis_index(AXES[0]) * lax.axis_size(AXES[1]) + lax.axis_index(AXES[1])


def is_odd():
    return lax.axis_index(AXES[1]) % 2 == 1


def own_place():
    me = own_index()
    return (me // 2 % 4) * 4 + (me // 8 % 2) * 2 + me // 16 % 2


def head_at(step):
    core = lax.axis_index(AXES[1]) % 2
    return (2 - 2 * core if step < 2 else 2 * core) + step % 2


def halo_rows_kernel(feats_ref, index_ref, near_ref, far_ref, scratch):
    picked = one_hot(feats_ref.shape[0], index_ref, scratch, is_odd())
    rows = mm(picked, feats_ref[...], (0, 0)).astype(BF16)
    near_ref[...] = rows[: near_ref.shape[0]]
    far_ref[...] = rows[LANES : LANES + far_ref.shape[0]]


def project_kernel(
    feats_ref, proj_ref, skip_w_ref, neighbours_ref, mask_ref, zq_ref, skip_ref, count_ref, flipped_ref, padded,
    *, halo,
):
    node_rows = feats_ref.shape[0]
    columns, rows = count_ref.shape

    @pl.when(pl.program_id(0) == 0)
    def _():
        feats = pad_rows(feats_ref[...].astype(F32), rows).astype(BF16)
        padded[...] = feats
        flipped_ref[...] = feats.T

    zq_ref[...] = mm(padded[...], proj_ref[...], (1, 0)).astype(BF16)
    skip_ref[...] = mm(padded[...], skip_w_ref[...], (1, 0))

    names = neighbours_ref[...]
    names = names + jnp.where(names >= node_rows, rows - node_rows, 0)
    names = names + jnp.where(names >= rows + halo, STEP - halo, 0)
    names = jnp.where(mask_ref[...] > 0, names, -1)
    names = jnp.concatenate([names, jnp.full((names.shape[0], rows - node_rows), -1, jnp.int32)], axis=1)
    own = lax.broadcasted_iota(jnp.int32, (8, rows), 1)
    share = columns // 4

    def chunk(index, carry):
        start = pl.multiple_of(pl.program_id(0) * share + index * 8, 8)
        source = lax.broadcasted_iota(jnp.int32, (8, rows), 0) + start
        total = (source == own).astype(F32)
        for slot in range(names.shape[0]):
            total += jnp.where(source == names[slot : slot + 1, :], 1.0, 0.0)
        count_ref[pl.ds(start, 8), :] = jnp.where(total > 0, jnp.log(jnp.maximum(total, 1.0)) * (1.0 / LN2), NEG)
        return carry

    lax.fori_loop(0, share // 8, chunk, 0, unroll=4)


def attend_kernel(
    zq_ref, near_ref, far_ref, proj_ref, skip_ref, count_ref, src_ref, dst_ref, bias_ref, cot_ref, mask_ref,
    ext_ref, weight_ref, source_ref, target_ref, scale_ref, pre_ref, stats_ref, flipped_ref, halo_scr, score_scr,
):
    columns, rows = count_ref.shape
    half = (columns - rows) // 2
    heads, width = src_ref.shape
    halo_scr[...] = jnp.zeros_like(halo_scr)
    near_at = jnp.where(is_odd(), 0, half)
    halo_scr[pl.ds(pl.multiple_of(near_at, 16), near_ref.shape[0]), :] = near_ref[...]
    halo_scr[pl.ds(pl.multiple_of(half - near_at, 16), far_ref.shape[0]), :] = far_ref[...]
    flipped_ref[...] = halo_scr[...].T
    stats_ref[...] = jnp.zeros_like(stats_ref)
    nodes, real = real_rows(mask_ref, rows, width)
    for head in range(heads):
        lanes = slice(head * width, (head + 1) * width)
        own = zq_ref[:, lanes]
        ext_ref[0:rows, lanes] = own
        ext_ref[rows:columns, lanes] = mm(halo_scr[...], proj_ref[:, lanes], (1, 0)).astype(BF16)
        ext = ext_ref[:, lanes]
        parts = three_parts(src_ref[head : head + 1, :] * (1.0 / LN2))
        vectors = jnp.concatenate([jnp.broadcast_to(part, (LANES, width)) for part in parts], axis=0)
        source = mm(ext, vectors, (1, 1))
        source_ref[head] = source[:, :LANES] + source[:, LANES : 2 * LANES] + source[:, 2 * LANES :]
        parts = three_parts(dst_ref[head : head + 1, :] * (1.0 / LN2))
        vectors = jnp.concatenate([jnp.broadcast_to(part, (16, width)) for part in parts], axis=0)
        target = mm(vectors, own, (1, 1))
        target = target[0:8] + target[16:24] + target[32:40]
        target_ref[head] = target
        target = target[0:1]

        def score(index, highest, head=head, target=target):
            where = pl.ds(pl.multiple_of(index * CHUNK, CHUNK), CHUNK)
            value = repeat_lanes(source_ref[head, where, :], rows) + target
            small = jnp.exp2(-jnp.abs(value))
            result = jnp.maximum(value, 0.2 * value) + (0.8 / LN2) * jnp.log(1.0 + small) + count_ref[where, :]
            score_scr[where, :] = result
            return jnp.maximum(highest, jnp.max(fold_rows(result), axis=0))

        highest = lax.fori_loop(0, columns // CHUNK, score, jnp.full((8, rows), NEG, F32), unroll=4)
        highest = jnp.max(highest, axis=0, keepdims=True)

        def weigh(index, carry, head=head, highest=highest):
            where = pl.ds(pl.multiple_of(index * CHUNK, CHUNK), CHUNK)
            weight_ref[head, where, :] = jnp.exp2(score_scr[where, :] - highest).astype(BF16)
            return carry

        lax.fori_loop(0, columns // CHUNK, weigh, 0, unroll=4)
        wide = jnp.concatenate([ext, jnp.ones((columns, LANES), BF16)], axis=1)
        summed = mm(weight_ref[head], wide, (0, 0))
        scale = 1.0 / summed[:, width:]
        scale_ref[head] = scale
        pre = summed[:, :width] * repeat_lanes(scale, width) + skip_ref[:, lanes] + bias_ref[:, lanes]
        pre_ref[:, lanes] = pre
        act = jnp.where(pre > 0, pre, jnp.exp(jnp.minimum(pre, 0.0)) - 1.0)
        cot = jnp.where(real, pad_rows(cot_ref[:, lanes].astype(F32), rows), 0.0)
        mean = jnp.sum(jnp.where(real, act, 0.0), axis=0, keepdims=True) / nodes
        centred = jnp.where(real, act - mean, 0.0)
        stats_ref[0:1, lanes] = jnp.broadcast_to(nodes, mean.shape)
        stats_ref[1:2, lanes] = mean
        stats_ref[2:3, lanes] = jnp.sum(centred * centred, axis=0, keepdims=True)
        stats_ref[3:4, lanes] = jnp.sum(cot, axis=0, keepdims=True)
        stats_ref[4:5, lanes] = jnp.sum(cot * centred, axis=0, keepdims=True)


def merged(first, second):
    nodes = first[0:1] + second[0:1]
    gap = second[1:2] - first[1:2]
    part = second[0:1] / nodes
    mean = first[1:2] + gap * part
    spread = first[2:3] + second[2:3] + gap * gap * first[0:1] * part
    shift = first[3:4] + second[3:4]
    gain = first[4:5] + second[4:5] - (mean - first[1:2]) * first[3:4] - (mean - second[1:2]) * second[3:4]
    return nodes, mean, spread, shift, gain


def in_order(mine, other, bit):
    mine_first = bit == 0
    return jnp.where(mine_first, mine, other), jnp.where(mine_first, other, mine)


def merge_kernel(mine_ref, other_ref, out_ref, *, which):
    bit = own_index() // 2**which % 2
    lines = merged(*in_order(mine_ref[...], other_ref[...], bit))
    out_ref[...] = jnp.zeros_like(out_ref)
    for line, value in enumerate(lines):
        out_ref[line : line + 1, :] = value


def place_blocks(out_ref, value, me):
    size = value.shape[0] // SHARDS
    for block in range(SHARDS):
        at = pl.multiple_of((block ^ me) * size, size)
        out_ref[pl.ds(at, size), :] = value[block * size : (block + 1) * size, :]


def core_shares_kernel(keep_ref, other_ref, *outs):
    size = keep_ref.shape[1] // 4 - 4
    for head in range(2):
        vectors = two_parts(whole_of(keep_ref[head, 4 * size :, :]) + whole_of(other_ref[head, 4 * size :, :]))
        for index, out_ref in enumerate(outs):
            rows = slice(index * size, (index + 1) * size)
            out_ref[head, :size, :] = (keep_ref[head, rows, :].astype(F32) + other_ref[head, rows, :].astype(F32)).astype(BF16)
            out_ref[head, size:, :] = vectors


def sum_of_four(refs, head, rows):
    first, second, third, fourth = (ref[head, rows, :].astype(F32) for ref in refs)
    return (first + second + third + fourth).astype(BF16)


def ordered_sum(refs, start, me, scratch):
    for index, ref in enumerate(refs):
        for head in range(2):
            scratch[index ^ me, head] = whole_of(ref[head, start:, :])
    return [scratch[0, head] + scratch[1, head] + scratch[2, head] + scratch[3, head] for head in range(2)]


def plane_sum_kernel(*refs, deps):
    ins, outs, scratch = refs[:4], refs[4 + deps : -1], refs[-1]
    size = outs[0].shape[1] - 16
    vectors = ordered_sum(ins, 4 * size, own_place() // 4, scratch)
    for head in range(2):
        for index, out_ref in enumerate(outs):
            out_ref[head, :size, :] = sum_of_four(ins, head, slice(index * size, (index + 1) * size))
            out_ref[head, size:, :] = two_parts(vectors[head])


def line_sum_kernel(*refs, deps):
    ins, (out_ref, small_ref, scratch) = refs[:4], refs[4 + deps :]
    size = out_ref.shape[1]
    vectors = ordered_sum(ins, size, own_place() % 4, scratch)
    for head in range(2):
        out_ref[head] = sum_of_four(ins, head, slice(0, size))
        small_ref[head] = vectors[head]


def vectors_kernel(mine_ref, other_ref, dep_ref, src_ref, dst_ref, bias_ref):
    odd = is_odd()
    width = src_ref.shape[1]
    for head in range(4):
        mine, other = mine_ref[head % 2], other_ref[head % 2]
        value = jnp.where(odd == (head >= 2), mine, other)
        src_ref[head : head + 1, :] = value[0:1]
        dst_ref[head : head + 1, :] = value[1:2]
        bias_ref[:, head * width : (head + 1) * width] = value[2:3]


def share_sum_kernel(*refs, deps):
    ins, outs = refs[:4], refs[4 + deps :]
    size = outs[0].shape[1]
    for head in range(2):
        for index, out_ref in enumerate(outs):
            out_ref[head] = sum_of_four(ins, head, slice(index * size, (index + 1) * size))


def pair_join_kernel(mine_ref, other_ref, *rest):
    size = mine_ref.shape[1]
    rest[-1][:, :size, :] = mine_ref[...]
    rest[-1][:, size:, :] = other_ref[...]


def heads_join_kernel(mine_ref, other_ref, *outs):
    size = mine_ref.shape[1]
    for head, out_ref in enumerate(outs):
        out_ref[:size, :] = mine_ref[head]
        out_ref[size:, :] = other_ref[head]


def half_join_kernel(*refs):
    for share, near, out_ref in zip(refs[:2], refs[2:4], refs[4:]):
        size = share.shape[0]
        out_ref[:size, :] = share[...]
        out_ref[size:, :] = near[...]


def plane_join_kernel(half_one, half_two, far_one, far_two, *rest):
    low_ref, high_ref = rest[-2:]
    size = half_one.shape[0] // 2
    low_ref[0] = half_one[...]
    high_ref[0] = far_one[...]
    for part, out_ref in ((slice(0, size), low_ref), (slice(size, 2 * size), high_ref)):
        out_ref[1, :size, :] = half_two[part, :]
        out_ref[1, size:, :] = far_two[part, :]


def two_sum_kernel(mine_ref, other_ref, *outs, deps=0):
    outs = outs[deps:]
    size = outs[0].shape[1]
    for piece, out_ref in enumerate(outs):
        rows = slice(piece * size, (piece + 1) * size)
        out_ref[...] = (mine_ref[:, rows, :].astype(F32) + other_ref[:, rows, :].astype(F32)).astype(BF16)


def norm_kernel(
    pre_ref, stats_ref, other_ref, cot_ref, mask_ref, gain_ref, shift_ref, flipped_ref,
    out_ref, dskip_ref, send_ref, keep_ref, small_ref, gain_grad_ref, shift_grad_ref, out_scr, done, *, last_bit,
):
    rows = pre_ref.shape[0]
    node_rows, width = out_scr.shape[1:]
    real = real_rows(mask_ref, rows, width)[1]
    copies = []
    for step in range(4):
        head = head_at(step)
        lanes = pl.ds(pl.multiple_of(head * width, width), width)
        pre = pre_ref[:, lanes]
        steep = jnp.exp(jnp.minimum(pre, 0.0))
        act = jnp.where(pre > 0, pre, steep - 1.0)
        first, second = in_order(stats_ref[:, lanes], other_ref[:, lanes], own_index() // 2**last_bit % 2)
        nodes, mean, spread, total, cross = merged(first, second)
        inverse = lax.rsqrt(spread / nodes + 1e-05)
        normed = (act - mean) * inverse
        gain = gain_ref[:, lanes]
        out_scr[step] = jnp.where(real, gain * normed + shift_ref[:, lanes], 0.0)[:node_rows].astype(BF16)
        copies.append(pltpu.make_async_copy(out_scr.at[step], out_ref.at[:, lanes], done.at[step]))
        copies[-1].start()
        gain_grad_ref[:, lanes] = cross * inverse
        shift_grad_ref[:, lanes] = total
        grad = pad_rows(cot_ref[:, lanes].astype(F32), rows) - total / nodes - normed * (cross * inverse / nodes)
        grad_pre = jnp.where(real, grad * (inverse * gain) * steep, 0.0)
        small_ref[head] = jnp.broadcast_to(jnp.sum(grad_pre, axis=0, keepdims=True), small_ref.shape[1:])
        dskip = grad_pre.astype(BF16)
        dskip_ref[:, lanes] = dskip
        grads = mm(flipped_ref[...], dskip, (1, 0)).astype(BF16)
        place_blocks((send_ref if step < 2 else keep_ref).at[step % 2], grads, own_place())
    for copy in copies:
        copy.wait()


def back_kernel(
    weight_ref, source_ref, target_ref, scale_ref, ext_ref, dskip_ref, src_ref, dst_ref, flipped_ref, halo_ref,
    small_in, *rest, part,
):
    grad_ref, own_ref, near_ref, far_ref, dal_scr, sum_scr = rest[-6:]
    columns, rows = weight_ref.shape[1:]
    half = (columns - rows) // 2
    width = src_ref.shape[1]
    depth = flipped_ref.shape[0]
    count = near_ref.shape[0]
    if part:
        near_ref[:, : 2 * width] = rest[0][...]
        far_ref[:, : 2 * width] = rest[1][...]
    for step in range(2):
        head = head_at(part + step)
        lanes = pl.ds(pl.multiple_of(head * width, width), width)
        target = target_ref[head, 0:1, :]
        dskip = dskip_ref[:, lanes]
        dal_scr[...] = mm(ext_ref[:, lanes], dskip, (1, 1))

        def average(index, carry):
            total, mean = carry
            where = pl.ds(pl.multiple_of(index * CHUNK, CHUNK), CHUNK)
            weight = weight_ref[head, where, :].astype(F32)
            return total + jnp.sum(fold_rows(weight), axis=0), mean + jnp.sum(fold_rows(weight * dal_scr[where, :]), axis=0)

        nothing = jnp.zeros((8, rows), F32)
        total, mean = lax.fori_loop(0, columns // CHUNK, average, (nothing, nothing), unroll=4)
        scale = 1.0 / jnp.sum(total, axis=0, keepdims=True)
        mean = jnp.sum(mean, axis=0, keepdims=True) * scale

        def slopes(index, by_target):
            where = pl.ds(pl.multiple_of(index * CHUNK, CHUNK), CHUNK)
            value = repeat_lanes(source_ref[head, where, :], rows) + target
            slope = (0.6 + 0.4 * jnp.tanh(value * (0.5 * LN2))) * scale
            du = weight_ref[head, where, :].astype(F32) * slope * (dal_scr[where, :] - mean)
            sum_scr[where, :] = sum(du[:, at : at + LANES] for at in range(0, rows, LANES))
            return by_target + jnp.sum(fold_rows(du), axis=0)

        by_target = lax.fori_loop(0, columns // CHUNK, slopes, nothing, unroll=4)
        by_target = jnp.sum(by_target, axis=0, keepdims=True)
        by_source = jnp.sum(sum_scr[...], axis=1, keepdims=True)
        ext = ext_ref[:, lanes]
        scaled = (dskip.astype(F32) * repeat_lanes(scale_ref[head], width)).astype(BF16)
        dz = mm(weight_ref[head], scaled, (1, 0)) + by_source * src_ref[pl.ds(head, 1), :]
        high, middle, low = three_parts(by_target)
        row = lax.broadcasted_iota(jnp.int32, (16, rows), 0)
        lines = jnp.where(row == 1, middle.astype(F32), jnp.where(row == 3, low.astype(F32), high.astype(F32)))
        lines = jnp.where(row < 4, lines, 0.0).astype(BF16)
        dst_high, dst_middle, _ = three_parts(dst_ref[pl.ds(head, 1), :])
        row = lax.broadcasted_iota(jnp.int32, (16, width), 0)
        vectors = jnp.where(row == 2, dst_middle.astype(F32), dst_high.astype(F32)).astype(BF16)
        dz_own = dz[:rows] + mm(lines, vectors, (0, 0))
        mine = slice(step * width, (step + 1) * width)
        dz_own = dz_own.astype(BF16)
        own_ref[:, mine] = dz_own
        dz_halo = dz[rows:].astype(BF16)
        below, above = dz[rows : rows + count], dz[rows + half : rows + half + count]
        odd = is_odd()
        at = part * width + step * width
        near_ref[:, at : at + width] = jnp.where(odd, below, above).astype(BF16)
        far_ref[:, at : at + width] = jnp.where(odd, above, below).astype(BF16)
        sums = mm(lines, ext[:rows], (1, 0))
        source_sum = jnp.sum(by_source * ext.astype(F32), axis=0, keepdims=True)
        row = lax.broadcasted_iota(jnp.int32, (8, width), 0)
        lines = jnp.where(row == 0, source_sum, jnp.where(row == 1, sums[0:1] + sums[1:2] + sums[3:4], small_in[head]))
        grad_ref[step, depth:, :] = two_parts(jnp.where(row < 3, lines, 0.0))
        grads = mm(flipped_ref[...], dz_own, (1, 0)) + mm(halo_ref[...], dz_halo, (1, 0))
        place_blocks(grad_ref.at[step], grads.astype(BF16), own_place())


def feats_kernel(own_one, own_two, dskip_ref, proj_ref, skip_ref, dep_ref, total_ref):
    width = own_one.shape[1] // 2
    total = mm(dskip_ref[...], skip_ref[...], (1, 1))
    for step in range(4):
        lanes = pl.ds(pl.multiple_of(head_at(step) * width, width), width)
        own = (own_one if step < 2 else own_two)[:, step % 2 * width : (step % 2 + 1) * width]
        total += mm(own, proj_ref[:, lanes], (1, 1))
    total_ref[...] = total


def feats_halo_kernel(total_ref, near_ref, far_ref, index_ref, proj_ref, out_ref, scratch):
    rows = total_ref.shape[0]
    count = near_ref.shape[0]
    width = near_ref.shape[1] // 4
    picks = one_hot(rows, index_ref, scratch, is_odd())
    picks = jnp.concatenate([picks[:, :count], picks[:, LANES : LANES + count]], axis=1)
    sent = jnp.concatenate([near_ref[...], far_ref[...]], axis=0)
    product = jnp.zeros((2 * count, proj_ref.shape[0]), F32)
    for step in range(4):
        lanes = pl.ds(pl.multiple_of(head_at(step) * width, width), width)
        other = (step + 2) % 4 * width
        product += mm(sent[:, other : other + width], proj_ref[:, lanes], (1, 1))
    high, middle, _ = three_parts(product)
    total = total_ref[...] + mm(picks, high, (1, 0)) + mm(picks, middle, (1, 0))
    out_ref[...] = total[: out_ref.shape[0]].astype(BF16)


def assemble_kernel(*refs, first, pieces):
    out_ref, scratch, done = refs[-3:]
    size, width = scratch.shape[2:]
    me = own_place()
    each = SHARDS // pieces
    copies = []
    for step in range(2):
        lanes = pl.ds(pl.multiple_of(head_at(first + step) * width, width), width)
        for block in range(SHARDS):
            at = pl.multiple_of((block ^ me) * size, size)
            rows = slice(block % each * size, (block % each + 1) * size)
            scratch[step, block] = refs[block // each][step, rows, :].astype(F32)
            copies.append(pltpu.make_async_copy(scratch.at[step, block], out_ref.at[pl.ds(at, size), lanes], done.at[step, block]))
            copies[-1].start()
    for copy in copies:
        copy.wait()


def per_device(
    feats, w_proj, w_skip, attn_src, attn_dst, bias, gain, shift, cotangent, neighbours, edge_mask, node_mask, send_index,
):
    node_rows, depth = feats.shape
    heads, width = attn_src.shape
    concat = heads * width
    slots = neighbours.shape[1]
    halo = send_index.shape[2]
    devices = lax.axis_size(AXES)
    bits = devices.bit_length() - 1
    rows = -(-node_rows // LANES) * LANES
    columns = rows + 2 * STEP
    halo_pad = -(-halo // 16) * 16

    def far_swapped(value):
        pairs = [(low, low + 1) for low in range(1, devices - 1, 2)]
        return lax.ppermute(value, AXES, pairs + [(high, low) for low, high in pairs])

    def swapped(value, distance):
        return lax.ppermute(value, AXES, [(source, source ^ distance) for source in range(devices)])

    mask = node_mask.reshape(1, node_rows)
    bias2, gain2, shift2 = bias[None], gain[None], shift[None]

    in_hbm = lambda value: pltpu.with_memory_space_constraint(value, pltpu.HBM)
    near, far = pl.pallas_call(
        halo_rows_kernel,
        out_shape=[jax.ShapeDtypeStruct((halo_pad, depth), BF16)] * 2,
        scratch_shapes=[pltpu.VMEM((8, 2 * LANES), jnp.int32)],
        compiler_params=params(8),
        name="halo_rows",
    )(in_hbm(feats), in_hbm(send_index))
    near, far = swapped(near, 1), far_swapped(far)

    def spec(shape, index):
        return pl.BlockSpec(shape, index)

    def whole(*shape):
        return pl.BlockSpec(shape, lambda *_: (0,) * len(shape))

    by_head = lambda n: pl.BlockSpec((n, width), lambda h, *_: (0, h))
    stacked = lambda *shape: pl.BlockSpec((1, *shape), lambda h, *_: (h, 0, 0))
    shape_of = jax.ShapeDtypeStruct
    zq, skip, count, flipped = pl.pallas_call(
        functools.partial(project_kernel, halo=halo),
        grid=(heads,),
        in_specs=[
            whole(node_rows, depth), by_head(depth), by_head(depth), whole(slots, node_rows), whole(slots, node_rows),
        ],
        out_specs=[by_head(rows), by_head(rows), whole(columns, rows), whole(depth, rows)],
        scratch_shapes=[pltpu.VMEM((rows, depth), BF16)],
        out_shape=[
            shape_of((rows, concat), BF16),
            shape_of((rows, concat), F32),
            shape_of((columns, rows), F32),
            shape_of((depth, rows), BF16),
        ],
        compiler_params=params(),
        cost_estimate=cost(5),
        name="project",
    )(in_hbm(feats), in_hbm(w_proj), in_hbm(w_skip), in_hbm(neighbours.T), in_hbm(edge_mask.T))

    vmem = pl.BlockSpec(memory_space=pltpu.VMEM)
    anywhere = pl.BlockSpec(memory_space=pl.ANY)
    ext, weight, source, target, scale, pre, stats, halo_flipped = pl.pallas_call(
        attend_kernel,
        in_specs=[vmem] * 11,
        out_shape=[
            shape_of((columns, concat), BF16),
            shape_of((heads, columns, rows), BF16),
            shape_of((heads, columns, LANES), F32),
            shape_of((heads, 8, rows), F32),
            shape_of((heads, rows, LANES), F32),
            shape_of((rows, concat), F32),
            shape_of((8, concat), F32),
            shape_of((depth, columns - rows), BF16),
        ],
        scratch_shapes=[pltpu.VMEM((columns - rows, depth), BF16), pltpu.VMEM((columns, rows), F32)],
        compiler_params=params(8),
        cost_estimate=cost(8),
        name="attend",
    )(zq, near, far, w_proj, skip, count, attn_src, attn_dst, bias2, cotangent, mask)

    for which in range(bits - 1):
        stats = pl.pallas_call(
            functools.partial(merge_kernel, which=which),
            in_specs=[pl.BlockSpec(memory_space=pltpu.VMEM)] * 2,
            out_shape=shape_of(stats.shape, F32),
            compiler_params=params(1),
            name="merge",
        )(stats, swapped(stats, 1 << which))
    other = swapped(stats, 1 << (bits - 1))

    half_grad = shape_of((2, depth, width), BF16)
    output, dskip, skip_send, skip_keep, small, gain_grad, shift_grad = pl.pallas_call(
        functools.partial(norm_kernel, last_bit=bits - 1),
        in_specs=[vmem] * 8,
        out_specs=[anywhere] + [vmem] * 6,
        out_shape=[
            pltpu.HBM((node_rows, concat), BF16),
            shape_of((rows, concat), BF16),
            half_grad,
            half_grad,
            shape_of((heads, 8, width), F32),
            jax.ShapeDtypeStruct((1, concat), F32),
            jax.ShapeDtypeStruct((1, concat), F32),
        ],
        scratch_shapes=[pltpu.VMEM((heads, node_rows, width), BF16), pltpu.SemaphoreType.DMA((heads,))],
        compiler_params=params(16),
        cost_estimate=cost(0.1),
        name="norm",
    )(pre, stats, other, cotangent, mask, gain2, shift2, flipped)

    def backward(part, arrays=(), deps=()):
        return pl.pallas_call(
            functools.partial(back_kernel, part=part),
            in_specs=[vmem] * (11 + len(arrays)) + [anywhere] * len(deps),
            out_shape=[
                shape_of((2, depth + 16, width), BF16),
                shape_of((rows, 2 * width), BF16),
                shape_of((halo_pad, (2 + part) * width), BF16),
                shape_of((halo_pad, (2 + part) * width), BF16),
            ],
            scratch_shapes=[pltpu.VMEM((columns, rows), F32), pltpu.VMEM((columns, LANES), F32)],
            compiler_params=params(8),
            cost_estimate=cost(0.1),
            name="back",
        )(weight, source, target, scale, ext, dskip, attn_src, attn_dst, flipped, halo_flipped, small, *arrays, *deps)

    quarter = (2, depth // 4, width)
    piece = (2, depth // SHARDS, width)
    def step_call(kernel, name, shapes, arrays, deps=()):
        return pl.pallas_call(
            kernel,
            in_specs=[vmem] * len(arrays) + [anywhere] * len(deps),
            out_shape=[shape_of(shape, BF16) for shape in shapes],
            compiler_params=params(1),
            cost_estimate=cost(COSTS.get(name, 0.1)),
            name=name,
        )(*arrays, *deps)

    def over_plane(shares):
        return [swapped(share, distance << 1) for distance, share in zip((1, 2, 3), shares)]

    def over_line(shares):
        return [swapped(share, distance) for distance, share in zip((16, 8, 24), shares)]

    def ordered_call(kernel, name, shapes, arrays, deps):
        return pl.pallas_call(
            functools.partial(kernel, deps=len(deps)),
            in_specs=[vmem] * len(arrays) + [anywhere] * len(deps),
            out_shape=shapes,
            scratch_shapes=[pltpu.VMEM((4, 2, 8, width), F32)],
            compiler_params=params(1),
            cost_estimate=cost(COSTS.get(name, 0.1)),
            name=name,
        )(*arrays, *deps)

    def plane_sum(arrays, deps):
        shapes = [shape_of((2, depth // SHARDS + 16, width), BF16)] * 4
        return ordered_call(plane_sum_kernel, "p_plane", shapes, arrays, deps)

    def line_sum(arrays, deps):
        shapes = [shape_of(piece, BF16), shape_of((2, 8, width), F32)]
        return ordered_call(line_sum_kernel, "p_line", shapes, arrays, deps)

    def two_sum(name, arrays, count, deps=()):
        shapes = [(2, arrays[0].shape[1] // count, width)] * count
        return step_call(functools.partial(two_sum_kernel, deps=len(deps)), name, shapes, arrays, deps)

    def pair_join(name, mine, other, deps=()):
        return step_call(pair_join_kernel, name, [(2, 2 * mine.shape[1], width)], [mine, other], deps)[0]

    def share_sum(name, arrays, count, deps):
        shapes = [(2, arrays[0].shape[1] // count, width)] * count
        return step_call(functools.partial(share_sum_kernel, deps=len(deps)), name, shapes, arrays, deps)

    def assemble(pieces, first, *out):
        return pl.pallas_call(
            functools.partial(assemble_kernel, first=first, pieces=len(pieces)),
            in_specs=[vmem] * len(pieces) + [anywhere] * len(out),
            out_specs=anywhere,
            out_shape=pltpu.HBM((depth, concat), F32),
            scratch_shapes=[pltpu.VMEM((2, SHARDS, depth // SHARDS, width), F32), pltpu.SemaphoreType.DMA((2, SHARDS))],
            input_output_aliases={len(pieces): 0} if out else {},
            compiler_params=params(8),
            cost_estimate=cost(0.1),
            name="assemble",
        )(*pieces, *out)

    def beyond(value):
        for which in range(5, bits):
            value = value + swapped(value, 1 << which)
        return value

    def after(value, *others):
        return lax.optimization_barrier((value, *others))[0]

    skip_other = swapped(skip_send, 1)
    proj_send, own_send, near_send, far_send = backward(0)
    proj_other = swapped(proj_send, 1)
    s_mine, *s_rest = step_call(
        functools.partial(two_sum_kernel, deps=1), "s_core", [quarter] * 4, [skip_keep, skip_other], [proj_send]
    )
    s_got = over_plane(s_rest)
    proj_keep, own_keep, back_near, back_far = backward(2, [near_send, far_send], [s_mine])
    p_mine, *p_rest = step_call(core_shares_kernel, "p_core", [(2, depth // 4 + 16, width)] * 4, [proj_keep, proj_other])
    p_got = over_plane(p_rest)
    s_mine, s_rest = share_sum("s_plane", [s_mine, *s_got], 2, [p_mine])
    s_mine, s_rest = two_sum("s_line", [s_mine, swapped(s_rest, 8)], 2)
    p_mine, *p_rest = plane_sum([p_mine, *p_got], [])
    p_got = over_line(p_rest)
    s_piece = beyond(two_sum("s_line", [s_mine, swapped(s_rest, 16)], 1, [p_mine])[0])
    s_piece = pair_join("s_join", s_piece, swapped(s_piece, 16))
    s_share = step_call(heads_join_kernel, "s_share", [(depth // 4, width)] * 2, [s_piece, swapped(s_piece, 8)])
    s_near = (swapped(s_share[0], 2), swapped(s_share[1], 4))
    s_sent = step_call(half_join_kernel, "s_near", [(depth // 2, width)] * 2, [*s_share, *s_near])
    s_far = (swapped(s_sent[0], 4), swapped(s_sent[1], 2))
    back_near, back_far = swapped(after(back_near, p_mine), 1), far_swapped(after(back_far, p_mine))
    p_piece, small = line_sum([p_mine, *p_got], [back_near, back_far])
    p_piece, small = beyond(p_piece), beyond(small)
    small_other = swapped(small, 1)
    p_piece = pair_join("p_join", p_piece, swapped(p_piece, 16))
    p_share = pair_join("p_join", p_piece, swapped(p_piece, 8), [small_other])
    p_got = over_plane([p_share] * 3)
    feats_total = pl.pallas_call(
        feats_kernel,
        in_specs=[vmem] * 5 + [anywhere],
        out_specs=vmem,
        out_shape=shape_of((rows, depth), F32),
        compiler_params=params(8),
        cost_estimate=cost(0.1),
        name="features",
    )(own_send, own_keep, dskip, w_proj, w_skip, s_far[0])
    grad_src, grad_dst, grad_bias = pl.pallas_call(
        vectors_kernel,
        in_specs=[vmem] * 2 + [anywhere],
        out_shape=[
            jax.ShapeDtypeStruct((heads, width), F32),
            jax.ShapeDtypeStruct((heads, width), F32),
            jax.ShapeDtypeStruct((1, concat), F32),
        ],
        compiler_params=params(1),
        cost_estimate=cost(0.1),
        name="vectors",
    )(small, small_other, s_far[0])
    grad_feats = pl.pallas_call(
        feats_halo_kernel,
        in_specs=[vmem] * 5,
        out_specs=vmem,
        scratch_shapes=[pltpu.VMEM((8, 2 * LANES), jnp.int32)],
        out_shape=pltpu.HBM((node_rows, depth), BF16),
        compiler_params=params(8),
        cost_estimate=cost(0.1),
        name="features_halo",
    )(feats_total, back_near, back_far, send_index, w_proj)
    p_got = [p_share, *p_got]
    p_other = [swapped(share, 1) for share in p_got]
    s_halves = step_call(
        plane_join_kernel, "s_half", [(2, depth // 2, width)] * 2, [*s_sent, *s_far], [grad_feats, grad_src]
    )
    s_other = [swapped(half, 1) for half in s_halves]
    grad_skip = assemble(s_other, 0, assemble(s_halves, 2))
    grad_proj = assemble(p_other, 0, assemble(p_got, 2))

    return (
        output,
        grad_feats,
        grad_proj,
        grad_skip,
        grad_src,
        grad_dst,
        grad_bias.reshape(concat),
        gain_grad.reshape(concat),
        shift_grad.reshape(concat),
    )


def solution(mesh):
    rows = P(AXES, None)
    in_specs = (rows,) + (P(),) * 7 + (rows, rows, rows, P(AXES), P(AXES, None, None))
    out_specs = (rows, rows) + (P(),) * 7
    return jax.shard_map(per_device, mesh=mesh, in_specs=in_specs, out_specs=out_specs, check_vma=False)
```
